256 devices in a mesh: lon: 16 (over x, y), lat: 16 (over z, core).
Axes of the slice: x: 4, y: 4, z: 8, core: 2. Of those that a mesh axis runs over, the one named last changes fastest.
Arguments:
- level_patches: bfloat16 [16, 26624, 80], P('lat', 'lon'), may hold values from -6 to 6
- level_embed: bfloat16 [13, 512], replicated, may hold values from -6 to 6
- embed_weight: bfloat16 [80, 512], replicated, may hold values from -0.625 to 0.625
- kv_weight: bfloat16 [512, 1024], replicated, may hold values from -0.25 to 0.25
- query: bfloat16 [3, 512], replicated, may hold values from -420 to 420
- band_levels: int32 [16], P('lat'), may hold values from 7 to 13, as said below
- grad_out: bfloat16 [16, 2048, 3, 512], P('lat', 'lon'), may hold values from -0.078125 to 0.078125
Outputs:
- kv_grad: float32 [512, 1024], P(('lon', 'lat'))
- embed_grad: float32 [80, 512], P(None, 'lat')
- query_grad: float32 [3, 512], replicated
The draws below stay inside these ranges and needn't reach their ends.
Inputs may be any that keep to these rules, and one draw needn't show every extreme that they name: `band_levels`: the number of leading pressure levels that the dataset of each latitude band provides; in every draw one band has all 13 and another has 7.
All inputs are finite; a program needn't handle non-finite values.
Results may differ from the reference program's by a relative error of at most 0.017.
The reference program's roundings to bfloat16 on the way (of `hidden`, `key_value`, `attn_weights`, `grad_kv` and `grad_embedded`) count: a program that leaves them out, or rounds other values in their place, can miss the bound.
Values may be sent and summed in bfloat16 or wider, within the bound.
No kernel may reach another device: no remote copies, remote signals or barrier semaphores. Data moves between devices by JAX's collectives and lax.ppermute only.
A program may use at most 64 MiB of HBM per device.

```python
import jax
import jax.numpy as jnp
from jax import lax

D = 512
HEADS = 16
LEVELS = 13
LATENT = 3
TOK_DEV = 128
FEAT = 80
BANDS = 16
TOK_BAND = 2048
N_LON = 16
N_LAT = 16


def draw_query(key, part):
    first_key = jax.random.fold_in(key, 0)
    entries = jnp.clip(jax.random.normal(first_key, (LATENT, D), jnp.float32), -6.0, 6.0)
    return entries.astype(jnp.bfloat16)


def draw_band_levels(key, part):
    first_key, second_key, third_key = jax.random.split(key, 3)
    counts = jax.random.randint(first_key, (BANDS,), 7, LEVELS + 1)
    full_band = jax.random.randint(second_key, (), 0, BANDS)
    short_band = (full_band + jax.random.randint(third_key, (), 1, BANDS)) % BANDS
    counts = counts.at[full_band].set(LEVELS).at[short_band].set(7)
    return counts.astype(jnp.int32)


def steps_of(rng, dims, pieces, smallest, largest):
    loudness = 1.0
    for dim, parts in pieces:
        draws = jax.random.uniform(jax.random.fold_in(jax.random.fold_in(rng, 6), dim), (parts,), jnp.float32, smallest / len(pieces), largest / len(pieces))
        loudness = loudness * jnp.repeat(jnp.exp(draws), dims[dim] // parts).reshape((-1,) + (1,) * (len(dims) - 1 - dim))
    return loudness


def gaussian(key, extent, width, most, pieces=(), kind=jnp.bfloat16):
    drawn = width * jax.random.normal(key, extent, jnp.float32)
    if pieces:
        drawn = drawn * steps_of(key, extent, pieces, -0.22, 0.18)
    return jnp.clip(drawn, -most, most).astype(kind)


def setup_inputs(seed: int = 0) -> dict:
    key_list = jax.random.split(jax.random.key(seed), 8)
    return {
        "level_patches": gaussian(key_list[0], (BANDS, LEVELS * TOK_BAND, FEAT), 1.0, 6.0, ((0, 16), (1, 16))),
        "level_embed": gaussian(key_list[1], (LEVELS, D), 1.0, 6.0),
        "embed_weight": gaussian(key_list[2], (FEAT, D), FEAT ** -0.5, 0.625),
        "kv_weight": gaussian(key_list[3], (D, 2 * D), D ** -0.5, 0.25),
        "query": draw_query(jax.random.fold_in(key_list[7], 71), 0),
        "band_levels": draw_band_levels(jax.random.fold_in(key_list[7], 71), 0),
        "grad_out": gaussian(key_list[6], (BANDS, TOK_BAND, LATENT, D), (1.0 / (TOK_DEV * N_LON * N_LAT) ** 0.5), 0.078125, ((0, 16), (1, 16))),
    }


SCORE_SCALE = 0.125
EPSILON = 1e-05
MASKED = -1e+30

def band_terms(patch_band, grad_band, level_count, level_embed, embed_weight, kv_weight, query):
    model_width = kv_weight.shape[0]
    head_size = model_width // HEADS
    band_tokens = grad_band.shape[0]
    patch_rows = patch_band.reshape(LEVELS * band_tokens, FEAT)
    embedded = jnp.dot(patch_rows, embed_weight, preferred_element_type=jnp.float32)
    embedded = embedded.reshape(LEVELS, band_tokens, model_width) + level_embed.astype(jnp.float32)[:, None, :]
    center = embedded - lax.optimization_barrier(jnp.mean(embedded, axis=-1, keepdims=True))
    inv_std = lax.rsqrt(lax.optimization_barrier(jnp.mean(center * center, axis=-1, keepdims=True)) + EPSILON)
    normed = (center * inv_std).reshape(LEVELS * band_tokens, model_width)
    inv_std = inv_std.reshape(LEVELS * band_tokens, 1)
    hidden = normed.astype(jnp.bfloat16)
    key_value = jnp.dot(hidden, kv_weight, preferred_element_type=jnp.float32).astype(jnp.bfloat16)
    key_value = key_value.reshape(LEVELS, band_tokens, 2 * model_width)
    key_heads = key_value[:, :, :model_width].reshape(LEVELS, band_tokens, HEADS, head_size).astype(jnp.float32)
    value_heads = key_value[:, :, model_width:].reshape(LEVELS, band_tokens, HEADS, head_size).astype(jnp.float32)
    queries = query.astype(jnp.float32).reshape(LATENT, HEADS, head_size)
    grad_rows = grad_band.astype(jnp.float32).reshape(band_tokens, LATENT, HEADS, head_size)
    score = jnp.einsum('ahd,lthd->tahl', queries, key_heads) * SCORE_SCALE
    usable = jnp.arange(LEVELS, dtype=jnp.int32) < level_count
    score = jnp.where(usable[None, None, None, :], score, MASKED)
    peak_score = lax.optimization_barrier(jnp.max(score, axis=-1, keepdims=True))
    exponent = jnp.exp(score - peak_score)
    attention = exponent / lax.optimization_barrier(jnp.sum(exponent, axis=-1, keepdims=True))
    attn_weights = attention.astype(jnp.bfloat16)
    grad_attn = jnp.einsum('tahd,lthd->tahl', grad_rows, value_heads)
    grad_score = attention * (grad_attn - lax.optimization_barrier(jnp.sum(attention * grad_attn, axis=-1, keepdims=True)))
    grad_keys = (jnp.einsum('tahl,ahd->lthd', grad_score, queries) * SCORE_SCALE).astype(jnp.bfloat16)
    grad_values = jnp.einsum('tahl,tahd->lthd', attn_weights.astype(jnp.float32), grad_rows).astype(jnp.bfloat16)
    query_term = (jnp.einsum('tahl,lthd->ahd', grad_score, key_heads) * SCORE_SCALE).reshape(LATENT, model_width)
    grad_kv = jnp.concatenate((grad_keys.reshape(LEVELS, band_tokens, model_width), grad_values.reshape(LEVELS, band_tokens, model_width)), axis=-1)
    grad_kv = grad_kv.reshape(LEVELS * band_tokens, 2 * model_width)
    kv_term = jnp.dot(hidden.T, grad_kv, preferred_element_type=jnp.float32)
    grad_hidden = jnp.dot(grad_kv, kv_weight.T, preferred_element_type=jnp.float32)
    grad_embedded = inv_std * (grad_hidden - lax.optimization_barrier(jnp.mean(grad_hidden, axis=-1, keepdims=True)) - normed * lax.optimization_barrier(jnp.mean(grad_hidden * normed, axis=-1, keepdims=True)))
    grad_embedded = grad_embedded.astype(jnp.bfloat16)
    embed_term = jnp.dot(patch_rows.T, grad_embedded, preferred_element_type=jnp.float32)
    return (kv_term, embed_term, query_term)

def reference(level_patches, level_embed, embed_weight, kv_weight, query, band_levels, grad_out):
    model_width = kv_weight.shape[0]

    def step(totals, inputs):
        patch_band, grad_band, level_count = inputs
        terms = band_terms(patch_band, grad_band, level_count, level_embed, embed_weight, kv_weight, query)
        return (jax.tree.map(lambda left, right: left + right, totals, terms), None)
    zeros = (jnp.zeros((model_width, 2 * model_width), jnp.float32), jnp.zeros((FEAT, model_width), jnp.float32), jnp.zeros((LATENT, model_width), jnp.float32))
    totals, unused = lax.scan(step, zeros, (level_patches, grad_out, band_levels))
    return (totals[0], totals[1], totals[2])
```

```python
import functools

import jax
import jax.numpy as jnp
from jax import lax
from jax.experimental import pallas as pl
from jax.experimental.pallas import tpu as pltpu
from jax.sharding import PartitionSpec as P

HEADS = 16
SCORE_SCALE = 0.125
EPSILON = 1e-05
MASKED = -1e30
BF16 = jnp.bfloat16
F32 = jnp.float32

LEVELS = 13
TOK = 128
PAIRS = 7
WIDE = 2 * TOK
SPAN = PAIRS * WIDE
D = 512
FEAT = 80
AUG = 96
LATENT = 3
AH = LATENT * HEADS
NT = (((1,), (1,)), ((), ()))
RING = 16

VMEM = pl.BlockSpec(memory_space=pltpu.VMEM)
SMEM = pl.BlockSpec(memory_space=pltpu.SMEM)


def params(mib):
    return pltpu.CompilerParams(vmem_limit_bytes=mib * 1024 * 1024)


def slot_kernel(lon_ref, patch_ref, slot_ref):
    lon = lon_ref[0]
    for i in range(LEVELS):
        owner = lax.rem(lon * LEVELS + i, RING)
        block = patch_ref[i * TOK : (i + 1) * TOK, :].astype(F32)
        slot_ref[owner] = block.T.astype(BF16)


def prep_kernel(
    kvw_ref, embed_w_ref, level_ref, query_ref, grad_ref, kvwt_ref, waug_ref, qbdt_ref, qbd2_ref, gt_ref, rows
):
    for c in range(4):
        kvwt_ref[c * 256 : (c + 1) * 256, :] = kvw_ref[:, c * 256 : (c + 1) * 256].astype(F32).T.astype(BF16)
    rows[...] = jnp.zeros_like(rows)
    rows[:FEAT, :] = embed_w_ref[...].astype(F32)
    rows[FEAT : FEAT + LEVELS, :] = level_ref[...].astype(F32)
    waug_ref[...] = rows[...].T.astype(BF16)
    head = lax.broadcasted_iota(jnp.int32, (HEADS, D), 0)
    owner = lax.broadcasted_iota(jnp.int32, (HEADS, D), 1) // (D // HEADS)
    for a in range(LATENT):
        block = jnp.where(head == owner, query_ref[a : a + 1, :].astype(F32), 0.0)
        rows[a * HEADS : (a + 1) * HEADS, :] = block
        rows[AH + a * HEADS : AH + (a + 1) * HEADS, :] = block
    qbdt_ref[...] = rows[:AH, :].astype(BF16)
    qbd2_ref[...] = rows[...].T.astype(BF16)
    for a in range(LATENT):
        gt_ref[a] = grad_ref[:, a * D : (a + 1) * D].astype(F32).T.astype(BF16)


def main_kernel(
    lon_ref, count_ref, recv_ref, waug_ref, kvwt_ref, kvw_ref, qbdt_ref, qbd2_ref, gt_ref,
    kv_out, embed_out, query_out,
    g2, paug_s, hid_s, kv_s, gkv_s, ge_s, nrm_s, inv_s, sc_s, ga_s, w_s, gs_s,
):
    lon = lon_ref[0]
    count = count_ref[0]
    for a in range(LATENT):
        wide = gt_ref[a].astype(F32)
        g2[a, :, :TOK] = wide
        g2[a, :, TOK:] = wide

    def forward(p, carry):
        at = pl.ds(pl.multiple_of(p * WIDE, WIDE), WIDE)
        first = 2 * p
        second = jnp.minimum(2 * p + 1, LEVELS - 1)
        paug_s[:FEAT, at] = jnp.concatenate(
            [recv_ref[(RING * first + lon) // LEVELS], recv_ref[(RING * second + lon) // LEVELS]], axis=1
        )
        row = lax.broadcasted_iota(jnp.int32, (AUG - FEAT, WIDE), 0)
        lane = lax.broadcasted_iota(jnp.int32, (AUG - FEAT, WIDE), 1)
        level = jnp.where(lane >= TOK, second, first)
        paug_s[FEAT:, at] = jnp.where(row == level, 1.0, 0.0).astype(BF16)
        embedded = jnp.dot(waug_ref[...], paug_s[:, at], preferred_element_type=F32)
        center = embedded - jnp.mean(embedded, axis=0, keepdims=True)
        inv_std = lax.rsqrt(jnp.mean(center * center, axis=0, keepdims=True) + EPSILON)
        normed = center * inv_std
        inv_s[:, at] = inv_std
        nrm_s[:, at] = normed
        hid_s[:, at] = normed.astype(BF16)
        kv_s[:, at] = jnp.dot(kvwt_ref[...], hid_s[:, at], preferred_element_type=F32).astype(BF16)
        sc_s[:, at] = (
            jnp.dot(qbdt_ref[...], kv_s[:D, at], preferred_element_type=F32) * SCORE_SCALE
        )
        values = kv_s[D:, at].astype(F32)
        for a in range(LATENT):
            product = (g2[a] * values).reshape(HEADS, D // HEADS, WIDE)
            ga_s[a * HEADS : (a + 1) * HEADS, at] = jnp.sum(product, axis=1)
        return carry

    lax.fori_loop(0, PAIRS, forward, 0)

    score = [
        jnp.where(l < count, sc_s[:, l * TOK : (l + 1) * TOK], MASKED) for l in range(LEVELS)
    ]
    peak = functools.reduce(jnp.maximum, score)
    total = jnp.zeros_like(peak)
    for l in range(LEVELS):
        exponent = jnp.exp(score[l] - peak)
        sc_s[:, l * TOK : (l + 1) * TOK] = exponent
        total = total + exponent
    inverse = 1.0 / total
    inner = jnp.zeros_like(peak)
    for l in range(LEVELS):
        lanes = slice(l * TOK, (l + 1) * TOK)
        attention = sc_s[:, lanes] * inverse
        sc_s[:, lanes] = attention
        w_s[:, lanes] = attention.astype(BF16).astype(F32)
        inner = inner + attention * ga_s[:, lanes]
    for l in range(LEVELS):
        lanes = slice(l * TOK, (l + 1) * TOK)
        grad_score = sc_s[:, lanes] * (ga_s[:, lanes] - inner) * SCORE_SCALE
        high = grad_score.astype(BF16)
        gs_s[:AH, lanes] = high
        gs_s[AH:, lanes] = (grad_score - high.astype(F32)).astype(BF16)
    tail = slice(LEVELS * TOK, SPAN)
    w_s[:, tail] = jnp.zeros((AH, TOK), F32)
    gs_s[:, tail] = jnp.zeros((2 * AH, TOK), BF16)

    def backward(p, carry):
        at = pl.ds(pl.multiple_of(p * WIDE, WIDE), WIDE)
        gkv_s[:D, at] = jnp.dot(qbd2_ref[...], gs_s[:, at], preferred_element_type=F32).astype(BF16)
        grad_values = None
        for a in range(LATENT):
            weight = w_s[a * HEADS : (a + 1) * HEADS, at].reshape(HEADS, 1, WIDE)
            term = weight * g2[a].reshape(HEADS, D // HEADS, WIDE)
            grad_values = term if grad_values is None else grad_values + term
        gkv_s[D:, at] = grad_values.reshape(D, WIDE).astype(BF16)
        grad_hidden = jnp.dot(kvw_ref[...], gkv_s[:, at], preferred_element_type=F32)
        normed = nrm_s[:, at]
        mean = jnp.mean(grad_hidden, axis=0, keepdims=True)
        slope = jnp.mean(grad_hidden * normed, axis=0, keepdims=True)
        ge_s[:, at] = (inv_s[:, at] * (grad_hidden - mean - normed * slope)).astype(BF16)
        return carry

    lax.fori_loop(0, PAIRS, backward, 0)

    def project(c, carry):
        at = pl.ds(pl.multiple_of(c * WIDE, WIDE), WIDE)
        kv_out[:, at] = lax.dot_general(
            hid_s[...], gkv_s[at, :], NT, preferred_element_type=F32
        ).astype(BF16)
        return carry

    lax.fori_loop(0, 2 * D // WIDE, project, 0)
    embed_t = lax.dot_general(ge_s[...], paug_s[...], NT, preferred_element_type=F32)
    embed_out[:, :AUG] = embed_t.astype(BF16)
    embed_out[:, AUG:] = jnp.zeros((D, TOK - AUG), BF16)
    rows = lax.dot_general(gs_s[...], kv_s[:D, :], NT, preferred_element_type=F32)
    rows = rows[:AH] + rows[AH:]
    head = lax.broadcasted_iota(jnp.int32, (HEADS, D), 0)
    owner = lax.broadcasted_iota(jnp.int32, (HEADS, D), 1) // (D // HEADS)
    for a in range(LATENT):
        block = jnp.where(head == owner, rows[a * HEADS : (a + 1) * HEADS], 0.0)
        query_out[a : a + 1, :] = jnp.sum(block, axis=0, keepdims=True)


PACK = 64
SHARE = 48


def sum_lon_kernel(kv_ref, embed_ref, query_ref, pack_ref, total, tile):
    acc = kv_ref[0].astype(F32)
    for source in range(1, RING):
        acc = acc + kv_ref[source].astype(F32)
    total[...] = acc
    tile[...] = jnp.zeros_like(tile)
    for a in range(LATENT):
        for c in range(4):
            tile[16 + a * 4 + c : 17 + a * 4 + c, :] = query_ref[a : a + 1, c * TOK : (c + 1) * TOK]
    query_rows = tile[16:32, :].astype(BF16)
    for target in range(RING):
        for c in range(8):
            tile[2 * c : 2 * c + 2, :] = total[2 * target : 2 * target + 2, c * TOK : (c + 1) * TOK]
        pack_ref[target, 0:16, :] = tile[0:16, :].astype(BF16)
        pack_ref[target, 16:48, :] = embed_ref[target * 32 : (target + 1) * 32, :]
        pack_ref[target, 48:64, :] = query_rows


def sum_lat_kernel(pack_ref, kv_out, share_ref, tile):
    acc = pack_ref[0].astype(F32)
    for source in range(1, RING):
        acc = acc + pack_ref[source].astype(F32)
    tile[...] = acc
    for c in range(8):
        kv_out[:, c * TOK : (c + 1) * TOK] = tile[2 * c : 2 * c + 2, :]
    share = acc[16:, :].astype(BF16)
    for target in range(RING):
        share_ref[target] = share


def sum_share_kernel(share_ref, embed_out, query_out, tile):
    acc = share_ref[0].astype(F32)
    for source in range(1, RING):
        acc = acc + share_ref[source].astype(F32)
    tile[...] = acc
    embed_out[...] = tile[0:32, :].T[:FEAT, :]
    for a in range(LATENT):
        for c in range(4):
            query_out[a : a + 1, c * TOK : (c + 1) * TOK] = tile[32 + a * 4 + c : 33 + a * 4 + c, :]


def shape(*dims, dtype=BF16):
    return jax.ShapeDtypeStruct(dims, dtype)


def on_device(level_patches, level_embed, embed_weight, kv_weight, query, band_levels, grad_out):
    lon = lax.axis_index("lon").astype(jnp.int32).reshape(1)
    slots = pl.pallas_call(
        slot_kernel,
        out_shape=shape(RING, FEAT, TOK),
        in_specs=[SMEM, VMEM],
        out_specs=VMEM,
        compiler_params=params(16),
    )(lon, level_patches[0])
    kvwt, waug, qbdt, qbd2, grad_t = pl.pallas_call(
        prep_kernel,
        out_shape=(shape(2 * D, D), shape(D, AUG), shape(AH, D), shape(D, AUG), shape(LATENT, D, TOK)),
        in_specs=[VMEM] * 5,
        out_specs=(VMEM,) * 5,
        scratch_shapes=[pltpu.VMEM((AUG, D), F32)],
        compiler_params=params(24),
    )(kv_weight, embed_weight, level_embed, query, grad_out[0].reshape(TOK, LATENT * D))
    recv = lax.all_to_all(slots, "lon", 0, 0, tiled=True)
    kv_term, embed_term, query_term = pl.pallas_call(
        main_kernel,
        out_shape=(shape(D, 2 * D), shape(D, TOK), shape(LATENT, D, dtype=F32)),
        in_specs=[SMEM, SMEM] + [VMEM] * 7,
        out_specs=(VMEM,) * 3,
        scratch_shapes=[
            pltpu.VMEM((LATENT, D, WIDE), F32),
            pltpu.VMEM((AUG, SPAN), BF16),
            pltpu.VMEM((D, SPAN), BF16),
            pltpu.VMEM((2 * D, SPAN), BF16),
            pltpu.VMEM((2 * D, SPAN), BF16),
            pltpu.VMEM((D, SPAN), BF16),
            pltpu.VMEM((D, SPAN), F32),
            pltpu.VMEM((1, SPAN), F32),
            pltpu.VMEM((AH, SPAN), F32),
            pltpu.VMEM((AH, SPAN), F32),
            pltpu.VMEM((AH, SPAN), F32),
            pltpu.VMEM((2 * AH, SPAN), BF16),
        ],
        compiler_params=params(48),
    )(lon, band_levels, recv, waug, kvwt, kv_weight, qbdt, qbd2, grad_t)
    kv_lon = lax.all_to_all(kv_term.reshape(RING, D // RING, 2 * D), "lon", 0, 0, tiled=True)
    pack = pl.pallas_call(
        sum_lon_kernel,
        out_shape=shape(RING, PACK, TOK),
        in_specs=[VMEM] * 3,
        out_specs=VMEM,
        scratch_shapes=[pltpu.VMEM((D // RING, 2 * D), F32), pltpu.VMEM((32, TOK), F32)],
        compiler_params=params(16),
    )(kv_lon, embed_term, query_term)
    packed = lax.all_to_all(pack, "lat", 0, 0, tiled=True)
    kv_grad, share = pl.pallas_call(
        sum_lat_kernel,
        out_shape=(shape(2, 2 * D, dtype=F32), shape(RING, SHARE, TOK)),
        in_specs=[VMEM],
        out_specs=(VMEM, VMEM),
        scratch_shapes=[pltpu.VMEM((PACK, TOK), F32)],
        compiler_params=params(16),
    )(packed)
    shared = lax.all_to_all(share, "lon", 0, 0, tiled=True)
    embed_grad, query_grad = pl.pallas_call(
        sum_share_kernel,
        out_shape=(shape(FEAT, 32, dtype=F32), shape(LATENT, D, dtype=F32)),
        in_specs=[VMEM],
        out_specs=(VMEM, VMEM),
        scratch_shapes=[pltpu.VMEM((SHARE, TOK), F32)],
        compiler_params=params(16),
    )(shared)
    return (kv_grad, embed_grad, query_grad)


def solution(mesh):
    placed = (P("lat", "lon", None), P(), P(), P(), P(), P("lat"), P("lat", "lon", None, None))
    return jax.shard_map(
        on_device,
        mesh=mesh,
        in_specs=placed,
        out_specs=(P(("lon", "lat"), None), P(None, "lat"), P()),
        check_vma=False,
    )
```

```python
import functools

import jax
import jax.numpy as jnp
from jax import lax
from jax.experimental import pallas as pl
from jax.experimental.pallas import tpu as pltpu
from jax.sharding import PartitionSpec as P

HEADS = 16
SCORE_SCALE = 0.125
EPSILON = 1e-05
MASKED = -1e30
BF16 = jnp.bfloat16
F32 = jnp.float32

LEVELS = 13
TOK = 128
PAIRS = 7
WIDE = 2 * TOK
SPAN = PAIRS * WIDE
D = 512
HEAD = D // HEADS
FEAT = 80
AUG = 96
LATENT = 3
AH = LATENT * HEADS
GS = 128
NT = (((1,), (1,)), ((), ()))
RING = 16
ZED = 8
HALF = D // 2
ROW = 2 * D + TOK
SHARE = 48

VMEM = pl.BlockSpec(memory_space=pltpu.VMEM)
SMEM = pl.BlockSpec(memory_space=pltpu.SMEM)


def params(mib):
    return pltpu.CompilerParams(vmem_limit_bytes=mib * 1024 * 1024)


def shape(*dims, dtype=BF16):
    return jax.ShapeDtypeStruct(dims, dtype)


def slot_kernel(lon_ref, patch_ref, slot_ref):
    lon = lon_ref[0]
    for i in range(LEVELS):
        owner = lax.rem(lon * LEVELS + i, RING)
        slot_ref[owner] = patch_ref[:, i * TOK : (i + 1) * TOK]


def feature_of(position):
    core, z, lon, pair = position >> 8, (position >> 5) & 7, (position >> 1) & 15, position & 1
    return lon * 32 + z * 4 + core * 2 + pair


def prep_kernel(
    core_ref, kvw_ref, embed_w_ref, level_ref, query_ref, grad_ref,
    tall_ref, wide_ref,
    rows, spread,
):
    core = core_ref[0]
    down = lax.broadcasted_iota(jnp.int32, (D, D), 0)
    across = lax.broadcasted_iota(jnp.int32, (D, D), 1)
    reorder = jnp.where(feature_of(down) == across, 1.0, 0.0).astype(BF16)
    side = (core + (down >> 8)) & 1
    target = ((down >> 5) & 7) * 64 + side * 32 + (down & 31)
    wide_ref[:, 2 * D : 3 * D] = jnp.where(feature_of(across) == target, 1.0, 0.0).astype(BF16)
    for c in range(4):
        part = jnp.dot(reorder, kvw_ref[:, c * 256 : (c + 1) * 256], preferred_element_type=F32)
        wide_ref[:, c * 256 : (c + 1) * 256] = part.astype(BF16)
        tall_ref[c * 256 : (c + 1) * 256, :] = part.T.astype(BF16)
    rows[...] = jnp.zeros_like(rows)
    rows[:FEAT, :] = embed_w_ref[...].astype(F32)
    rows[FEAT : FEAT + LEVELS, :] = level_ref[...].astype(F32)
    weights = rows[...]
    weights = weights - jnp.mean(weights, axis=1, keepdims=True)
    high = weights.astype(BF16)
    spread[...] = jnp.zeros_like(spread)
    spread[:AUG, :] = high.astype(F32)
    spread[AUG : 2 * AUG, :] = weights - high.astype(F32)
    wide_ref[:, 3 * D : 3 * D + 256] = jnp.dot(
        reorder, spread[...].T.astype(BF16), preferred_element_type=F32
    ).astype(BF16)
    head = lax.broadcasted_iota(jnp.int32, (HEADS, D), 0)
    owner = lax.broadcasted_iota(jnp.int32, (HEADS, D), 1) >> 5
    spread[:32, :] = jnp.zeros((32, D), F32)
    for a in range(LATENT):
        block = jnp.where(head == owner, query_ref[a : a + 1, :].astype(F32), 0.0)
        spread[32 + a * HEADS : 32 + (a + 1) * HEADS, :] = block
        spread[80 + a * HEADS : 80 + (a + 1) * HEADS, :] = block
    tall_ref[2 * D : 2 * D + AH, :] = spread[80:128, :].astype(BF16)
    tall_ref[2 * D + AH :, :] = jnp.zeros((16, D), BF16)
    wide_ref[:, 3 * D + 256 : 3 * D + 384] = spread[:GS, :].T.astype(BF16)
    for a in range(LATENT):
        at = 4 * D + a * TOK
        wide_ref[:, at : at + TOK] = grad_ref[a].astype(F32).T.astype(BF16)


def main_kernel(
    place_ref, count_ref, recv_ref, tall_ref, wide_ref,
    keep_out, send_out,
    g2, paug_s, hid_s, kv_s, gkv_s, ge_s, nrm_s, inv_s, sc_s, ga_s, w_s, gs_s,
):
    lon = place_ref[0]
    core = place_ref[1]
    count = count_ref[0]
    for a in range(LATENT):
        wide = wide_ref[:, 4 * D + a * TOK : 4 * D + (a + 1) * TOK].astype(F32)
        g2[a, :, :TOK] = wide
        g2[a, :, TOK:] = wide
    gs_s[:32, :] = jnp.zeros((32, SPAN), BF16)

    def embed(p):
        at = slice(p * WIDE, (p + 1) * WIDE)
        first, second = 2 * p, min(2 * p + 1, LEVELS - 1)
        patches = jnp.concatenate(
            [recv_ref[(RING * first + lon) // LEVELS], recv_ref[(RING * second + lon) // LEVELS]], axis=1
        )
        row = lax.broadcasted_iota(jnp.int32, (AUG - FEAT, WIDE), 0)
        lane = lax.broadcasted_iota(jnp.int32, (AUG - FEAT, WIDE), 1)
        level = jnp.where(lane >= TOK, second, first)
        one_hot = jnp.where(row == level, 1.0, 0.0).astype(BF16)
        paug_s[:FEAT, at] = patches
        paug_s[FEAT:AUG, at] = one_hot
        paug_s[AUG : AUG + FEAT, at] = patches
        paug_s[AUG + FEAT :, at] = one_hot
        center = jnp.dot(
            wide_ref[:, 3 * D : 3 * D + 2 * AUG], paug_s[:, at], preferred_element_type=F32
        )
        inv_std = lax.rsqrt(jnp.mean(center * center, axis=0, keepdims=True) + EPSILON)
        normed = center * inv_std
        inv_s[:, at] = inv_std
        nrm_s[:, at] = normed
        hid_s[:, at] = normed.astype(BF16)

    def score(p):
        at = slice(p * WIDE, (p + 1) * WIDE)
        kv_s[:, at] = jnp.dot(tall_ref[: 2 * D, :], hid_s[:, at], preferred_element_type=F32).astype(BF16)
        sc_s[:, at] = (
            jnp.dot(tall_ref[2 * D : 2 * D + AH, :], kv_s[:D, at], preferred_element_type=F32) * SCORE_SCALE
        )
        values = kv_s[D:, at].astype(F32)
        for a in range(LATENT):
            product = (g2[a] * values).reshape(HEADS, HEAD, WIDE)
            ga_s[a * HEADS : (a + 1) * HEADS, at] = jnp.sum(product, axis=1)

    embed(0)
    for p in range(PAIRS):
        if p + 1 < PAIRS:
            embed(p + 1)
        score(p)

    masked = [
        jnp.where(l < count, sc_s[:, l * TOK : (l + 1) * TOK], MASKED) for l in range(LEVELS)
    ]
    peak = functools.reduce(jnp.maximum, masked)
    total = jnp.zeros_like(peak)
    for l in range(LEVELS):
        exponent = jnp.exp(masked[l] - peak)
        sc_s[:, l * TOK : (l + 1) * TOK] = exponent
        total = total + exponent
    inverse = 1.0 / total
    inner = jnp.zeros_like(peak)
    for l in range(LEVELS):
        lanes = slice(l * TOK, (l + 1) * TOK)
        attention = sc_s[:, lanes] * inverse
        sc_s[:, lanes] = attention
        w_s[:, lanes] = attention.astype(BF16).astype(F32)
        inner = inner + attention * ga_s[:, lanes]
    for l in range(LEVELS):
        lanes = slice(l * TOK, (l + 1) * TOK)
        grad_score = sc_s[:, lanes] * (ga_s[:, lanes] - inner) * SCORE_SCALE
        high = grad_score.astype(BF16)
        gs_s[32:80, lanes] = (grad_score - high.astype(F32)).astype(BF16)
        gs_s[80:, lanes] = high
    tail = slice(LEVELS * TOK, SPAN)
    w_s[:, tail] = jnp.zeros((AH, TOK), F32)
    gs_s[32:, tail] = jnp.zeros((2 * AH, TOK), BF16)

    def grad_kv(p):
        at = slice(p * WIDE, (p + 1) * WIDE)
        gkv_s[:D, at] = jnp.dot(
            wide_ref[:, 3 * D + 256 : 3 * D + 384], gs_s[:, at], preferred_element_type=F32
        ).astype(BF16)
        grad_values = None
        for a in range(LATENT):
            weight = w_s[a * HEADS : (a + 1) * HEADS, at].reshape(HEADS, 1, WIDE)
            term = weight * g2[a].reshape(HEADS, HEAD, WIDE)
            grad_values = term if grad_values is None else grad_values + term
        gkv_s[D:, at] = grad_values.reshape(D, WIDE).astype(BF16)

    def embed_back(p):
        at = slice(p * WIDE, (p + 1) * WIDE)
        grad_hidden = jnp.dot(wide_ref[:, : 2 * D], gkv_s[:, at], preferred_element_type=F32)
        normed = nrm_s[:, at]
        mean = jnp.mean(grad_hidden, axis=0, keepdims=True)
        slope = jnp.mean(grad_hidden * normed, axis=0, keepdims=True)
        ge_s[:, at] = (inv_s[:, at] * (grad_hidden - mean - normed * slope)).astype(BF16)

    grad_kv(0)
    for p in range(PAIRS):
        if p + 1 < PAIRS:
            grad_kv(p + 1)
        embed_back(p)

    mine = hid_s[pl.ds(pl.multiple_of(core * HALF, HALF), HALF), :]
    other = hid_s[pl.ds(pl.multiple_of((1 - core) * HALF, HALF), HALF), :]
    for c in range(4):
        at = slice(c * WIDE, (c + 1) * WIDE)
        send_out[:, at] = lax.dot_general(other, gkv_s[at, :], NT, preferred_element_type=F32).astype(BF16)
        keep_out[:, at] = lax.dot_general(mine, gkv_s[at, :], NT, preferred_element_type=F32)
    grads = lax.dot_general(ge_s[...], paug_s[:GS, :], NT, preferred_element_type=F32).astype(BF16)
    grads = jnp.dot(wide_ref[:, 2 * D : 3 * D], grads, preferred_element_type=F32)
    queries = lax.dot_general(kv_s[:D, :], gs_s[...], NT, preferred_element_type=F32)
    head = lax.broadcasted_iota(jnp.int32, (D, GS), 0) >> 5
    lane = lax.broadcasted_iota(jnp.int32, (D, GS), 1)
    queries = jnp.where((lane & 15) == head, queries, 0.0).reshape(HEADS, HEAD, GS)
    queries = jnp.sum(queries, axis=0)
    queries = queries + pltpu.roll(queries, AH, 1)
    queries = jnp.concatenate([queries] * HEADS, axis=0)
    block = jnp.where(lane < FEAT, grads, queries)
    keep_out[:, 2 * D :] = block[:HALF]
    send_out[:, 2 * D :] = block[HALF:].astype(BF16)


def pair_kernel(keep_ref, recv_ref, sum_ref):
    sum_ref[...] = (keep_ref[...] + recv_ref[...].astype(F32)).astype(BF16)


def sum_z_kernel(part_ref, share_ref, total, tile):
    acc = part_ref[0].astype(F32)
    for source in range(1, ZED):
        acc = acc + part_ref[source].astype(F32)
    total[...] = acc
    block = acc[:, 2 * D :].astype(BF16)
    for target in range(RING):
        for c in range(8):
            tile[target, 2 * c : 2 * c + 2, :] = total[2 * target : 2 * target + 2, c * TOK : (c + 1) * TOK]
        share_ref[target, 0:16, :] = tile[target].astype(BF16)
        share_ref[target, 16:48, :] = block


def sum_lon_kernel(share_ref, kv_out, embed_out, query_out, tile, turned):
    acc = share_ref[0].astype(F32)
    for source in range(1, RING):
        acc = acc + share_ref[source].astype(F32)
    tile[...] = acc[:16]
    for c in range(8):
        kv_out[:, c * TOK : (c + 1) * TOK] = tile[2 * c : 2 * c + 2, :]
    embed_out[...] = acc[16:, :FEAT]
    turned[...] = acc[16:, :].T
    for a in range(LATENT):
        for h in range(HEADS):
            at = FEAT + a * HEADS + h
            query_out[a : a + 1, h * HEAD : (h + 1) * HEAD] = turned[at : at + 1, :]


def on_device(level_patches, level_embed, embed_weight, kv_weight, query, band_levels, grad_out):
    lon = lax.axis_index("lon").astype(jnp.int32)
    core = (lax.axis_index("lat") % 2).astype(jnp.int32)
    place = jnp.stack([lon, core])
    slots = pl.pallas_call(
        slot_kernel,
        out_shape=shape(RING, FEAT, TOK),
        in_specs=[SMEM, VMEM],
        out_specs=VMEM,
        compiler_params=params(16),
        name="slots",
    )(lon.reshape(1), level_patches[0].T)
    tall, wide = pl.pallas_call(
        prep_kernel,
        out_shape=(shape(2 * D + 64, D), shape(D, 4 * D + LATENT * TOK)),
        in_specs=[SMEM] + [VMEM] * 5,
        out_specs=(VMEM,) * 2,
        scratch_shapes=[pltpu.VMEM((AUG, D), F32), pltpu.VMEM((256, D), F32)],
        compiler_params=params(24),
        name="prep",
    )(core.reshape(1), kv_weight, embed_weight, level_embed, query, grad_out[0].transpose(1, 0, 2))
    recv = lax.all_to_all(slots, "lon", 0, 0, tiled=True)
    keep, send = pl.pallas_call(
        main_kernel,
        out_shape=(shape(HALF, ROW, dtype=F32), shape(HALF, ROW)),
        in_specs=[SMEM, SMEM] + [VMEM] * 3,
        out_specs=(VMEM,) * 2,
        scratch_shapes=[
            pltpu.VMEM((LATENT, D, WIDE), F32),
            pltpu.VMEM((2 * AUG, SPAN), BF16),
            pltpu.VMEM((D, SPAN), BF16),
            pltpu.VMEM((2 * D, SPAN), BF16),
            pltpu.VMEM((2 * D, SPAN), BF16),
            pltpu.VMEM((D, SPAN), BF16),
            pltpu.VMEM((D, SPAN), F32),
            pltpu.VMEM((1, SPAN), F32),
            pltpu.VMEM((AH, SPAN), F32),
            pltpu.VMEM((AH, SPAN), F32),
            pltpu.VMEM((AH, SPAN), F32),
            pltpu.VMEM((GS, SPAN), BF16),
        ],
        compiler_params=params(28),
        name="main",
    )(place, band_levels, recv, tall, wide)
    lats = lax.axis_size("lat")
    other = lax.ppermute(send, "lat", [(i, i ^ 1) for i in range(lats)])
    paired = pl.pallas_call(
        pair_kernel,
        out_shape=shape(HALF, ROW),
        in_specs=[VMEM] * 2,
        out_specs=VMEM,
        compiler_params=params(16),
        name="pair",
    )(keep, other)
    parts = lax.all_to_all(
        paired.reshape(ZED, HALF // ZED, ROW),
        "lat",
        0,
        0,
        tiled=True,
        axis_index_groups=[[2 * z + c for z in range(ZED)] for c in range(2)],
    )
    share = pl.pallas_call(
        sum_z_kernel,
        out_shape=shape(RING, SHARE, TOK),
        in_specs=[VMEM],
        out_specs=VMEM,
        scratch_shapes=[pltpu.VMEM((HALF // ZED, ROW), F32), pltpu.VMEM((RING, 16, TOK), F32)],
        compiler_params=params(16),
        name="sum_z",
    )(parts)
    shared = lax.all_to_all(share, "lon", 0, 0, tiled=True)
    kv_grad, embed_grad, query_grad = pl.pallas_call(
        sum_lon_kernel,
        out_shape=(shape(2, 2 * D, dtype=F32), shape(32, FEAT, dtype=F32), shape(LATENT, D, dtype=F32)),
        in_specs=[VMEM],
        out_specs=(VMEM,) * 3,
        scratch_shapes=[pltpu.VMEM((16, TOK), F32), pltpu.VMEM((TOK, 32), F32)],
        compiler_params=params(16),
        name="sum_lon",
    )(shared)
    return (kv_grad, embed_grad.T, query_grad)


def solution(mesh):
    placed = (P("lat", "lon", None), P(), P(), P(), P(), P("lat"), P("lat", "lon", None, None))
    return jax.shard_map(
        on_device,
        mesh=mesh,
        in_specs=placed,
        out_specs=(P(("lon", "lat"), None), P(None, "lat"), P()),
        check_vma=False,
    )
```

```python
import functools

import jax
import jax.numpy as jnp
from jax import lax
from jax.experimental import pallas as pl
from jax.experimental.pallas import tpu as pltpu
from jax.sharding import PartitionSpec as P

HEADS = 16
SCORE_SCALE = 0.125
EPSILON = 1e-05
MASKED = -1e30
BF16 = jnp.bfloat16
F32 = jnp.float32

LEVELS = 13
TOK = 128
PAIRS = 7
WIDE = 2 * TOK
SPAN = PAIRS * WIDE
D = 512
HEAD = D // HEADS
FEAT = 80
AUG = 96
LATENT = 3
AH = LATENT * HEADS
GS = 128
NT = (((1,), (1,)), ((), ()))
RING = 16
ZED = 8
HALF = D // 2
PACKED = 768
SHARE = 80
LAST = 48

VMEM = pl.BlockSpec(memory_space=pltpu.VMEM)
SMEM = pl.BlockSpec(memory_space=pltpu.SMEM)


def params(mib):
    return pltpu.CompilerParams(vmem_limit_bytes=mib * 1024 * 1024)


def shape(*dims, dtype=BF16):
    return jax.ShapeDtypeStruct(dims, dtype)


def slot_kernel(lon_ref, patch_ref, slot_ref):
    lon = lon_ref[0]
    for i in range(LEVELS):
        owner = lax.rem(lon * LEVELS + i, RING)
        slot_ref[owner] = patch_ref[:, i * TOK : (i + 1) * TOK]


def feature_of(position):
    core, lon, z, pair = position >> 8, (position >> 4) & 15, (position >> 1) & 7, position & 1
    return lon * 32 + z * 4 + core * 2 + pair


def prep_kernel(
    core_ref, kvw_ref, embed_w_ref, level_ref, query_ref, grad_ref,
    tall_ref, wide_ref,
    rows, spread,
):
    core = core_ref[0]
    down = lax.broadcasted_iota(jnp.int32, (D, D), 0)
    across = lax.broadcasted_iota(jnp.int32, (D, D), 1)
    reorder = jnp.where(feature_of(down) == across, 1.0, 0.0).astype(BF16)
    side = (core + (down >> 8)) & 1
    target = ((down >> 5) & 7) * 64 + side * 32 + (down & 31)
    wide_ref[:, 2 * D : 3 * D] = jnp.where(feature_of(across) == target, 1.0, 0.0).astype(BF16)
    for c in range(4):
        part = jnp.dot(reorder, kvw_ref[:, c * 256 : (c + 1) * 256], preferred_element_type=F32)
        wide_ref[:, c * 256 : (c + 1) * 256] = part.astype(BF16)
        tall_ref[c * 256 : (c + 1) * 256, :] = part.T.astype(BF16)
    rows[...] = jnp.zeros_like(rows)
    rows[:FEAT, :] = embed_w_ref[...].astype(F32)
    rows[FEAT : FEAT + LEVELS, :] = level_ref[...].astype(F32)
    weights = rows[...]
    weights = weights - jnp.mean(weights, axis=1, keepdims=True)
    high = weights.astype(BF16)
    spread[...] = jnp.zeros_like(spread)
    spread[:AUG, :] = high.astype(F32)
    spread[AUG : 2 * AUG, :] = weights - high.astype(F32)
    wide_ref[:, 3 * D : 3 * D + 256] = jnp.dot(
        reorder, spread[...].T.astype(BF16), preferred_element_type=F32
    ).astype(BF16)
    head = lax.broadcasted_iota(jnp.int32, (HEADS, D), 0)
    owner = lax.broadcasted_iota(jnp.int32, (HEADS, D), 1) >> 5
    spread[:32, :] = jnp.zeros((32, D), F32)
    for a in range(LATENT):
        block = jnp.where(head == owner, query_ref[a : a + 1, :].astype(F32), 0.0)
        spread[32 + a * HEADS : 32 + (a + 1) * HEADS, :] = block
        spread[80 + a * HEADS : 80 + (a + 1) * HEADS, :] = block
    tall_ref[2 * D : 2 * D + AH, :] = spread[80:128, :].astype(BF16)
    tall_ref[2 * D + AH :, :] = jnp.zeros((16, D), BF16)
    wide_ref[:, 3 * D + 256 : 3 * D + 384] = spread[:GS, :].T.astype(BF16)
    for a in range(LATENT):
        at = 4 * D + a * TOK
        wide_ref[:, at : at + TOK] = grad_ref[a].astype(F32).T.astype(BF16)


def main_kernel(
    place_ref, count_ref, recv_ref, tall_ref, wide_ref,
    keep_out, block_out, send_out,
    g2, paug_s, hid_s, kv_s, gkv_s, ge_s, nrm_s, inv_s, sc_s, ga_s, w_s, gs_s,
):
    lon = place_ref[0]
    core = place_ref[1]
    count = count_ref[0]
    for a in range(LATENT):
        wide = wide_ref[:, 4 * D + a * TOK : 4 * D + (a + 1) * TOK].astype(F32)
        g2[a, :, :TOK] = wide
        g2[a, :, TOK:] = wide
    gs_s[:32, :] = jnp.zeros((32, SPAN), BF16)

    def embed(p):
        at = slice(p * WIDE, (p + 1) * WIDE)
        first, second = 2 * p, min(2 * p + 1, LEVELS - 1)
        patches = jnp.concatenate(
            [recv_ref[(RING * first + lon) // LEVELS], recv_ref[(RING * second + lon) // LEVELS]], axis=1
        )
        row = lax.broadcasted_iota(jnp.int32, (AUG - FEAT, WIDE), 0)
        lane = lax.broadcasted_iota(jnp.int32, (AUG - FEAT, WIDE), 1)
        level = jnp.where(lane >= TOK, second, first)
        one_hot = jnp.where(row == level, 1.0, 0.0).astype(BF16)
        paug_s[:FEAT, at] = patches
        paug_s[FEAT:AUG, at] = one_hot
        paug_s[AUG : AUG + FEAT, at] = patches
        paug_s[AUG + FEAT :, at] = one_hot
        center = jnp.dot(
            wide_ref[:, 3 * D : 3 * D + 2 * AUG], paug_s[:, at], preferred_element_type=F32
        )
        inv_std = lax.rsqrt(jnp.mean(center * center, axis=0, keepdims=True) + EPSILON)
        normed = center * inv_std
        inv_s[:, at] = inv_std
        nrm_s[:, at] = normed
        hid_s[:, at] = normed.astype(BF16)

    def score(p):
        at = slice(p * WIDE, (p + 1) * WIDE)
        kv_s[:, at] = jnp.dot(tall_ref[: 2 * D, :], hid_s[:, at], preferred_element_type=F32).astype(BF16)
        sc_s[:, at] = (
            jnp.dot(tall_ref[2 * D : 2 * D + AH, :], kv_s[:D, at], preferred_element_type=F32) * SCORE_SCALE
        )
        values = kv_s[D:, at].astype(F32)
        for a in range(LATENT):
            product = (g2[a] * values).reshape(HEADS, HEAD, WIDE)
            ga_s[a * HEADS : (a + 1) * HEADS, at] = jnp.sum(product, axis=1)

    embed(0)
    for p in range(PAIRS):
        if p + 1 < PAIRS:
            embed(p + 1)
        score(p)

    masked = [
        jnp.where(l < count, sc_s[:, l * TOK : (l + 1) * TOK], MASKED) for l in range(LEVELS)
    ]
    peak = functools.reduce(jnp.maximum, masked)
    total = jnp.zeros_like(peak)
    for l in range(LEVELS):
        exponent = jnp.exp(masked[l] - peak)
        sc_s[:, l * TOK : (l + 1) * TOK] = exponent
        total = total + exponent
    inverse = 1.0 / total
    inner = jnp.zeros_like(peak)
    for l in range(LEVELS):
        lanes = slice(l * TOK, (l + 1) * TOK)
        attention = sc_s[:, lanes] * inverse
        sc_s[:, lanes] = attention
        w_s[:, lanes] = attention.astype(BF16).astype(F32)
        inner = inner + attention * ga_s[:, lanes]
    for l in range(LEVELS):
        lanes = slice(l * TOK, (l + 1) * TOK)
        grad_score = sc_s[:, lanes] * (ga_s[:, lanes] - inner) * SCORE_SCALE
        high = grad_score.astype(BF16)
        gs_s[32:80, lanes] = (grad_score - high.astype(F32)).astype(BF16)
        gs_s[80:, lanes] = high
    tail = slice(LEVELS * TOK, SPAN)
    w_s[:, tail] = jnp.zeros((AH, TOK), F32)
    gs_s[32:, tail] = jnp.zeros((2 * AH, TOK), BF16)

    def grad_kv(p):
        at = slice(p * WIDE, (p + 1) * WIDE)
        gkv_s[:D, at] = jnp.dot(
            wide_ref[:, 3 * D + 256 : 3 * D + 384], gs_s[:, at], preferred_element_type=F32
        ).astype(BF16)
        grad_values = None
        for a in range(LATENT):
            weight = w_s[a * HEADS : (a + 1) * HEADS, at].reshape(HEADS, 1, WIDE)
            term = weight * g2[a].reshape(HEADS, HEAD, WIDE)
            grad_values = term if grad_values is None else grad_values + term
        gkv_s[D:, at] = grad_values.reshape(D, WIDE).astype(BF16)

    def embed_back(p):
        at = slice(p * WIDE, (p + 1) * WIDE)
        grad_hidden = jnp.dot(wide_ref[:, : 2 * D], gkv_s[:, at], preferred_element_type=F32)
        normed = nrm_s[:, at]
        mean = jnp.mean(grad_hidden, axis=0, keepdims=True)
        slope = jnp.mean(grad_hidden * normed, axis=0, keepdims=True)
        ge_s[:, at] = (inv_s[:, at] * (grad_hidden - mean - normed * slope)).astype(BF16)

    grad_kv(0)
    for p in range(PAIRS):
        if p + 1 < PAIRS:
            grad_kv(p + 1)
        embed_back(p)

    mine = hid_s[pl.ds(pl.multiple_of(core * HALF, HALF), HALF), :]
    other = hid_s[pl.ds(pl.multiple_of((1 - core) * HALF, HALF), HALF), :]
    for c in range(4):
        at = slice(c * WIDE, (c + 1) * WIDE)
        send_out[:HALF, at] = lax.dot_general(other, gkv_s[at, :], NT, preferred_element_type=F32).astype(BF16)
        keep_out[:, at] = lax.dot_general(mine, gkv_s[at, :], NT, preferred_element_type=F32)
    grads = lax.dot_general(ge_s[...], paug_s[:GS, :], NT, preferred_element_type=F32).astype(BF16)
    grads = jnp.dot(wide_ref[:, 2 * D : 3 * D], grads, preferred_element_type=F32)
    queries = lax.dot_general(kv_s[:D, :], gs_s[...], NT, preferred_element_type=F32)
    head = lax.broadcasted_iota(jnp.int32, (D, GS), 0) >> 5
    lane = lax.broadcasted_iota(jnp.int32, (D, GS), 1)
    queries = jnp.where((lane & 15) == head, queries, 0.0).reshape(HEADS, HEAD, GS)
    queries = jnp.sum(queries, axis=0)
    queries = queries[:, 80:GS] + queries[:, 32:80]
    blank = jnp.zeros((HEAD, PACKED - ZED * FEAT - AH), F32)

    def packed(half):
        parts = [grads[half * HALF + z * HEAD : half * HALF + (z + 1) * HEAD, :FEAT] for z in range(ZED)]
        return jnp.concatenate(parts + [queries, blank], axis=1)

    block_out[...] = packed(0)
    send_out[HALF:, :PACKED] = packed(1).astype(BF16)
    send_out[HALF:, PACKED:] = jnp.zeros((HEAD, 2 * D - PACKED), BF16)


def pair_kernel(keep_ref, block_ref, recv_ref, share_ref):
    for target in range(RING):
        rows = slice(target * 16, (target + 1) * 16)
        total = (keep_ref[rows, :] + recv_ref[rows, :].astype(F32)).astype(BF16)
        share_ref[target, 0:16, :] = total[:, :D]
        share_ref[target, 16:32, :] = total[:, D:]
    block = (block_ref[...] + recv_ref[HALF:, :PACKED].astype(F32)).astype(BF16)
    for target in range(RING):
        share_ref[target, 32:64, :] = block[:, :D]
        share_ref[target, 64:80, :256] = block[:16, D:PACKED]
        share_ref[target, 64:80, 256:] = block[16:, D:PACKED]


def sum_lon_kernel(share_ref, last_ref, total, tile):
    acc = share_ref[0].astype(F32)
    for source in range(1, RING):
        acc = acc + share_ref[source].astype(F32)
    total[...] = acc[:32]
    block = jnp.concatenate(
        [acc[32:64], jnp.concatenate([acc[64:80, :256], acc[64:80, 256:]], axis=0)], axis=1
    )
    queries = block[:, ZED * FEAT : ZED * FEAT + AH]
    for z in range(ZED):
        for c in range(8):
            row = 16 * (c // 4) + 2 * z
            tile[z, 2 * c : 2 * c + 2, :] = total[row : row + 2, (c % 4) * TOK : (c % 4 + 1) * TOK]
        last_ref[z, 0:16, :] = tile[z].astype(BF16)
        last_ref[z, 16:48, :] = jnp.concatenate(
            [block[:, z * FEAT : (z + 1) * FEAT], queries], axis=1
        ).astype(BF16)


def sum_z_kernel(last_ref, kv_out, embed_out, query_out, tile, turned):
    acc = last_ref[0].astype(F32)
    for source in range(1, ZED):
        acc = acc + last_ref[source].astype(F32)
    tile[...] = acc[:16]
    for c in range(8):
        kv_out[:, c * TOK : (c + 1) * TOK] = tile[2 * c : 2 * c + 2, :]
    embed_out[...] = acc[16:, :FEAT]
    turned[...] = acc[16:, :].T
    for a in range(LATENT):
        for h in range(HEADS):
            at = FEAT + a * HEADS + h
            query_out[a : a + 1, h * HEAD : (h + 1) * HEAD] = turned[at : at + 1, :]


def on_device(level_patches, level_embed, embed_weight, kv_weight, query, band_levels, grad_out):
    lon = lax.axis_index("lon").astype(jnp.int32)
    core = (lax.axis_index("lat") % 2).astype(jnp.int32)
    place = jnp.stack([lon, core])
    slots = pl.pallas_call(
        slot_kernel,
        out_shape=shape(RING, FEAT, TOK),
        in_specs=[SMEM, VMEM],
        out_specs=VMEM,
        compiler_params=params(16),
        name="slots",
    )(lon.reshape(1), level_patches[0].T)
    tall, wide = pl.pallas_call(
        prep_kernel,
        out_shape=(shape(2 * D + 64, D), shape(D, 4 * D + LATENT * TOK)),
        in_specs=[SMEM] + [VMEM] * 5,
        out_specs=(VMEM,) * 2,
        scratch_shapes=[pltpu.VMEM((AUG, D), F32), pltpu.VMEM((256, D), F32)],
        compiler_params=params(24),
        name="prep",
    )(core.reshape(1), kv_weight, embed_weight, level_embed, query, grad_out[0].transpose(1, 0, 2))
    recv = lax.all_to_all(slots, "lon", 0, 0, tiled=True)
    keep, block, send = pl.pallas_call(
        main_kernel,
        out_shape=(
            shape(HALF, 2 * D, dtype=F32),
            shape(HEAD, PACKED, dtype=F32),
            shape(HALF + HEAD, 2 * D),
        ),
        in_specs=[SMEM, SMEM] + [VMEM] * 3,
        out_specs=(VMEM,) * 3,
        scratch_shapes=[
            pltpu.VMEM((LATENT, D, WIDE), F32),
            pltpu.VMEM((2 * AUG, SPAN), BF16),
            pltpu.VMEM((D, SPAN), BF16),
            pltpu.VMEM((2 * D, SPAN), BF16),
            pltpu.VMEM((2 * D, SPAN), BF16),
            pltpu.VMEM((D, SPAN), BF16),
            pltpu.VMEM((D, SPAN), F32),
            pltpu.VMEM((1, SPAN), F32),
            pltpu.VMEM((AH, SPAN), F32),
            pltpu.VMEM((AH, SPAN), F32),
            pltpu.VMEM((AH, SPAN), F32),
            pltpu.VMEM((GS, SPAN), BF16),
        ],
        compiler_params=params(28),
        name="main",
    )(place, band_levels, recv, tall, wide)
    lats = lax.axis_size("lat")
    other = lax.ppermute(send, "lat", [(i, i ^ 1) for i in range(lats)])
    share = pl.pallas_call(
        pair_kernel,
        out_shape=shape(RING, SHARE, D),
        in_specs=[VMEM] * 3,
        out_specs=VMEM,
        compiler_params=params(16),
        name="pair",
    )(keep, block, other)
    shared = lax.all_to_all(share, "lon", 0, 0, tiled=True)
    last = pl.pallas_call(
        sum_lon_kernel,
        out_shape=shape(ZED, LAST, TOK),
        in_specs=[VMEM],
        out_specs=VMEM,
        scratch_shapes=[pltpu.VMEM((32, D), F32), pltpu.VMEM((ZED, 16, TOK), F32)],
        compiler_params=params(16),
        name="sum_lon",
    )(shared)
    lasts = lax.all_to_all(
        last,
        "lat",
        0,
        0,
        tiled=True,
        axis_index_groups=[[2 * z + c for z in range(ZED)] for c in range(2)],
    )
    kv_grad, embed_grad, query_grad = pl.pallas_call(
        sum_z_kernel,
        out_shape=(shape(2, 2 * D, dtype=F32), shape(32, FEAT, dtype=F32), shape(LATENT, D, dtype=F32)),
        in_specs=[VMEM],
        out_specs=(VMEM,) * 3,
        scratch_shapes=[pltpu.VMEM((16, TOK), F32), pltpu.VMEM((TOK, 32), F32)],
        compiler_params=params(16),
        name="sum_z",
    )(lasts)
    return (kv_grad, embed_grad.T, query_grad)


def solution(mesh):
    placed = (P("lat", "lon", None), P(), P(), P(), P(), P("lat"), P("lat", "lon", None, None))
    return jax.shard_map(
        on_device,
        mesh=mesh,
        in_specs=placed,
        out_specs=(P(("lon", "lat"), None), P(None, "lat"), P()),
        check_vma=False,
    )
```

```python
import functools

import jax
import jax.numpy as jnp
from jax import lax
from jax.experimental import pallas as pl
from jax.experimental.pallas import tpu as pltpu
from jax.sharding import PartitionSpec as P

HEADS = 16
SCORE_SCALE = 0.125
EPSILON = 1e-05
MASKED = -1e30
BF16 = jnp.bfloat16
F32 = jnp.float32

LEVELS = 13
TOK = 128
PAIRS = 7
WIDE = 2 * TOK
SPAN = PAIRS * WIDE
D = 512
HEAD = D // HEADS
FEAT = 80
AUG = 96
LATENT = 3
AH = LATENT * HEADS
GS = 128
NT = (((1,), (1,)), ((), ()))
RING = 16
ZED = 8
HALF = D // 2
WAUG = 0
QBD = 256
GRAD = 384
PLAIN = 768

VMEM = pl.BlockSpec(memory_space=pltpu.VMEM)
SMEM = pl.BlockSpec(memory_space=pltpu.SMEM)


def params(mib):
    return pltpu.CompilerParams(vmem_limit_bytes=mib * 1024 * 1024)


def shape(*dims, dtype=BF16):
    return jax.ShapeDtypeStruct(dims, dtype)


def slot_kernel(lon_ref, patch_ref, slot_ref):
    lon = lon_ref[0]
    for i in range(LEVELS):
        owner = lax.rem(lon * LEVELS + i, RING)
        slot_ref[owner] = patch_ref[:, i * TOK : (i + 1) * TOK]


def prep_kernel(kvw_ref, embed_w_ref, level_ref, query_ref, grad_ref, tall_ref, wide_ref, rows, spread):
    position = lax.broadcasted_iota(jnp.int32, (D, D), 0)
    feature = lax.broadcasted_iota(jnp.int32, (D, D), 1)
    core, lon, z, pair = position >> 8, (position >> 4) & 15, (position >> 1) & 7, position & 1
    reorder = jnp.where(lon * 32 + z * 4 + core * 2 + pair == feature, 1.0, 0.0).astype(BF16)
    for c in range(4):
        part = jnp.dot(reorder, kvw_ref[:, c * 256 : (c + 1) * 256], preferred_element_type=F32)
        tall_ref[c * 256 : (c + 1) * 256, :] = part.T.astype(BF16)
    rows[...] = jnp.zeros_like(rows)
    rows[:FEAT, :] = embed_w_ref[...].astype(F32)
    rows[FEAT : FEAT + LEVELS, :] = level_ref[...].astype(F32)
    weights = rows[...]
    weights = weights - jnp.mean(weights, axis=1, keepdims=True)
    high = weights.astype(BF16)
    spread[...] = jnp.zeros_like(spread)
    spread[:AUG, :] = high.astype(F32)
    spread[AUG : 2 * AUG, :] = weights - high.astype(F32)
    plain = spread[...].T.astype(BF16)
    wide_ref[:, PLAIN : PLAIN + 256] = plain
    wide_ref[:, WAUG : WAUG + 256] = jnp.dot(reorder, plain, preferred_element_type=F32).astype(BF16)
    head = lax.broadcasted_iota(jnp.int32, (HEADS, D), 0)
    owner = lax.broadcasted_iota(jnp.int32, (HEADS, D), 1) >> 5
    spread[:32, :] = jnp.zeros((32, D), F32)
    for a in range(LATENT):
        block = jnp.where(head == owner, query_ref[a : a + 1, :].astype(F32), 0.0)
        spread[32 + a * HEADS : 32 + (a + 1) * HEADS, :] = block
        spread[80 + a * HEADS : 80 + (a + 1) * HEADS, :] = block
    tall_ref[2 * D : 2 * D + AH, :] = spread[80:128, :].astype(BF16)
    tall_ref[2 * D + AH :, :] = jnp.zeros((16, D), BF16)
    wide_ref[:, QBD : QBD + GS] = spread[:GS, :].T.astype(BF16)
    for a in range(LATENT):
        at = GRAD + a * TOK
        wide_ref[:, at : at + TOK] = grad_ref[a].astype(F32).T.astype(BF16)


def main_kernel(
    lon_ref, count_ref, recv_ref, kvw_ref, tall_ref, wide_ref,
    hid_s, gkv_s, eq_out,
    g2, paug_s, kv_s, pin_s, inv_s, sc_s, ga_s, w_s, gs_s, xs_s,
):
    lon = lon_ref[0]
    count = count_ref[0]
    for a in range(LATENT):
        wide = wide_ref[:, GRAD + a * TOK : GRAD + (a + 1) * TOK].astype(F32)
        g2[a, :, :TOK] = wide
        g2[a, :, TOK:] = wide
    gs_s[:32, :] = jnp.zeros((32, SPAN), BF16)
    pin_s[FEAT:, :] = jnp.zeros((TOK - FEAT, SPAN), BF16)

    def embed(p):
        at = slice(p * WIDE, (p + 1) * WIDE)
        first, second = 2 * p, min(2 * p + 1, LEVELS - 1)
        patches = jnp.concatenate(
            [recv_ref[(RING * first + lon) // LEVELS], recv_ref[(RING * second + lon) // LEVELS]], axis=1
        )
        row = lax.broadcasted_iota(jnp.int32, (AUG - FEAT, WIDE), 0)
        lane = lax.broadcasted_iota(jnp.int32, (AUG - FEAT, WIDE), 1)
        level = jnp.where(lane >= TOK, second, first)
        one_hot = jnp.where(row == level, 1.0, 0.0).astype(BF16)
        paug_s[:FEAT, at] = patches
        paug_s[FEAT:AUG, at] = one_hot
        paug_s[AUG : AUG + FEAT, at] = patches
        paug_s[AUG + FEAT :, at] = one_hot
        center = jnp.dot(wide_ref[:, WAUG : WAUG + 2 * AUG], paug_s[:, at], preferred_element_type=F32)
        inv_std = lax.rsqrt(jnp.mean(center * center, axis=0, keepdims=True) + EPSILON)
        inv_s[:, at] = inv_std
        hid_s[:, at] = (center * inv_std).astype(BF16)
        pin_s[:FEAT, at] = (patches.astype(F32) * inv_std).astype(BF16)

    def score(p):
        at = slice(p * WIDE, (p + 1) * WIDE)
        kv_s[:, at] = jnp.dot(tall_ref[: 2 * D, :], hid_s[:, at], preferred_element_type=F32).astype(BF16)
        sc_s[:, at] = (
            jnp.dot(tall_ref[2 * D : 2 * D + AH, :], kv_s[:D, at], preferred_element_type=F32) * SCORE_SCALE
        )
        values = kv_s[D:, at].astype(F32)
        for a in range(LATENT):
            product = (g2[a] * values).reshape(HEADS, HEAD, WIDE)
            ga_s[a * HEADS : (a + 1) * HEADS, at] = jnp.sum(product, axis=1)

    embed(0)
    for p in range(PAIRS):
        if p + 1 < PAIRS:
            embed(p + 1)
        score(p)

    masked = [jnp.where(l < count, sc_s[:, l * TOK : (l + 1) * TOK], MASKED) for l in range(LEVELS)]
    peak = functools.reduce(jnp.maximum, masked)
    total = jnp.zeros_like(peak)
    for l in range(LEVELS):
        exponent = jnp.exp(masked[l] - peak)
        w_s[:, l * TOK : (l + 1) * TOK] = exponent
        total = total + exponent
    inverse = 1.0 / total
    inner = jnp.zeros_like(peak)
    for l in range(LEVELS):
        lanes = slice(l * TOK, (l + 1) * TOK)
        inner = inner + w_s[:, lanes] * inverse * ga_s[:, lanes]
    for l in range(LEVELS):
        lanes = slice(l * TOK, (l + 1) * TOK)
        attention = w_s[:, lanes] * inverse
        weight = attention.astype(BF16).astype(F32)
        w_s[:, lanes] = weight
        grad_attn = ga_s[:, lanes]
        grad_score = attention * (grad_attn - inner)
        slope = jnp.sum(grad_score * sc_s[:, lanes] + weight * grad_attn, axis=0, keepdims=True)
        scale = slope * inv_s[:, lanes] * (1.0 / D)
        xs_s[:, lanes] = (paug_s[:AUG, lanes].astype(F32) * scale).astype(BF16)
        grad_score = grad_score * SCORE_SCALE
        high = grad_score.astype(BF16)
        gs_s[32:80, lanes] = (grad_score - high.astype(F32)).astype(BF16)
        gs_s[80:, lanes] = high
    tail = slice(LEVELS * TOK, SPAN)
    w_s[:, tail] = jnp.zeros((AH, TOK), F32)
    gs_s[32:, tail] = jnp.zeros((2 * AH, TOK), BF16)
    xs_s[:, tail] = jnp.zeros((AUG, TOK), BF16)

    for p in range(PAIRS):
        at = slice(p * WIDE, (p + 1) * WIDE)
        gkv_s[:D, at] = jnp.dot(
            wide_ref[:, QBD : QBD + GS], gs_s[:, at], preferred_element_type=F32
        ).astype(BF16)
        grad_values = None
        for a in range(LATENT):
            weight = w_s[a * HEADS : (a + 1) * HEADS, at].reshape(HEADS, 1, WIDE)
            term = weight * g2[a].reshape(HEADS, HEAD, WIDE)
            grad_values = term if grad_values is None else grad_values + term
        gkv_s[D:, at] = grad_values.reshape(D, WIDE).astype(BF16)

    outer = lax.dot_general(gkv_s[...], pin_s[...], NT, preferred_element_type=F32)
    high = outer.astype(BF16)
    low = (outer - high.astype(F32)).astype(BF16)
    grads = jnp.dot(kvw_ref[...], jnp.concatenate([high, low], axis=1), preferred_element_type=F32)
    grads = grads[:, :TOK] + grads[:, TOK:]
    gram = lax.dot_general(xs_s[...], pin_s[...], NT, preferred_element_type=F32).astype(BF16)
    grads = grads - jnp.dot(
        wide_ref[:, PLAIN : PLAIN + 2 * AUG], jnp.concatenate([gram, gram], axis=0), preferred_element_type=F32
    )
    grads = grads - jnp.mean(grads, axis=0, keepdims=True)
    queries = lax.dot_general(kv_s[:D, :], gs_s[...], NT, preferred_element_type=F32)
    head = lax.broadcasted_iota(jnp.int32, (D, GS), 0) >> 5
    lane = lax.broadcasted_iota(jnp.int32, (D, GS), 1)
    queries = jnp.where((lane & 15) == head, queries, 0.0).reshape(HEADS, HEAD, GS)
    queries = jnp.sum(queries, axis=0)
    queries = queries + pltpu.roll(queries, AH, 1)
    queries = jnp.concatenate([queries] * HEADS, axis=0)
    eq_out[...] = jnp.where(lane < FEAT, grads, queries).astype(BF16)


def project_kernel(core_ref, hid_ref, gkv_ref, keep_out, send_out):
    core = core_ref[0]
    mine = hid_ref[pl.ds(pl.multiple_of(core * HALF, HALF), HALF), :]
    other = hid_ref[pl.ds(pl.multiple_of((1 - core) * HALF, HALF), HALF), :]
    for c in range(4):
        at = slice(c * WIDE, (c + 1) * WIDE)
        send_out[:, at] = lax.dot_general(other, gkv_ref[at, :], NT, preferred_element_type=F32).astype(BF16)
        keep_out[:, at] = lax.dot_general(mine, gkv_ref[at, :], NT, preferred_element_type=F32)


def pair_kernel(keep_ref, recv_ref, eq_ref, share_ref):
    for target in range(RING):
        rows = slice(target * 16, (target + 1) * 16)
        share_ref[target, :, : 2 * D] = (keep_ref[rows, :] + recv_ref[rows, :].astype(F32)).astype(BF16)
    block = eq_ref[0].astype(F32)
    for source in range(1, RING):
        block = block + eq_ref[source].astype(F32)
    block = block.astype(BF16)
    for target in range(RING):
        share_ref[target, :, 2 * D : 2 * D + TOK] = block[:16]
        share_ref[target, :, 2 * D + TOK :] = block[16:]


def sum_lon_kernel(share_ref, last_ref, embed_out, query_out, total, tile, turned):
    acc = share_ref[0].astype(F32)
    for source in range(1, RING):
        acc = acc + share_ref[source].astype(F32)
    total[...] = acc
    for z in range(ZED):
        for c in range(8):
            tile[z, 2 * c : 2 * c + 2, :] = total[2 * z : 2 * z + 2, c * TOK : (c + 1) * TOK]
        last_ref[z] = tile[z].astype(BF16)
    block = jnp.concatenate([acc[:, 2 * D : 2 * D + TOK], acc[:, 2 * D + TOK :]], axis=0)
    embed_out[...] = block[:, :FEAT]
    turned[...] = block.T
    for a in range(LATENT):
        for h in range(HEADS):
            at = FEAT + a * HEADS + h
            query_out[a : a + 1, h * HEAD : (h + 1) * HEAD] = turned[at : at + 1, :]


def sum_z_kernel(last_ref, kv_out, tile):
    acc = last_ref[0].astype(F32)
    for source in range(1, ZED):
        acc = acc + last_ref[source].astype(F32)
    tile[...] = acc
    for c in range(8):
        kv_out[:, c * TOK : (c + 1) * TOK] = tile[2 * c : 2 * c + 2, :]


def call(kernel, outs, in_specs, scratch, mib, name, flops=10**8, size=10**6):
    return pl.pallas_call(
        kernel,
        out_shape=outs,
        in_specs=in_specs,
        out_specs=jax.tree.map(lambda _: VMEM, outs),
        scratch_shapes=scratch,
        compiler_params=params(mib),
        cost_estimate=pl.CostEstimate(flops=flops, bytes_accessed=size, transcendentals=0),
        name=name,
    )


def on_device(level_patches, level_embed, embed_weight, kv_weight, query, band_levels, grad_out):
    lon = lax.axis_index("lon").astype(jnp.int32).reshape(1)
    core = (lax.axis_index("lat").astype(jnp.int32) & 1).reshape(1)
    slots = call(slot_kernel, shape(RING, FEAT, TOK), [SMEM, VMEM], [], 16, "slots")(lon, level_patches[0].T)
    tall, wide = call(
        prep_kernel,
        (shape(2 * D + 64, D), shape(D, 2 * D)),
        [VMEM] * 5,
        [pltpu.VMEM((AUG, D), F32), pltpu.VMEM((256, D), F32)],
        24,
        "prep",
    )(kv_weight, embed_weight, level_embed, query, grad_out[0].transpose(1, 0, 2))
    recv = lax.all_to_all(slots, "lon", 0, 0, tiled=True)
    hidden, grad_kv, block = call(
        main_kernel,
        (shape(D, SPAN), shape(2 * D, SPAN), shape(D, TOK)),
        [SMEM, SMEM] + [VMEM] * 4,
        [
            pltpu.VMEM((LATENT, D, WIDE), F32),
            pltpu.VMEM((2 * AUG, SPAN), BF16),
            pltpu.VMEM((2 * D, SPAN), BF16),
            pltpu.VMEM((TOK, SPAN), BF16),
            pltpu.VMEM((1, SPAN), F32),
            pltpu.VMEM((AH, SPAN), F32),
            pltpu.VMEM((AH, SPAN), F32),
            pltpu.VMEM((AH, SPAN), F32),
            pltpu.VMEM((GS, SPAN), BF16),
            pltpu.VMEM((AUG, SPAN), BF16),
        ],
        24,
        "main",
    )(lon, band_levels, recv, kv_weight, tall, wide)
    blocks = lax.all_to_all(block.reshape(RING, D // RING, TOK), "lat", 0, 0, tiled=True)
    keep, send = call(
        project_kernel,
        (shape(HALF, 2 * D, dtype=F32), shape(HALF, 2 * D)),
        [SMEM] + [VMEM] * 2,
        [],
        16,
        "project",
        4 * 10**9,
        8 * 10**6,
    )(core, hidden, grad_kv)
    lats = lax.axis_size("lat")
    other = lax.ppermute(send, "lat", [(i, i ^ 1) for i in range(lats)])
    share = call(pair_kernel, shape(RING, 16, 2 * D + 2 * TOK), [VMEM] * 3, [], 16, "pair")(keep, other, blocks)
    shared = lax.all_to_all(share, "lon", 0, 0, tiled=True)
    last, embed_grad, query_grad = call(
        sum_lon_kernel,
        (shape(ZED, 16, TOK), shape(32, FEAT, dtype=F32), shape(LATENT, D, dtype=F32)),
        [VMEM],
        [
            pltpu.VMEM((16, 2 * D + 2 * TOK), F32),
            pltpu.VMEM((ZED, 16, TOK), F32),
            pltpu.VMEM((TOK, 32), F32),
        ],
        16,
        "sum_lon",
    )(shared)
    lasts = lax.all_to_all(
        last,
        "lat",
        0,
        0,
        tiled=True,
        axis_index_groups=[[2 * z + c for z in range(ZED)] for c in range(2)],
    )
    kv_grad = call(
        sum_z_kernel, shape(2, 2 * D, dtype=F32), [VMEM], [pltpu.VMEM((16, TOK), F32)], 16, "sum_z"
    )(lasts)
    return (kv_grad, embed_grad.T, query_grad)


def solution(mesh):
    placed = (P("lat", "lon", None), P(), P(), P(), P(), P("lat"), P("lat", "lon", None, None))
    return jax.shard_map(
        on_device,
        mesh=mesh,
        in_specs=placed,
        out_specs=(P(("lon", "lat"), None), P(None, "lat"), P()),
        check_vma=False,
    )
```

```python
import functools

import jax
import jax.numpy as jnp
from jax import lax
from jax.experimental import pallas as pl
from jax.experimental.pallas import tpu as pltpu
from jax.sharding import PartitionSpec as P

HEADS = 16
SCORE_SCALE = 0.125
EPSILON = 1e-05
MASKED = -1e30
BF16 = jnp.bfloat16
F32 = jnp.float32

LEVELS = 13
TOK = 128
PAIRS = 7
WIDE = 2 * TOK
SPAN = PAIRS * WIDE
D = 512
HEAD = D // HEADS
FEAT = 80
AUG = 96
LATENT = 3
AH = LATENT * HEADS
GS = 128
NT = (((1,), (1,)), ((), ()))
RING = 16
ZED = 8
HALF = D // 2
WAUG = 0
QBD = 256
GRAD = 384
PLAIN = 768
DEEP = 256
ROW = 2 * D + TOK
SHARE = 48

VMEM = pl.BlockSpec(memory_space=pltpu.VMEM)
SMEM = pl.BlockSpec(memory_space=pltpu.SMEM)
HBM = pl.BlockSpec(memory_space=pltpu.HBM)


def params(mib):
    return pltpu.CompilerParams(vmem_limit_bytes=mib * 1024 * 1024)


def shape(*dims, dtype=BF16):
    return jax.ShapeDtypeStruct(dims, dtype)


def slot_kernel(lon_ref, patch_ref, slot_ref, sems):
    lon = lon_ref[0]
    copies = [
        pltpu.make_async_copy(
            patch_ref.at[:, pl.ds(i * TOK, TOK)], slot_ref.at[lax.rem(lon * LEVELS + i, RING)], sems.at[i]
        )
        for i in range(LEVELS)
    ]
    for copy in copies:
        copy.start()
    for copy in copies:
        copy.wait()


def prep_kernel(kvw_ref, embed_w_ref, level_ref, query_ref, grad_ref, tall_ref, wide_ref, rows, spread):
    position = lax.broadcasted_iota(jnp.int32, (D, D), 0)
    feature = lax.broadcasted_iota(jnp.int32, (D, D), 1)
    core, z, lon, pair = position >> 8, (position >> 5) & 7, (position >> 1) & 15, position & 1
    reorder = jnp.where(lon * 32 + z * 4 + core * 2 + pair == feature, 1.0, 0.0).astype(BF16)
    for c in range(4):
        part = jnp.dot(reorder, kvw_ref[:, c * 256 : (c + 1) * 256], preferred_element_type=F32)
        tall_ref[c * 256 : (c + 1) * 256, :] = part.T.astype(BF16)
    rows[...] = jnp.zeros_like(rows)
    rows[:FEAT, :] = embed_w_ref[...].astype(F32)
    rows[FEAT : FEAT + LEVELS, :] = level_ref[...].astype(F32)
    weights = rows[...]
    weights = weights - jnp.mean(weights, axis=1, keepdims=True)
    high = weights.astype(BF16)
    spread[...] = jnp.zeros_like(spread)
    spread[:AUG, :] = high.astype(F32)
    spread[TOK : TOK + AUG, :] = weights - high.astype(F32)
    plain = spread[...].T.astype(BF16)
    wide_ref[:, PLAIN : PLAIN + 256] = plain
    wide_ref[:, WAUG : WAUG + 256] = jnp.dot(reorder, plain, preferred_element_type=F32).astype(BF16)
    head = lax.broadcasted_iota(jnp.int32, (HEADS, D), 0)
    owner = lax.broadcasted_iota(jnp.int32, (HEADS, D), 1) >> 5
    spread[:32, :] = jnp.zeros((32, D), F32)
    for a in range(LATENT):
        block = jnp.where(head == owner, query_ref[a : a + 1, :].astype(F32), 0.0)
        spread[32 + a * HEADS : 32 + (a + 1) * HEADS, :] = block
        spread[80 + a * HEADS : 80 + (a + 1) * HEADS, :] = block
    tall_ref[2 * D : 2 * D + AH, :] = spread[80:128, :].astype(BF16)
    tall_ref[2 * D + AH :, :] = jnp.zeros((16, D), BF16)
    wide_ref[:, QBD : QBD + GS] = spread[:GS, :].T.astype(BF16)
    for a in range(LATENT):
        at = GRAD + a * TOK
        wide_ref[:, at : at + TOK] = grad_ref[a].astype(F32).T.astype(BF16)


def main_kernel(
    place_ref, count_ref, recv_ref, kvw_ref, tall_ref, wide_ref,
    keep_out, send_out,
    g2, paug_s, hid_s, kv_s, gkv_s, pin_s, inv_s, sc_s, ga_s, w_s, gs_s, xs_s, eq_s,
):
    lon = place_ref[0]
    core = place_ref[1]
    count = count_ref[0]
    for a in range(LATENT):
        wide = wide_ref[:, GRAD + a * TOK : GRAD + (a + 1) * TOK].astype(F32)
        g2[a, :, :TOK] = wide
        g2[a, :, TOK:] = wide
    gs_s[:32, :] = jnp.zeros((32, SPAN), BF16)
    pin_s[AUG:, :] = jnp.zeros((TOK - AUG, SPAN), BF16)
    paug_s[AUG:TOK, :] = jnp.zeros((TOK - AUG, SPAN), BF16)
    paug_s[TOK + AUG :, :] = jnp.zeros((TOK - AUG, SPAN), BF16)

    def embed(p):
        at = slice(p * WIDE, (p + 1) * WIDE)
        first, second = 2 * p, min(2 * p + 1, LEVELS - 1)
        patches = jnp.concatenate(
            [recv_ref[(RING * first + lon) // LEVELS], recv_ref[(RING * second + lon) // LEVELS]], axis=1
        )
        row = lax.broadcasted_iota(jnp.int32, (AUG - FEAT, WIDE), 0)
        lane = lax.broadcasted_iota(jnp.int32, (AUG - FEAT, WIDE), 1)
        level = jnp.where(lane >= TOK, second, first)
        one_hot = jnp.where(row == level, 1.0, 0.0).astype(BF16)
        paug_s[:FEAT, at] = patches
        paug_s[FEAT:AUG, at] = one_hot
        paug_s[TOK : TOK + FEAT, at] = patches
        paug_s[TOK + FEAT : TOK + AUG, at] = one_hot
        center = jnp.dot(wide_ref[:, WAUG : WAUG + DEEP], paug_s[:, at], preferred_element_type=F32)
        inv_std = lax.rsqrt(jnp.mean(center * center, axis=0, keepdims=True) + EPSILON)
        inv_s[:, at] = inv_std
        hid_s[:, at] = (center * inv_std).astype(BF16)
        pin_s[:FEAT, at] = (patches.astype(F32) * inv_std).astype(BF16)
        pin_s[FEAT:AUG, at] = jnp.where(row == level, inv_std, 0.0).astype(BF16)

    def score(p):
        at = slice(p * WIDE, (p + 1) * WIDE)
        kv_s[:, at] = jnp.dot(tall_ref[: 2 * D, :], hid_s[:, at], preferred_element_type=F32).astype(BF16)
        sc_s[:, at] = (
            jnp.dot(tall_ref[2 * D : 2 * D + AH, :], kv_s[:D, at], preferred_element_type=F32) * SCORE_SCALE
        )
        values = kv_s[D:, at].astype(F32)
        for a in range(LATENT):
            product = (g2[a] * values).reshape(HEADS, HEAD, WIDE)
            ga_s[a * HEADS : (a + 1) * HEADS, at] = jnp.sum(product, axis=1)

    embed(0)
    for p in range(PAIRS):
        if p + 1 < PAIRS:
            embed(p + 1)
        score(p)

    masked = [jnp.where(l < count, sc_s[:, l * TOK : (l + 1) * TOK], MASKED) for l in range(LEVELS)]
    peak = functools.reduce(jnp.maximum, masked)
    total = jnp.zeros_like(peak)
    for l in range(LEVELS):
        exponent = jnp.exp(masked[l] - peak)
        w_s[:, l * TOK : (l + 1) * TOK] = exponent
        total = total + exponent
    inverse = 1.0 / total
    inner = jnp.zeros_like(peak)
    for l in range(LEVELS):
        lanes = slice(l * TOK, (l + 1) * TOK)
        inner = inner + w_s[:, lanes] * inverse * ga_s[:, lanes]
    for l in range(LEVELS):
        lanes = slice(l * TOK, (l + 1) * TOK)
        attention = w_s[:, lanes] * inverse
        weight = attention.astype(BF16).astype(F32)
        w_s[:, lanes] = weight
        grad_attn = ga_s[:, lanes]
        grad_score = attention * (grad_attn - inner)
        slope = jnp.sum(grad_score * sc_s[:, lanes] + weight * grad_attn, axis=0, keepdims=True)
        scale = slope * inv_s[:, lanes] * (1.0 / D)
        xs_s[:AUG, lanes] = (paug_s[:AUG, lanes].astype(F32) * scale).astype(BF16)
        grad_score = grad_score * SCORE_SCALE
        high = grad_score.astype(BF16)
        gs_s[32:80, lanes] = (grad_score - high.astype(F32)).astype(BF16)
        gs_s[80:, lanes] = high
    tail = slice(LEVELS * TOK, SPAN)
    w_s[:, tail] = jnp.zeros((AH, TOK), F32)
    gs_s[32:, tail] = jnp.zeros((2 * AH, TOK), BF16)
    xs_s[:AUG, tail] = jnp.zeros((AUG, TOK), BF16)
    xs_s[AUG:, :] = jnp.zeros((TOK - AUG, SPAN), BF16)

    for p in range(PAIRS):
        at = slice(p * WIDE, (p + 1) * WIDE)
        gkv_s[:D, at] = jnp.dot(
            wide_ref[:, QBD : QBD + GS], gs_s[:, at], preferred_element_type=F32
        ).astype(BF16)
        grad_values = None
        for a in range(LATENT):
            weight = w_s[a * HEADS : (a + 1) * HEADS, at].reshape(HEADS, 1, WIDE)
            term = weight * g2[a].reshape(HEADS, HEAD, WIDE)
            grad_values = term if grad_values is None else grad_values + term
        gkv_s[D:, at] = grad_values.reshape(D, WIDE).astype(BF16)

    outer = lax.dot_general(gkv_s[...], pin_s[...], NT, preferred_element_type=F32)
    high = outer.astype(BF16)
    low = (outer - high.astype(F32)).astype(BF16)
    twice = jnp.concatenate([high, high], axis=1)
    mine = wide_ref[pl.ds(pl.multiple_of(core * HALF, HALF), HALF), WAUG : WAUG + DEEP]
    other = wide_ref[pl.ds(pl.multiple_of((1 - core) * HALF, HALF), HALF), WAUG : WAUG + DEEP]
    send_out[:, : 2 * D] = lax.dot_general(other, twice, NT, preferred_element_type=F32).astype(BF16)
    keep_out[:, : 2 * D] = lax.dot_general(mine, twice, NT, preferred_element_type=F32)
    grads = jnp.dot(kvw_ref[...], jnp.concatenate([high, low], axis=1), preferred_element_type=F32)
    grads = grads[:, :TOK] + grads[:, TOK:]
    gram = lax.dot_general(xs_s[...], pin_s[...], NT, preferred_element_type=F32).astype(BF16)
    grads = grads - jnp.dot(
        wide_ref[:, PLAIN : PLAIN + DEEP], jnp.concatenate([gram, gram], axis=0), preferred_element_type=F32
    )
    grads = grads - jnp.mean(grads, axis=0, keepdims=True)
    queries = lax.dot_general(kv_s[:D, :], gs_s[...], NT, preferred_element_type=F32)
    head = lax.broadcasted_iota(jnp.int32, (D, GS), 0) >> 5
    lane = lax.broadcasted_iota(jnp.int32, (D, GS), 1)
    queries = jnp.where((lane & 15) == head, queries, 0.0).reshape(HEADS, HEAD, GS)
    queries = jnp.sum(queries, axis=0)
    queries = queries + pltpu.roll(queries, AH, 1)
    queries = jnp.concatenate([queries] * HEADS, axis=0)
    eq_s[...] = jnp.where(lane < FEAT, grads, queries)
    for z in range(ZED):
        rows = slice(z * HEAD, (z + 1) * HEAD)
        start = z * 2 * HEAD
        keep_out[rows, 2 * D :] = eq_s[pl.ds(pl.multiple_of(start + core * HEAD, HEAD), HEAD), :]
        send_out[rows, 2 * D :] = eq_s[pl.ds(pl.multiple_of(start + (1 - core) * HEAD, HEAD), HEAD), :].astype(BF16)


def pair_kernel(keep_ref, recv_ref, sum_ref):
    sum_ref[...] = (keep_ref[...] + recv_ref[...].astype(F32)).astype(BF16)


def sum_z_kernel(part_ref, share_ref, total, tile):
    acc = part_ref[0].astype(F32)
    for source in range(1, ZED):
        acc = acc + part_ref[source].astype(F32)
    total[...] = acc
    block = acc[:, 2 * D :].astype(BF16)
    for target in range(RING):
        for c in range(8):
            tile[target, 2 * c : 2 * c + 2, :] = total[2 * target : 2 * target + 2, c * TOK : (c + 1) * TOK]
        share_ref[target, 0:16, :] = tile[target].astype(BF16)
        share_ref[target, 16:48, :] = block


def sum_lon_kernel(share_ref, kv_out, embed_out, query_out, tile, turned):
    acc = share_ref[0].astype(F32)
    for source in range(1, RING):
        acc = acc + share_ref[source].astype(F32)
    tile[...] = acc[:16]
    for c in range(8):
        kv_out[:, c * TOK : (c + 1) * TOK] = tile[2 * c : 2 * c + 2, :]
    embed_out[...] = acc[16:, :FEAT]
    turned[...] = acc[16:, :].T
    for a in range(LATENT):
        for h in range(HEADS):
            at = FEAT + a * HEADS + h
            query_out[a : a + 1, h * HEAD : (h + 1) * HEAD] = turned[at : at + 1, :]


def call(kernel, outs, in_specs, scratch, mib, name):
    return pl.pallas_call(
        kernel,
        out_shape=outs,
        in_specs=in_specs,
        out_specs=jax.tree.map(lambda _: VMEM, outs),
        scratch_shapes=scratch,
        compiler_params=params(mib),
        name=name,
    )


def on_device(level_patches, level_embed, embed_weight, kv_weight, query, band_levels, grad_out):
    lon = lax.axis_index("lon").astype(jnp.int32)
    core = lax.axis_index("lat").astype(jnp.int32) & 1
    slots = pl.pallas_call(
        slot_kernel,
        out_shape=shape(RING, FEAT, TOK),
        in_specs=[SMEM, HBM],
        out_specs=HBM,
        scratch_shapes=[pltpu.SemaphoreType.DMA((LEVELS,))],
        compiler_params=params(8),
        name="slots",
    )(lon.reshape(1), level_patches[0].T)
    tall, wide = call(
        prep_kernel,
        (shape(2 * D + 64, D), shape(D, 2 * D)),
        [VMEM] * 5,
        [pltpu.VMEM((AUG, D), F32), pltpu.VMEM((DEEP, D), F32)],
        24,
        "prep",
    )(kv_weight, embed_weight, level_embed, query, grad_out[0].transpose(1, 0, 2))
    recv = lax.all_to_all(slots, "lon", 0, 0, tiled=True)
    keep, send = call(
        main_kernel,
        (shape(HALF, ROW, dtype=F32), shape(HALF, ROW)),
        [SMEM, SMEM] + [VMEM] * 4,
        [
            pltpu.VMEM((LATENT, D, WIDE), F32),
            pltpu.VMEM((DEEP, SPAN), BF16),
            pltpu.VMEM((D, SPAN), BF16),
            pltpu.VMEM((2 * D, SPAN), BF16),
            pltpu.VMEM((2 * D, SPAN), BF16),
            pltpu.VMEM((TOK, SPAN), BF16),
            pltpu.VMEM((1, SPAN), F32),
            pltpu.VMEM((AH, SPAN), F32),
            pltpu.VMEM((AH, SPAN), F32),
            pltpu.VMEM((AH, SPAN), F32),
            pltpu.VMEM((GS, SPAN), BF16),
            pltpu.VMEM((TOK, SPAN), BF16),
            pltpu.VMEM((D, TOK), F32),
        ],
        24,
        "main",
    )(jnp.stack([lon, core]), band_levels, recv, kv_weight, tall, wide)
    lats = lax.axis_size("lat")
    other = lax.ppermute(send, "lat", [(i, i ^ 1) for i in range(lats)])
    paired = call(pair_kernel, shape(HALF, ROW), [VMEM] * 2, [], 8, "pair")(keep, other)
    parts = lax.all_to_all(
        paired.reshape(ZED, HALF // ZED, ROW),
        "lat",
        0,
        0,
        tiled=True,
        axis_index_groups=[[2 * z + c for z in range(ZED)] for c in range(2)],
    )
    share = call(
        sum_z_kernel,
        shape(RING, SHARE, TOK),
        [VMEM],
        [pltpu.VMEM((HALF // ZED, ROW), F32), pltpu.VMEM((RING, 16, TOK), F32)],
        8,
        "sum_z",
    )(parts)
    shared = lax.all_to_all(share, "lon", 0, 0, tiled=True)
    kv_grad, embed_grad, query_grad = call(
        sum_lon_kernel,
        (shape(2, 2 * D, dtype=F32), shape(32, FEAT, dtype=F32), shape(LATENT, D, dtype=F32)),
        [VMEM],
        [pltpu.VMEM((16, TOK), F32), pltpu.VMEM((TOK, 32), F32)],
        8,
        "sum_lon",
    )(shared)
    return (kv_grad, embed_grad.T, query_grad)


def solution(mesh):
    placed = (P("lat", "lon", None), P(), P(), P(), P(), P("lat"), P("lat", "lon", None, None))
    return jax.shard_map(
        on_device,
        mesh=mesh,
        in_specs=placed,
        out_specs=(P(("lon", "lat"), None), P(None, "lat"), P()),
        check_vma=False,
    )
```

```python
import functools

import jax
import jax.numpy as jnp
from jax import lax
from jax.experimental import pallas as pl
from jax.experimental.pallas import tpu as pltpu
from jax.sharding import PartitionSpec as P

HEADS = 16
SCORE_SCALE = 0.125
EPSILON = 1e-05
MASKED = -1e30
BF16 = jnp.bfloat16
F32 = jnp.float32

LEVELS = 13
TOK = 128
SPAN = LEVELS * TOK
D = 512
HEAD = D // HEADS
FEAT = 80
AUG = 96
LATENT = 3
AH = LATENT * HEADS
GS = 128
LEFT = 2 * D + 2 * GS
OWN = D // 2 + 32
NT = (((1,), (1,)), ((), ()))
RING = 16
ZED = 8
HALF = D // 2
WAUG = 0
QBD = 256
GRAD = 384
QUERY = 768
DEEP = 256
ROW = 2 * D + TOK
SHARE = 48

VMEM = pl.BlockSpec(memory_space=pltpu.VMEM)
SMEM = pl.BlockSpec(memory_space=pltpu.SMEM)
HBM = pl.BlockSpec(memory_space=pltpu.HBM)


def params(mib):
    return pltpu.CompilerParams(vmem_limit_bytes=mib * 1024 * 1024)


def shape(*dims, dtype=BF16):
    return jax.ShapeDtypeStruct(dims, dtype)


def slot_kernel(lon_ref, patch_ref, slot_ref, sems):
    lon = lon_ref[0]
    copies = [
        pltpu.make_async_copy(
            patch_ref.at[:, pl.ds(i * TOK, TOK)], slot_ref.at[lax.rem(lon * LEVELS + i, RING)], sems.at[i]
        )
        for i in range(LEVELS)
    ]
    for copy in copies:
        copy.start()
    for copy in copies:
        copy.wait()


def prep_kernel(
    core_ref, kvw_ref, embed_w_ref, level_ref, query_ref, grad_ref, tall_ref, wide_ref, own_ref, rows, spread, plain
):
    position = lax.broadcasted_iota(jnp.int32, (D, D), 0)
    feature = lax.broadcasted_iota(jnp.int32, (D, D), 1)
    core, z, lon, pair = position >> 8, (position >> 5) & 7, (position >> 1) & 15, position & 1
    reorder = jnp.where(lon * 32 + z * 4 + core * 2 + pair == feature, 1.0, 0.0).astype(BF16)
    for c in range(4):
        part = jnp.dot(reorder, kvw_ref[:, c * 256 : (c + 1) * 256], preferred_element_type=F32)
        tall_ref[c * 256 : (c + 1) * 256, :] = part.T.astype(BF16)
    rows[...] = jnp.zeros_like(rows)
    rows[:FEAT, :] = embed_w_ref[...].astype(F32)
    rows[FEAT : FEAT + LEVELS, :] = level_ref[...].astype(F32)
    weights = rows[...]
    weights = weights - jnp.mean(weights, axis=1, keepdims=True)
    high = weights.astype(BF16)
    spread[...] = jnp.zeros_like(spread)
    spread[:AUG, :] = high.astype(F32)
    spread[TOK : TOK + AUG, :] = weights - high.astype(F32)
    plain[...] = spread[...].T.astype(BF16)
    wide_ref[:, WAUG : WAUG + 256] = jnp.dot(reorder, plain[...], preferred_element_type=F32).astype(BF16)
    product = jnp.dot(tall_ref[:D, :], wide_ref[:, WAUG : WAUG + 256], preferred_element_type=F32)
    product = product[:, :TOK] + product[:, TOK:]
    high = product.astype(BF16)
    wide_ref[:, QUERY : QUERY + TOK] = high
    wide_ref[:, QUERY + TOK : QUERY + 256] = (product - high.astype(F32)).astype(BF16)
    side = core_ref[0] * HEAD
    for z in range(ZED):
        rows_here = slice(z * HEAD, (z + 1) * HEAD)
        start = pl.multiple_of(z * 2 * HEAD + side, HEAD)
        own_ref[rows_here, : 2 * D] = kvw_ref[pl.ds(start, HEAD), :]
        own_ref[rows_here, 2 * D :] = plain[pl.ds(start, HEAD), :]
    mean = jnp.mean(kvw_ref[...].astype(F32), axis=0, keepdims=True)
    high = mean.astype(BF16).astype(F32)
    row = lax.broadcasted_iota(jnp.int32, (OWN - HALF, 2 * D), 0)
    own_ref[HALF:, : 2 * D] = jnp.where(row == 0, high, jnp.where(row == 1, mean - high, 0.0)).astype(BF16)
    own_ref[HALF:, 2 * D :] = jnp.zeros((OWN - HALF, DEEP), BF16)
    head = lax.broadcasted_iota(jnp.int32, (HEADS, D), 0)
    owner = lax.broadcasted_iota(jnp.int32, (HEADS, D), 1) >> 5
    spread[:32, :] = jnp.zeros((32, D), F32)
    for a in range(LATENT):
        block = jnp.where(head == owner, query_ref[a : a + 1, :].astype(F32), 0.0)
        spread[32 + a * HEADS : 32 + (a + 1) * HEADS, :] = block
        spread[80 + a * HEADS : 80 + (a + 1) * HEADS, :] = block
    tall_ref[2 * D : 2 * D + AH, :] = spread[80:128, :].astype(BF16)
    tall_ref[2 * D + AH :, :] = jnp.zeros((16, D), BF16)
    wide_ref[:, QBD : QBD + GS] = spread[:GS, :].T.astype(BF16)
    for a in range(LATENT):
        at = GRAD + a * TOK
        wide_ref[:, at : at + TOK] = grad_ref[a].astype(F32).T.astype(BF16)


def main_kernel(
    lon_ref, count_ref, recv_ref, tall_ref, wide_ref,
    keep_out, send_out,
    g_s, paug_s, hid_s, kv_s, left_s, pin_s, inv_s, sc_s, ga_s, w_s,
):
    lon = lon_ref[0]
    count = count_ref[0]
    for a in range(LATENT):
        g_s[a] = wide_ref[:, GRAD + a * TOK : GRAD + (a + 1) * TOK].astype(F32)
    left_s[2 * D : 2 * D + 32, :] = jnp.zeros((32, SPAN), BF16)
    left_s[2 * D + GS + AUG :, :] = jnp.zeros((TOK - AUG, SPAN), BF16)
    pin_s[AUG:, :] = jnp.zeros((TOK - AUG, SPAN), BF16)
    for start in (AUG, TOK + AUG):
        paug_s[start : start + TOK - AUG, :] = jnp.zeros((TOK - AUG, SPAN), BF16)

    def lanes_of(group):
        return slice(group[0] * TOK, (group[-1] + 1) * TOK)

    def embed(group):
        at = lanes_of(group)
        row = lax.broadcasted_iota(jnp.int32, (AUG - FEAT, TOK), 0)
        for l in group:
            lanes = slice(l * TOK, (l + 1) * TOK)
            patches = recv_ref[(RING * l + lon) // LEVELS]
            one_hot = jnp.where(row == l, 1.0, 0.0).astype(BF16)
            for start in (0, TOK):
                paug_s[start : start + FEAT, lanes] = patches
                paug_s[start + FEAT : start + AUG, lanes] = one_hot
        center = jnp.dot(wide_ref[:, WAUG : WAUG + DEEP], paug_s[:, at], preferred_element_type=F32)
        inv_std = lax.rsqrt(jnp.mean(center * center, axis=0, keepdims=True) + EPSILON)
        inv_s[:, at] = inv_std
        hid_s[:, at] = (center * inv_std).astype(BF16)
        pin_s[:AUG, at] = (paug_s[:AUG, at].astype(F32) * inv_std).astype(BF16)

    def keys(group):
        at = lanes_of(group)
        kv_s[:, at] = jnp.dot(tall_ref[: 2 * D, :], hid_s[:, at], preferred_element_type=F32).astype(BF16)

    def score(group):
        at = lanes_of(group)
        sc_s[:, at] = (
            jnp.dot(tall_ref[2 * D : 2 * D + AH, :], kv_s[:D, at], preferred_element_type=F32) * SCORE_SCALE
        )
        for h in range(HEADS):
            rows = slice(h * HEAD, (h + 1) * HEAD)
            grads = [g_s[a, rows, :] for a in range(LATENT)]
            for l in group:
                lanes = slice(l * TOK, (l + 1) * TOK)
                values = kv_s[D + h * HEAD : D + (h + 1) * HEAD, lanes].astype(F32)
                for a in range(LATENT):
                    product = (grads[a] * values).reshape(4, 8, TOK)
                    ah = a * HEADS + h
                    ga_s[ah : ah + 1, lanes] = jnp.sum(jnp.sum(product, axis=0), axis=0, keepdims=True)

    every = tuple(range(LEVELS))
    embed(every)
    keys(every)
    score(every)

    masked = [jnp.where(l < count, sc_s[:, l * TOK : (l + 1) * TOK], MASKED) for l in range(LEVELS)]
    peak = functools.reduce(jnp.maximum, masked)
    total = jnp.zeros_like(peak)
    for l in range(LEVELS):
        exponent = jnp.exp(masked[l] - peak)
        w_s[:, l * TOK : (l + 1) * TOK] = exponent
        total = total + exponent
    inverse = 1.0 / total
    inner = jnp.zeros_like(peak)
    for l in range(LEVELS):
        lanes = slice(l * TOK, (l + 1) * TOK)
        inner = inner + w_s[:, lanes] * inverse * ga_s[:, lanes]
    for l in range(LEVELS):
        lanes = slice(l * TOK, (l + 1) * TOK)
        attention = w_s[:, lanes] * inverse
        weight = attention.astype(BF16).astype(F32)
        w_s[:, lanes] = weight
        grad_attn = ga_s[:, lanes]
        grad_score = attention * (grad_attn - inner)
        slope = jnp.sum(grad_score * sc_s[:, lanes] + weight * grad_attn, axis=0, keepdims=True)
        scale = slope * inv_s[:, lanes] * (1.0 / D)
        left_s[2 * D + GS : 2 * D + GS + AUG, lanes] = (paug_s[:AUG, lanes].astype(F32) * scale).astype(BF16)
        grad_score = grad_score * SCORE_SCALE
        high = grad_score.astype(BF16)
        left_s[2 * D + 32 : 2 * D + 80, lanes] = (grad_score - high.astype(F32)).astype(BF16)
        left_s[2 * D + 80 : 2 * D + GS, lanes] = high

    def grad_kv(group):
        at = lanes_of(group)
        left_s[:D, at] = jnp.dot(
            wide_ref[:, QBD : QBD + GS], left_s[2 * D : 2 * D + GS, at], preferred_element_type=F32
        ).astype(BF16)
        for h in range(HEADS):
            rows = slice(h * HEAD, (h + 1) * HEAD)
            grads = [g_s[a, rows, :] for a in range(LATENT)]
            for l in group:
                lanes = slice(l * TOK, (l + 1) * TOK)
                grad_values = None
                for a in range(LATENT):
                    term = w_s[a * HEADS + h : a * HEADS + h + 1, lanes] * grads[a]
                    grad_values = term if grad_values is None else grad_values + term
                left_s[D + h * HEAD : D + (h + 1) * HEAD, lanes] = grad_values.astype(BF16)

    grad_kv(every)

    outer = lax.dot_general(left_s[...], pin_s[...], NT, preferred_element_type=F32)
    keep_out[...] = outer
    send_out[...] = outer.astype(BF16)


def post_kernel(core_ref, keep_ref, recv_ref, wide_ref, own_ref, part_ref):
    total = keep_ref[...] + recv_ref[...].astype(F32)
    outer = total[: 2 * D]
    high = outer.astype(BF16)
    low = (outer - high.astype(F32)).astype(BF16)
    start = pl.multiple_of(core_ref[0] * HALF, HALF)
    part_ref[:, : 2 * D] = lax.dot_general(
        wide_ref[pl.ds(start, HALF), WAUG : WAUG + DEEP],
        jnp.concatenate([high, high], axis=1),
        NT,
        preferred_element_type=F32,
    ).astype(BF16)
    grads = jnp.dot(own_ref[:, : 2 * D], jnp.concatenate([high, low], axis=1), preferred_element_type=F32)
    grads = grads[:, :TOK] + grads[:, TOK:]
    gram = total[2 * D + GS :].astype(BF16)
    grads = (
        grads[:HALF]
        - (grads[HALF : HALF + 1] + grads[HALF + 1 : HALF + 2])
        - jnp.dot(own_ref[:HALF, 2 * D :], jnp.concatenate([gram, gram], axis=0), preferred_element_type=F32)
    )
    scores = total[2 * D : 2 * D + GS]
    scores = jnp.concatenate([jnp.zeros((FEAT, TOK), F32), scores[80:] + scores[32:80]], axis=0).astype(BF16)
    queries = lax.dot_general(
        wide_ref[:, QUERY : QUERY + DEEP],
        jnp.concatenate([scores, scores], axis=1),
        NT,
        preferred_element_type=F32,
    )
    head = lax.broadcasted_iota(jnp.int32, (D, GS), 0) >> 5
    lane = lax.broadcasted_iota(jnp.int32, (D, GS), 1)
    queries = jnp.where((lane & 15) == head, queries, 0.0).reshape(HEADS, HEAD, GS)
    queries = jnp.concatenate([jnp.sum(queries, axis=0)] * ZED, axis=0)
    part_ref[:, 2 * D :] = jnp.where(lane[:HALF] < FEAT, grads, queries).astype(BF16)


def sum_z_kernel(part_ref, share_ref, total, tile):
    acc = part_ref[0].astype(F32)
    for source in range(1, ZED):
        acc = acc + part_ref[source].astype(F32)
    total[...] = acc
    block = acc[:, 2 * D :].astype(BF16)
    for target in range(RING):
        for c in range(8):
            tile[target, 2 * c : 2 * c + 2, :] = total[2 * target : 2 * target + 2, c * TOK : (c + 1) * TOK]
        share_ref[target, 0:16, :] = tile[target].astype(BF16)
        share_ref[target, 16:48, :] = block


def sum_lon_kernel(share_ref, kv_out, embed_out, query_out, tile, turned):
    acc = share_ref[0].astype(F32)
    for source in range(1, RING):
        acc = acc + share_ref[source].astype(F32)
    tile[...] = acc[:16]
    for c in range(8):
        kv_out[:, c * TOK : (c + 1) * TOK] = tile[2 * c : 2 * c + 2, :]
    embed_out[...] = acc[16:, :FEAT]
    turned[...] = acc[16:, :].T
    for a in range(LATENT):
        for h in range(HEADS):
            at = FEAT + a * HEADS + h
            query_out[a : a + 1, h * HEAD : (h + 1) * HEAD] = turned[at : at + 1, :]


def call(kernel, outs, in_specs, scratch, mib, name):
    return pl.pallas_call(
        kernel,
        out_shape=outs,
        in_specs=in_specs,
        out_specs=jax.tree.map(lambda _: VMEM, outs),
        scratch_shapes=scratch,
        compiler_params=params(mib),
        name=name,
    )


def on_device(level_patches, level_embed, embed_weight, kv_weight, query, band_levels, grad_out):
    lon = lax.axis_index("lon").astype(jnp.int32).reshape(1)
    core = (lax.axis_index("lat").astype(jnp.int32) & 1).reshape(1)
    slots = pl.pallas_call(
        slot_kernel,
        out_shape=shape(RING, FEAT, TOK),
        in_specs=[SMEM, HBM],
        out_specs=HBM,
        scratch_shapes=[pltpu.SemaphoreType.DMA((LEVELS,))],
        compiler_params=params(8),
        name="slots",
    )(lon, level_patches[0].T)
    tall, wide, own = call(
        prep_kernel,
        (shape(2 * D + 64, D), shape(D, 2 * D), shape(OWN, 2 * D + DEEP)),
        [SMEM] + [VMEM] * 5,
        [pltpu.VMEM((AUG, D), F32), pltpu.VMEM((DEEP, D), F32), pltpu.VMEM((D, DEEP), BF16)],
        24,
        "prep",
    )(core, kv_weight, embed_weight, level_embed, query, grad_out[0].transpose(1, 0, 2))
    recv = lax.all_to_all(slots, "lon", 0, 0, tiled=True)
    keep, send = call(
        main_kernel,
        (shape(LEFT, TOK, dtype=F32), shape(LEFT, TOK)),
        [SMEM, SMEM] + [VMEM] * 3,
        [
            pltpu.VMEM((LATENT, D, TOK), F32),
            pltpu.VMEM((DEEP, SPAN), BF16),
            pltpu.VMEM((D, SPAN), BF16),
            pltpu.VMEM((2 * D, SPAN), BF16),
            pltpu.VMEM((LEFT, SPAN), BF16),
            pltpu.VMEM((TOK, SPAN), BF16),
            pltpu.VMEM((1, SPAN), F32),
            pltpu.VMEM((AH, SPAN), F32),
            pltpu.VMEM((AH, SPAN), F32),
            pltpu.VMEM((AH, SPAN), F32),
        ],
        28,
        "main",
    )(lon, band_levels, recv, tall, wide)
    lats = lax.axis_size("lat")
    other = lax.ppermute(send, "lat", [(i, i ^ 1) for i in range(lats)])
    part = call(post_kernel, shape(HALF, ROW), [SMEM] + [VMEM] * 4, [], 16, "post")(core, keep, other, wide, own)
    parts = lax.all_to_all(
        part.reshape(ZED, HALF // ZED, ROW),
        "lat",
        0,
        0,
        tiled=True,
        axis_index_groups=[[2 * z + c for z in range(ZED)] for c in range(2)],
    )
    share = call(
        sum_z_kernel,
        shape(RING, SHARE, TOK),
        [VMEM],
        [pltpu.VMEM((HALF // ZED, ROW), F32), pltpu.VMEM((RING, 16, TOK), F32)],
        8,
        "sum_z",
    )(parts)
    shared = lax.all_to_all(share, "lon", 0, 0, tiled=True)
    kv_grad, embed_grad, query_grad = call(
        sum_lon_kernel,
        (shape(2, 2 * D, dtype=F32), shape(32, FEAT, dtype=F32), shape(LATENT, D, dtype=F32)),
        [VMEM],
        [pltpu.VMEM((16, TOK), F32), pltpu.VMEM((TOK, 32), F32)],
        8,
        "sum_lon",
    )(shared)
    return (kv_grad, embed_grad.T, query_grad)


def solution(mesh):
    placed = (P("lat", "lon", None), P(), P(), P(), P(), P("lat"), P("lat", "lon", None, None))
    return jax.shard_map(
        on_device,
        mesh=mesh,
        in_specs=placed,
        out_specs=(P(("lon", "lat"), None), P(None, "lat"), P()),
        check_vma=False,
    )
```

```python
import functools

import jax
import jax.numpy as jnp
from jax import lax
from jax.experimental import pallas as pl
from jax.experimental.pallas import tpu as pltpu
from jax.sharding import PartitionSpec as P

HEADS = 16
SCORE_SCALE = 0.125
EPSILON = 1e-05
MASKED = -1e30
BF16 = jnp.bfloat16
F32 = jnp.float32

LEVELS = 13
TOK = 128
SPAN = LEVELS * TOK
D = 512
HEAD = D // HEADS
FEAT = 80
AUG = 96
LATENT = 3
AH = LATENT * HEADS
GS = 128
LEFT = 2 * D + 2 * GS
OWN = D // 2 + 32
NT = (((1,), (1,)), ((), ()))
RING = 16
ZED = 8
HALF = D // 2
WAUG = 0
QBD = 256
GRAD = 384
QUERY = 768
DEEP = 256
ROW = 2 * D + TOK
SHARE = 48

VMEM = pl.BlockSpec(memory_space=pltpu.VMEM)
SMEM = pl.BlockSpec(memory_space=pltpu.SMEM)
HBM = pl.BlockSpec(memory_space=pltpu.HBM)


def params(mib):
    return pltpu.CompilerParams(vmem_limit_bytes=mib * 1024 * 1024)


def shape(*dims, dtype=BF16):
    return jax.ShapeDtypeStruct(dims, dtype)


def slot_kernel(lon_ref, patch_ref, slot_ref, sems):
    lon = lon_ref[0]
    copies = [
        pltpu.make_async_copy(
            patch_ref.at[:, pl.ds(i * TOK, TOK)], slot_ref.at[lax.rem(lon * LEVELS + i, RING)], sems.at[i]
        )
        for i in range(LEVELS)
    ]
    for copy in copies:
        copy.start()
    for copy in copies:
        copy.wait()


def prep_kernel(
    core_ref, kvw_ref, embed_w_ref, level_ref, query_ref, grad_ref, tall_ref, wide_ref, own_ref, rows, spread, plain
):
    position = lax.broadcasted_iota(jnp.int32, (D, D), 0)
    feature = lax.broadcasted_iota(jnp.int32, (D, D), 1)
    core, z, lon, pair = position >> 8, (position >> 5) & 7, (position >> 1) & 15, position & 1
    reorder = jnp.where(lon * 32 + z * 4 + core * 2 + pair == feature, 1.0, 0.0).astype(BF16)
    for c in range(4):
        part = jnp.dot(reorder, kvw_ref[:, c * 256 : (c + 1) * 256], preferred_element_type=F32)
        tall_ref[c * 256 : (c + 1) * 256, :] = part.T.astype(BF16)
    rows[...] = jnp.zeros_like(rows)
    rows[:FEAT, :] = embed_w_ref[...].astype(F32)
    rows[FEAT : FEAT + LEVELS, :] = level_ref[...].astype(F32)
    weights = rows[...]
    weights = weights - jnp.mean(weights, axis=1, keepdims=True)
    high = weights.astype(BF16)
    spread[...] = jnp.zeros_like(spread)
    spread[:AUG, :] = high.astype(F32)
    spread[TOK : TOK + AUG, :] = weights - high.astype(F32)
    plain[...] = spread[...].T.astype(BF16)
    wide_ref[:, WAUG : WAUG + 256] = jnp.dot(reorder, plain[...], preferred_element_type=F32).astype(BF16)
    product = jnp.dot(tall_ref[:D, :], wide_ref[:, WAUG : WAUG + 256], preferred_element_type=F32)
    product = product[:, :TOK] + product[:, TOK:]
    high = product.astype(BF16)
    wide_ref[:, QUERY : QUERY + TOK] = high
    wide_ref[:, QUERY + TOK : QUERY + 256] = (product - high.astype(F32)).astype(BF16)
    side = core_ref[0] * HEAD
    for z in range(ZED):
        rows_here = slice(z * HEAD, (z + 1) * HEAD)
        start = pl.multiple_of(z * 2 * HEAD + side, HEAD)
        own_ref[rows_here, : 2 * D] = kvw_ref[pl.ds(start, HEAD), :]
        own_ref[rows_here, 2 * D :] = plain[pl.ds(start, HEAD), :]
    mean = jnp.mean(kvw_ref[...].astype(F32), axis=0, keepdims=True)
    high = mean.astype(BF16).astype(F32)
    row = lax.broadcasted_iota(jnp.int32, (OWN - HALF, 2 * D), 0)
    own_ref[HALF:, : 2 * D] = jnp.where(row == 0, high, jnp.where(row == 1, mean - high, 0.0)).astype(BF16)
    own_ref[HALF:, 2 * D :] = jnp.zeros((OWN - HALF, DEEP), BF16)
    head = lax.broadcasted_iota(jnp.int32, (HEADS, D), 0)
    owner = lax.broadcasted_iota(jnp.int32, (HEADS, D), 1) >> 5
    spread[:32, :] = jnp.zeros((32, D), F32)
    for a in range(LATENT):
        block = jnp.where(head == owner, query_ref[a : a + 1, :].astype(F32), 0.0)
        spread[32 + a * HEADS : 32 + (a + 1) * HEADS, :] = block
        spread[80 + a * HEADS : 80 + (a + 1) * HEADS, :] = block
    tall_ref[2 * D : 2 * D + AH, :] = spread[80:128, :].astype(BF16)
    tall_ref[2 * D + AH :, :] = jnp.zeros((16, D), BF16)
    wide_ref[:, QBD : QBD + GS] = spread[:GS, :].T.astype(BF16)
    for a in range(LATENT):
        at = GRAD + a * TOK
        wide_ref[:, at : at + TOK] = grad_ref[a].astype(F32).T.astype(BF16)


def main_kernel(
    lon_ref, count_ref, recv_ref, tall_ref, wide_ref,
    keep_out, send_out,
    g_s, paug_s, hid_s, kv_s, left_s, pin_s, inv_s, sc_s, ga_s, w_s,
):
    lon = lon_ref[0]
    count = count_ref[0]
    for a in range(LATENT):
        g_s[a] = wide_ref[:, GRAD + a * TOK : GRAD + (a + 1) * TOK].astype(F32)
    left_s[2 * D : 2 * D + 32, :] = jnp.zeros((32, SPAN), BF16)
    left_s[2 * D + GS + AUG :, :] = jnp.zeros((TOK - AUG, SPAN), BF16)
    pin_s[AUG:, :] = jnp.zeros((TOK - AUG, SPAN), BF16)
    for start in (AUG, TOK + AUG):
        paug_s[start : start + TOK - AUG, :] = jnp.zeros((TOK - AUG, SPAN), BF16)

    def lanes_of(group):
        return slice(group[0] * TOK, (group[-1] + 1) * TOK)

    def embed(group):
        at = lanes_of(group)
        row = lax.broadcasted_iota(jnp.int32, (AUG - FEAT, TOK), 0)
        for l in group:
            lanes = slice(l * TOK, (l + 1) * TOK)
            patches = recv_ref[(RING * l + lon) // LEVELS]
            one_hot = jnp.where(row == l, 1.0, 0.0).astype(BF16)
            for start in (0, TOK):
                paug_s[start : start + FEAT, lanes] = patches
                paug_s[start + FEAT : start + AUG, lanes] = one_hot
        center = jnp.dot(wide_ref[:, WAUG : WAUG + DEEP], paug_s[:, at], preferred_element_type=F32)
        inv_std = lax.rsqrt(jnp.mean(center * center, axis=0, keepdims=True) + EPSILON)
        inv_s[:, at] = inv_std
        hid_s[:, at] = (center * inv_std).astype(BF16)
        pin_s[:AUG, at] = (paug_s[:AUG, at].astype(F32) * inv_std).astype(BF16)

    def keys(group):
        at = lanes_of(group)
        kv_s[:, at] = jnp.dot(tall_ref[: 2 * D, :], hid_s[:, at], preferred_element_type=F32).astype(BF16)

    def score(group):
        at = lanes_of(group)
        sc_s[:, at] = (
            jnp.dot(tall_ref[2 * D : 2 * D + AH, :], kv_s[:D, at], preferred_element_type=F32) * SCORE_SCALE
        )
        for h in range(HEADS):
            rows = slice(h * HEAD, (h + 1) * HEAD)
            grads = [g_s[a, rows, :] for a in range(LATENT)]
            for l in group:
                lanes = slice(l * TOK, (l + 1) * TOK)
                values = kv_s[D + h * HEAD : D + (h + 1) * HEAD, lanes].astype(F32)
                for a in range(LATENT):
                    product = (grads[a] * values).reshape(4, 8, TOK)
                    ah = a * HEADS + h
                    ga_s[ah : ah + 1, lanes] = jnp.sum(jnp.sum(product, axis=0), axis=0, keepdims=True)

    every = tuple(range(LEVELS))
    embed(every)
    keys(every)
    score(every)

    masked = [jnp.where(l < count, sc_s[:, l * TOK : (l + 1) * TOK], MASKED) for l in range(LEVELS)]
    peak = functools.reduce(jnp.maximum, masked)
    total = jnp.zeros_like(peak)
    for l in range(LEVELS):
        exponent = jnp.exp(masked[l] - peak)
        w_s[:, l * TOK : (l + 1) * TOK] = exponent
        total = total + exponent
    inverse = 1.0 / total
    inner = jnp.zeros_like(peak)
    for l in range(LEVELS):
        lanes = slice(l * TOK, (l + 1) * TOK)
        inner = inner + w_s[:, lanes] * inverse * ga_s[:, lanes]
    for l in range(LEVELS):
        lanes = slice(l * TOK, (l + 1) * TOK)
        attention = w_s[:, lanes] * inverse
        weight = attention.astype(BF16).astype(F32)
        w_s[:, lanes] = weight
        grad_attn = ga_s[:, lanes]
        grad_score = attention * (grad_attn - inner)
        slope = jnp.sum(grad_score * sc_s[:, lanes] + weight * grad_attn, axis=0, keepdims=True)
        scale = slope * inv_s[:, lanes] * (1.0 / D)
        left_s[2 * D + GS : 2 * D + GS + AUG, lanes] = (paug_s[:AUG, lanes].astype(F32) * scale).astype(BF16)
        grad_score = grad_score * SCORE_SCALE
        high = grad_score.astype(BF16)
        left_s[2 * D + 32 : 2 * D + 80, lanes] = (grad_score - high.astype(F32)).astype(BF16)
        left_s[2 * D + 80 : 2 * D + GS, lanes] = high

    def grad_kv(group):
        at = lanes_of(group)
        left_s[:D, at] = jnp.dot(
            wide_ref[:, QBD : QBD + GS], left_s[2 * D : 2 * D + GS, at], preferred_element_type=F32
        ).astype(BF16)
        for h in range(HEADS):
            rows = slice(h * HEAD, (h + 1) * HEAD)
            grads = [g_s[a, rows, :] for a in range(LATENT)]
            for l in group:
                lanes = slice(l * TOK, (l + 1) * TOK)
                grad_values = None
                for a in range(LATENT):
                    term = w_s[a * HEADS + h : a * HEADS + h + 1, lanes] * grads[a]
                    grad_values = term if grad_values is None else grad_values + term
                left_s[D + h * HEAD : D + (h + 1) * HEAD, lanes] = grad_values.astype(BF16)

    grad_kv(every)

    outer = lax.dot_general(left_s[...], pin_s[...], NT, preferred_element_type=F32)
    keep_out[...] = outer
    send_out[...] = outer.astype(BF16)


def post_kernel(core_ref, keep_ref, recv_ref, wide_ref, own_ref, part_ref):
    total = keep_ref[...] + recv_ref[...].astype(F32)
    outer = total[: 2 * D]
    high = outer.astype(BF16)
    low = (outer - high.astype(F32)).astype(BF16)
    start = pl.multiple_of(core_ref[0] * HALF, HALF)
    part_ref[:, : 2 * D] = lax.dot_general(
        wide_ref[pl.ds(start, HALF), WAUG : WAUG + DEEP],
        jnp.concatenate([high, high], axis=1),
        NT,
        preferred_element_type=F32,
    ).astype(BF16)
    grads = jnp.dot(own_ref[:, : 2 * D], jnp.concatenate([high, low], axis=1), preferred_element_type=F32)
    grads = grads[:, :TOK] + grads[:, TOK:]
    gram = total[2 * D + GS :].astype(BF16)
    grads = (
        grads[:HALF]
        - (grads[HALF : HALF + 1] + grads[HALF + 1 : HALF + 2])
        - jnp.dot(own_ref[:HALF, 2 * D :], jnp.concatenate([gram, gram], axis=0), preferred_element_type=F32)
    )
    scores = total[2 * D : 2 * D + GS]
    scores = jnp.concatenate([jnp.zeros((FEAT, TOK), F32), scores[80:] + scores[32:80]], axis=0).astype(BF16)
    queries = lax.dot_general(
        wide_ref[:, QUERY : QUERY + DEEP],
        jnp.concatenate([scores, scores], axis=1),
        NT,
        preferred_element_type=F32,
    )
    head = lax.broadcasted_iota(jnp.int32, (D, GS), 0) >> 5
    lane = lax.broadcasted_iota(jnp.int32, (D, GS), 1)
    queries = jnp.where((lane & 15) == head, queries, 0.0).reshape(HEADS, HEAD, GS)
    queries = jnp.concatenate([jnp.sum(queries, axis=0)] * ZED, axis=0)
    part_ref[:, 2 * D :] = jnp.where(lane[:HALF] < FEAT, grads, queries).astype(BF16)


def sum_z_kernel(part_ref, share_ref, total, tile):
    acc = part_ref[0].astype(F32)
    for source in range(1, ZED):
        acc = acc + part_ref[source].astype(F32)
    total[...] = acc
    block = acc[:, 2 * D :].astype(BF16)
    for target in range(RING):
        for c in range(8):
            tile[target, 2 * c : 2 * c + 2, :] = total[2 * target : 2 * target + 2, c * TOK : (c + 1) * TOK]
        share_ref[target, 0:16, :] = tile[target].astype(BF16)
        share_ref[target, 16:48, :] = block


def sum_lon_kernel(share_ref, kv_out, embed_out, query_out, tile, turned):
    acc = share_ref[0].astype(F32)
    for source in range(1, RING):
        acc = acc + share_ref[source].astype(F32)
    tile[...] = acc[:16]
    for c in range(8):
        kv_out[:, c * TOK : (c + 1) * TOK] = tile[2 * c : 2 * c + 2, :]
    embed_out[...] = acc[16:, :FEAT]
    turned[...] = acc[16:, :].T
    for a in range(LATENT):
        for h in range(HEADS):
            at = FEAT + a * HEADS + h
            query_out[a : a + 1, h * HEAD : (h + 1) * HEAD] = turned[at : at + 1, :]


def call(kernel, outs, in_specs, scratch, mib, name):
    return pl.pallas_call(
        kernel,
        out_shape=outs,
        in_specs=in_specs,
        out_specs=jax.tree.map(lambda _: VMEM, outs),
        scratch_shapes=scratch,
        compiler_params=params(mib),
        name=name,
    )


def on_device(level_patches, level_embed, embed_weight, kv_weight, query, band_levels, grad_out):
    lon = lax.axis_index("lon").astype(jnp.int32).reshape(1)
    core = (lax.axis_index("lat").astype(jnp.int32) & 1).reshape(1)
    slots = pl.pallas_call(
        slot_kernel,
        out_shape=shape(RING, FEAT, TOK),
        in_specs=[SMEM, HBM],
        out_specs=HBM,
        scratch_shapes=[pltpu.SemaphoreType.DMA((LEVELS,))],
        compiler_params=params(60),
        name="slots",
    )(lon, level_patches[0].T)
    tall, wide, own = call(
        prep_kernel,
        (shape(2 * D + 64, D), shape(D, 2 * D), shape(OWN, 2 * D + DEEP)),
        [SMEM] + [VMEM] * 5,
        [pltpu.VMEM((AUG, D), F32), pltpu.VMEM((DEEP, D), F32), pltpu.VMEM((D, DEEP), BF16)],
        24,
        "prep",
    )(core, kv_weight, embed_weight, level_embed, query, grad_out[0].transpose(1, 0, 2))
    recv = lax.all_to_all(slots, "lon", 0, 0, tiled=True)
    keep, send = call(
        main_kernel,
        (shape(LEFT, TOK, dtype=F32), shape(LEFT, TOK)),
        [SMEM, SMEM] + [VMEM] * 3,
        [
            pltpu.VMEM((LATENT, D, TOK), F32),
            pltpu.VMEM((DEEP, SPAN), BF16),
            pltpu.VMEM((D, SPAN), BF16),
            pltpu.VMEM((2 * D, SPAN), BF16),
            pltpu.VMEM((LEFT, SPAN), BF16),
            pltpu.VMEM((TOK, SPAN), BF16),
            pltpu.VMEM((1, SPAN), F32),
            pltpu.VMEM((AH, SPAN), F32),
            pltpu.VMEM((AH, SPAN), F32),
            pltpu.VMEM((AH, SPAN), F32),
        ],
        28,
        "main",
    )(lon, band_levels, recv, tall, wide)
    lats = lax.axis_size("lat")
    other = lax.ppermute(send, "lat", [(i, i ^ 1) for i in range(lats)])
    part = call(post_kernel, shape(HALF, ROW), [SMEM] + [VMEM] * 4, [], 16, "post")(core, keep, other, wide, own)
    parts = lax.all_to_all(
        part.reshape(ZED, HALF // ZED, ROW),
        "lat",
        0,
        0,
        tiled=True,
        axis_index_groups=[[2 * z + c for z in range(ZED)] for c in range(2)],
    )
    share = call(
        sum_z_kernel,
        shape(RING, SHARE, TOK),
        [VMEM],
        [pltpu.VMEM((HALF // ZED, ROW), F32), pltpu.VMEM((RING, 16, TOK), F32)],
        8,
        "sum_z",
    )(parts)
    shared = lax.all_to_all(share, "lon", 0, 0, tiled=True)
    kv_grad, embed_grad, query_grad = call(
        sum_lon_kernel,
        (shape(2, 2 * D, dtype=F32), shape(32, FEAT, dtype=F32), shape(LATENT, D, dtype=F32)),
        [VMEM],
        [pltpu.VMEM((16, TOK), F32), pltpu.VMEM((TOK, 32), F32)],
        8,
        "sum_lon",
    )(shared)
    return (kv_grad, embed_grad.T, query_grad)


def solution(mesh):
    placed = (P("lat", "lon", None), P(), P(), P(), P(), P("lat"), P("lat", "lon", None, None))
    return jax.shard_map(
        on_device,
        mesh=mesh,
        in_specs=placed,
        out_specs=(P(("lon", "lat"), None), P(None, "lat"), P()),
        check_vma=False,
    )
```

```python
import functools

import jax
import jax.numpy as jnp
from jax import lax
from jax.experimental import pallas as pl
from jax.experimental.pallas import tpu as pltpu
from jax.sharding import PartitionSpec as P

HEADS = 16
SCORE_SCALE = 0.125
EPSILON = 1e-05
MASKED = -1e30
BF16 = jnp.bfloat16
F32 = jnp.float32

LEVELS = 13
TOK = 128
SPAN = LEVELS * TOK
D = 512
HEAD = D // HEADS
FEAT = 80
AUG = 96
LATENT = 3
AH = LATENT * HEADS
GS = 128
LEFT = 2 * D + 2 * GS
OWN = D // 2 + 32
NT = (((1,), (1,)), ((), ()))
RING = 16
ZED = 8
HALF = D // 2
WAUG = 0
QBD = 256
GRAD = 384
QUERY = 768
DEEP = 256
ROW = 2 * D + TOK
SHARE = 48

VMEM = pl.BlockSpec(memory_space=pltpu.VMEM)
SMEM = pl.BlockSpec(memory_space=pltpu.SMEM)
HBM = pl.BlockSpec(memory_space=pltpu.HBM)


def params(mib):
    return pltpu.CompilerParams(vmem_limit_bytes=mib * 1024 * 1024)


def shape(*dims, dtype=BF16):
    return jax.ShapeDtypeStruct(dims, dtype)


def slot_kernel(lon_ref, patch_ref, slot_ref, sems):
    lon = lon_ref[0]
    copies = [
        pltpu.make_async_copy(
            patch_ref.at[:, pl.ds(i * TOK, TOK)], slot_ref.at[lax.rem(lon * LEVELS + i, RING)], sems.at[i]
        )
        for i in range(LEVELS)
    ]
    for copy in copies:
        copy.start()
    for copy in copies:
        copy.wait()


def prep_kernel(
    core_ref, kvw_ref, embed_w_ref, level_ref, query_ref, grad_ref, tall_ref, wide_ref, own_ref, ready_ref,
    rows, spread, plain,
):
    position = lax.broadcasted_iota(jnp.int32, (D, D), 0)
    feature = lax.broadcasted_iota(jnp.int32, (D, D), 1)
    core, z, lon, pair = position >> 8, (position >> 5) & 7, (position >> 1) & 15, position & 1
    reorder = jnp.where(lon * 32 + z * 4 + core * 2 + pair == feature, 1.0, 0.0).astype(BF16)
    for c in range(4):
        part = jnp.dot(reorder, kvw_ref[:, c * 256 : (c + 1) * 256], preferred_element_type=F32)
        tall_ref[c * 256 : (c + 1) * 256, :] = part.T.astype(BF16)
    rows[...] = jnp.zeros_like(rows)
    rows[:FEAT, :] = embed_w_ref[...].astype(F32)
    rows[FEAT : FEAT + LEVELS, :] = level_ref[...].astype(F32)
    weights = rows[...]
    weights = weights - jnp.mean(weights, axis=1, keepdims=True)
    high = weights.astype(BF16)
    spread[...] = jnp.zeros_like(spread)
    spread[:AUG, :] = high.astype(F32)
    spread[TOK : TOK + AUG, :] = weights - high.astype(F32)
    plain[...] = spread[...].T.astype(BF16)
    wide_ref[:, WAUG : WAUG + 256] = jnp.dot(reorder, plain[...], preferred_element_type=F32).astype(BF16)
    product = jnp.dot(tall_ref[:D, :], wide_ref[:, WAUG : WAUG + 256], preferred_element_type=F32)
    product = product[:, :TOK] + product[:, TOK:]
    high = product.astype(BF16)
    wide_ref[:, QUERY : QUERY + TOK] = high
    wide_ref[:, QUERY + TOK : QUERY + 256] = (product - high.astype(F32)).astype(BF16)
    side = core_ref[0] * HEAD
    for z in range(ZED):
        rows_here = slice(z * HEAD, (z + 1) * HEAD)
        start = pl.multiple_of(z * 2 * HEAD + side, HEAD)
        own_ref[rows_here, : 2 * D] = kvw_ref[pl.ds(start, HEAD), :]
        own_ref[rows_here, 2 * D :] = plain[pl.ds(start, HEAD), :]
    mean = jnp.mean(kvw_ref[...].astype(F32), axis=0, keepdims=True)
    high = mean.astype(BF16).astype(F32)
    row = lax.broadcasted_iota(jnp.int32, (OWN - HALF, 2 * D), 0)
    own_ref[HALF:, : 2 * D] = jnp.where(row == 0, high, jnp.where(row == 1, mean - high, 0.0)).astype(BF16)
    own_ref[HALF:, 2 * D :] = jnp.zeros((OWN - HALF, DEEP), BF16)
    ready_ref[...] = rows[:16, :TOK]
    head = lax.broadcasted_iota(jnp.int32, (HEADS, D), 0)
    owner = lax.broadcasted_iota(jnp.int32, (HEADS, D), 1) >> 5
    spread[:32, :] = jnp.zeros((32, D), F32)
    for a in range(LATENT):
        block = jnp.where(head == owner, query_ref[a : a + 1, :].astype(F32), 0.0)
        spread[32 + a * HEADS : 32 + (a + 1) * HEADS, :] = block
        spread[80 + a * HEADS : 80 + (a + 1) * HEADS, :] = block
    tall_ref[2 * D : 2 * D + AH, :] = spread[80:128, :].astype(BF16)
    tall_ref[2 * D + AH :, :] = jnp.zeros((16, D), BF16)
    wide_ref[:, QBD : QBD + GS] = spread[:GS, :].T.astype(BF16)
    for a in range(LATENT):
        at = GRAD + a * TOK
        wide_ref[:, at : at + TOK] = grad_ref[a].astype(F32).T.astype(BF16)


def main_kernel(
    lon_ref, count_ref, recv_ref, tall_ref, wide_ref, ready_ref,
    keep_out, send_out,
    g_s, paug_s, hid_s, kv_s, left_s, pin_s, inv_s, sc_s, ga_s, w_s,
):
    lon = lon_ref[0]
    count = count_ref[0]
    for a in range(LATENT):
        g_s[a] = wide_ref[:, GRAD + a * TOK : GRAD + (a + 1) * TOK].astype(F32)
    left_s[2 * D : 2 * D + 32, :] = jnp.zeros((32, SPAN), BF16)
    left_s[2 * D + GS + AUG :, :] = jnp.zeros((TOK - AUG, SPAN), BF16)
    pin_s[AUG:, :] = jnp.zeros((TOK - AUG, SPAN), BF16)
    for start in (AUG, TOK + AUG):
        paug_s[start : start + TOK - AUG, :] = jnp.zeros((TOK - AUG, SPAN), BF16)

    def lanes_of(group):
        return slice(group[0] * TOK, (group[-1] + 1) * TOK)

    def embed(group):
        at = lanes_of(group)
        row = lax.broadcasted_iota(jnp.int32, (AUG - FEAT, TOK), 0)
        for l in group:
            lanes = slice(l * TOK, (l + 1) * TOK)
            patches = recv_ref[(RING * l + lon) // LEVELS]
            one_hot = jnp.where(row == l, 1.0, 0.0).astype(BF16)
            for start in (0, TOK):
                paug_s[start : start + FEAT, lanes] = patches
                paug_s[start + FEAT : start + AUG, lanes] = one_hot
        center = jnp.dot(wide_ref[:, WAUG : WAUG + DEEP], paug_s[:, at], preferred_element_type=F32)
        inv_std = lax.rsqrt(jnp.mean(center * center, axis=0, keepdims=True) + EPSILON)
        inv_s[:, at] = inv_std
        hid_s[:, at] = (center * inv_std).astype(BF16)
        pin_s[:AUG, at] = (paug_s[:AUG, at].astype(F32) * inv_std).astype(BF16)

    def keys(group):
        at = lanes_of(group)
        kv_s[:, at] = jnp.dot(tall_ref[: 2 * D, :], hid_s[:, at], preferred_element_type=F32).astype(BF16)

    def score(group):
        at = lanes_of(group)
        sc_s[:, at] = (
            jnp.dot(tall_ref[2 * D : 2 * D + AH, :], kv_s[:D, at], preferred_element_type=F32) * SCORE_SCALE
        )
        for h in range(HEADS):
            rows = slice(h * HEAD, (h + 1) * HEAD)
            grads = [g_s[a, rows, :] for a in range(LATENT)]
            for l in group:
                lanes = slice(l * TOK, (l + 1) * TOK)
                values = kv_s[D + h * HEAD : D + (h + 1) * HEAD, lanes].astype(F32)
                for a in range(LATENT):
                    product = (grads[a] * values).reshape(4, 8, TOK)
                    ah = a * HEADS + h
                    ga_s[ah : ah + 1, lanes] = jnp.sum(jnp.sum(product, axis=0), axis=0, keepdims=True)

    every = tuple(range(LEVELS))
    embed(every)
    keys(every)
    score(every)

    masked = [jnp.where(l < count, sc_s[:, l * TOK : (l + 1) * TOK], MASKED) for l in range(LEVELS)]
    peak = functools.reduce(jnp.maximum, masked)
    total = jnp.zeros_like(peak)
    for l in range(LEVELS):
        exponent = jnp.exp(masked[l] - peak)
        w_s[:, l * TOK : (l + 1) * TOK] = exponent
        total = total + exponent
    inverse = 1.0 / total
    inner = jnp.zeros_like(peak)
    for l in range(LEVELS):
        lanes = slice(l * TOK, (l + 1) * TOK)
        inner = inner + w_s[:, lanes] * inverse * ga_s[:, lanes]
    for l in range(LEVELS):
        lanes = slice(l * TOK, (l + 1) * TOK)
        attention = w_s[:, lanes] * inverse
        weight = attention.astype(BF16).astype(F32)
        w_s[:, lanes] = weight
        grad_attn = ga_s[:, lanes]
        grad_score = attention * (grad_attn - inner)
        slope = jnp.sum(grad_score * sc_s[:, lanes] + weight * grad_attn, axis=0, keepdims=True)
        scale = slope * inv_s[:, lanes] * (1.0 / D)
        left_s[2 * D + GS : 2 * D + GS + AUG, lanes] = (paug_s[:AUG, lanes].astype(F32) * scale).astype(BF16)
        grad_score = grad_score * SCORE_SCALE
        high = grad_score.astype(BF16)
        left_s[2 * D + 32 : 2 * D + 80, lanes] = (grad_score - high.astype(F32)).astype(BF16)
        left_s[2 * D + 80 : 2 * D + GS, lanes] = high

    def grad_kv(group):
        at = lanes_of(group)
        left_s[:D, at] = jnp.dot(
            wide_ref[:, QBD : QBD + GS], left_s[2 * D : 2 * D + GS, at], preferred_element_type=F32
        ).astype(BF16)
        for h in range(HEADS):
            rows = slice(h * HEAD, (h + 1) * HEAD)
            grads = [g_s[a, rows, :] for a in range(LATENT)]
            for l in group:
                lanes = slice(l * TOK, (l + 1) * TOK)
                grad_values = None
                for a in range(LATENT):
                    term = w_s[a * HEADS + h : a * HEADS + h + 1, lanes] * grads[a]
                    grad_values = term if grad_values is None else grad_values + term
                left_s[D + h * HEAD : D + (h + 1) * HEAD, lanes] = grad_values.astype(BF16)

    grad_kv(every)

    outer = lax.dot_general(left_s[...], pin_s[...], NT, preferred_element_type=F32)
    keep_out[...] = outer
    send_out[...] = outer.astype(BF16)


def post_kernel(core_ref, keep_ref, recv_ref, wide_ref, own_ref, part_ref):
    total = keep_ref[...] + recv_ref[...].astype(F32)
    outer = total[: 2 * D]
    high = outer.astype(BF16)
    low = (outer - high.astype(F32)).astype(BF16)
    start = pl.multiple_of(core_ref[0] * HALF, HALF)
    part_ref[:, : 2 * D] = lax.dot_general(
        wide_ref[pl.ds(start, HALF), WAUG : WAUG + DEEP],
        jnp.concatenate([high, high], axis=1),
        NT,
        preferred_element_type=F32,
    ).astype(BF16)
    grads = jnp.dot(own_ref[:, : 2 * D], jnp.concatenate([high, low], axis=1), preferred_element_type=F32)
    grads = grads[:, :TOK] + grads[:, TOK:]
    gram = total[2 * D + GS :].astype(BF16)
    grads = (
        grads[:HALF]
        - (grads[HALF : HALF + 1] + grads[HALF + 1 : HALF + 2])
        - jnp.dot(own_ref[:HALF, 2 * D :], jnp.concatenate([gram, gram], axis=0), preferred_element_type=F32)
    )
    scores = total[2 * D : 2 * D + GS]
    scores = jnp.concatenate([jnp.zeros((FEAT, TOK), F32), scores[80:] + scores[32:80]], axis=0).astype(BF16)
    queries = lax.dot_general(
        wide_ref[:, QUERY : QUERY + DEEP],
        jnp.concatenate([scores, scores], axis=1),
        NT,
        preferred_element_type=F32,
    )
    head = lax.broadcasted_iota(jnp.int32, (D, GS), 0) >> 5
    lane = lax.broadcasted_iota(jnp.int32, (D, GS), 1)
    queries = jnp.where((lane & 15) == head, queries, 0.0).reshape(HEADS, HEAD, GS)
    queries = jnp.concatenate([jnp.sum(queries, axis=0)] * ZED, axis=0)
    part_ref[:, 2 * D :] = jnp.where(lane[:HALF] < FEAT, grads, queries).astype(BF16)


def sum_z_kernel(part_ref, share_ref, total, tile):
    acc = part_ref[0].astype(F32)
    for source in range(1, ZED):
        acc = acc + part_ref[source].astype(F32)
    total[...] = acc
    block = acc[:, 2 * D :].astype(BF16)
    for target in range(RING):
        for c in range(8):
            tile[target, 2 * c : 2 * c + 2, :] = total[2 * target : 2 * target + 2, c * TOK : (c + 1) * TOK]
        share_ref[target, 0:16, :] = tile[target].astype(BF16)
        share_ref[target, 16:48, :] = block


def sum_lon_kernel(share_ref, kv_out, embed_out, query_out, tile, turned):
    acc = share_ref[0].astype(F32)
    for source in range(1, RING):
        acc = acc + share_ref[source].astype(F32)
    tile[...] = acc[:16]
    for c in range(8):
        kv_out[:, c * TOK : (c + 1) * TOK] = tile[2 * c : 2 * c + 2, :]
    embed_out[...] = acc[16:, :FEAT]
    turned[...] = acc[16:, :].T
    for a in range(LATENT):
        for h in range(HEADS):
            at = FEAT + a * HEADS + h
            query_out[a : a + 1, h * HEAD : (h + 1) * HEAD] = turned[at : at + 1, :]


def call(kernel, outs, in_specs, scratch, mib, name):
    return pl.pallas_call(
        kernel,
        out_shape=outs,
        in_specs=in_specs,
        out_specs=jax.tree.map(lambda _: VMEM, outs),
        scratch_shapes=scratch,
        compiler_params=params(mib),
        name=name,
    )


def on_device(level_patches, level_embed, embed_weight, kv_weight, query, band_levels, grad_out):
    lon = lax.axis_index("lon").astype(jnp.int32).reshape(1)
    core = (lax.axis_index("lat").astype(jnp.int32) & 1).reshape(1)
    slots = pl.pallas_call(
        slot_kernel,
        out_shape=shape(RING, FEAT, TOK),
        in_specs=[SMEM, HBM],
        out_specs=HBM,
        scratch_shapes=[pltpu.SemaphoreType.DMA((LEVELS,))],
        compiler_params=params(8),
        name="slots",
    )(lon, level_patches[0].T)
    tall, wide, own, ready = call(
        prep_kernel,
        (shape(2 * D + 64, D), shape(D, 2 * D), shape(OWN, 2 * D + DEEP), shape(16, TOK, dtype=F32)),
        [SMEM] + [VMEM] * 5,
        [pltpu.VMEM((AUG, D), F32), pltpu.VMEM((DEEP, D), F32), pltpu.VMEM((D, DEEP), BF16)],
        24,
        "prep",
    )(core, kv_weight, embed_weight, level_embed, query, grad_out[0].transpose(1, 0, 2))
    recv = lax.all_to_all(slots, "lon", 0, 0, tiled=True)
    lats = lax.axis_size("lat")
    ready = lax.ppermute(ready, "lat", [(i, (i + lats // 2) % lats) for i in range(lats)])
    keep, send = call(
        main_kernel,
        (shape(LEFT, TOK, dtype=F32), shape(LEFT, TOK)),
        [SMEM, SMEM] + [VMEM] * 4,
        [
            pltpu.VMEM((LATENT, D, TOK), F32),
            pltpu.VMEM((DEEP, SPAN), BF16),
            pltpu.VMEM((D, SPAN), BF16),
            pltpu.VMEM((2 * D, SPAN), BF16),
            pltpu.VMEM((LEFT, SPAN), BF16),
            pltpu.VMEM((TOK, SPAN), BF16),
            pltpu.VMEM((1, SPAN), F32),
            pltpu.VMEM((AH, SPAN), F32),
            pltpu.VMEM((AH, SPAN), F32),
            pltpu.VMEM((AH, SPAN), F32),
        ],
        28,
        "main",
    )(lon, band_levels, recv, tall, wide, ready)
    other = lax.ppermute(send, "lat", [(i, i ^ 1) for i in range(lats)])
    part = call(post_kernel, shape(HALF, ROW), [SMEM] + [VMEM] * 4, [], 16, "post")(core, keep, other, wide, own)
    parts = lax.all_to_all(
        part.reshape(ZED, HALF // ZED, ROW),
        "lat",
        0,
        0,
        tiled=True,
        axis_index_groups=[[2 * z + c for z in range(ZED)] for c in range(2)],
    )
    share = call(
        sum_z_kernel,
        shape(RING, SHARE, TOK),
        [VMEM],
        [pltpu.VMEM((HALF // ZED, ROW), F32), pltpu.VMEM((RING, 16, TOK), F32)],
        8,
        "sum_z",
    )(parts)
    shared = lax.all_to_all(share, "lon", 0, 0, tiled=True)
    kv_grad, embed_grad, query_grad = call(
        sum_lon_kernel,
        (shape(2, 2 * D, dtype=F32), shape(32, FEAT, dtype=F32), shape(LATENT, D, dtype=F32)),
        [VMEM],
        [pltpu.VMEM((16, TOK), F32), pltpu.VMEM((TOK, 32), F32)],
        8,
        "sum_lon",
    )(shared)
    return (kv_grad, embed_grad.T, query_grad)


def solution(mesh):
    placed = (P("lat", "lon", None), P(), P(), P(), P(), P("lat"), P("lat", "lon", None, None))
    return jax.shard_map(
        on_device,
        mesh=mesh,
        in_specs=placed,
        out_specs=(P(("lon", "lat"), None), P(None, "lat"), P()),
        check_vma=False,
    )
```

```python
import functools

import jax
import jax.numpy as jnp
from jax import lax
from jax.experimental import pallas as pl
from jax.experimental.pallas import tpu as pltpu
from jax.sharding import PartitionSpec as P

HEADS = 16
SCORE_SCALE = 0.125
EPSILON = 1e-05
MASKED = -1e30
BF16 = jnp.bfloat16
F32 = jnp.float32

LEVELS = 13
TOK = 128
SPAN = LEVELS * TOK
D = 512
HEAD = D // HEADS
FEAT = 80
AUG = 96
LATENT = 3
AH = LATENT * HEADS
GS = 128
LEFT = 2 * D + 2 * GS
OWN = D // 2 + 32
NT = (((1,), (1,)), ((), ()))
RING = 16
ZED = 8
HALF = D // 2
WAUG = 0
QBD = 256
GRAD = 384
QUERY = 768
RAW = 1024
DEEP = 256
ROW = 2 * D + TOK
SHARE = 48

VMEM = pl.BlockSpec(memory_space=pltpu.VMEM)
SMEM = pl.BlockSpec(memory_space=pltpu.SMEM)
HBM = pl.BlockSpec(memory_space=pltpu.HBM)


def params(mib):
    return pltpu.CompilerParams(vmem_limit_bytes=mib * 1024 * 1024)


def shape(*dims, dtype=BF16):
    return jax.ShapeDtypeStruct(dims, dtype)


def slot_kernel(lon_ref, patch_ref, slot_ref, sems):
    lon = lon_ref[0]
    copies = [
        pltpu.make_async_copy(
            patch_ref.at[:, pl.ds(i * TOK, TOK)], slot_ref.at[lax.rem(lon * LEVELS + i, RING)], sems.at[i]
        )
        for i in range(LEVELS)
    ]
    for copy in copies:
        copy.start()
    for copy in copies:
        copy.wait()


def prep_kernel(
    core_ref, kvw_ref, embed_w_ref, level_ref, query_ref, grad_ref, tall_ref, wide_ref, own_ref, rows, spread, plain
):
    position = lax.broadcasted_iota(jnp.int32, (D, D), 0)
    feature = lax.broadcasted_iota(jnp.int32, (D, D), 1)
    core, z, lon, pair = position >> 8, (position >> 5) & 7, (position >> 1) & 15, position & 1
    reorder = jnp.where(lon * 32 + z * 4 + core * 2 + pair == feature, 1.0, 0.0).astype(BF16)
    for c in range(4):
        part = jnp.dot(reorder, kvw_ref[:, c * 256 : (c + 1) * 256], preferred_element_type=F32)
        tall_ref[c * 256 : (c + 1) * 256, :] = part.T.astype(BF16)
    rows[...] = jnp.zeros_like(rows)
    rows[:FEAT, :] = embed_w_ref[...].astype(F32)
    rows[FEAT : FEAT + LEVELS, :] = level_ref[...].astype(F32)
    weights = rows[...]
    spread[...] = jnp.zeros_like(spread)
    spread[:AUG, :] = weights
    plain[:, :TOK] = spread[:TOK, :].T.astype(BF16)
    wide_ref[:, RAW : RAW + TOK] = jnp.dot(reorder, plain[:, :TOK], preferred_element_type=F32).astype(BF16)
    weights = weights - jnp.mean(weights, axis=1, keepdims=True)
    high = weights.astype(BF16)
    spread[...] = jnp.zeros_like(spread)
    spread[:AUG, :] = high.astype(F32)
    spread[TOK : TOK + AUG, :] = weights - high.astype(F32)
    plain[...] = spread[...].T.astype(BF16)
    wide_ref[:, WAUG : WAUG + 256] = jnp.dot(reorder, plain[...], preferred_element_type=F32).astype(BF16)
    product = jnp.dot(tall_ref[:D, :], wide_ref[:, WAUG : WAUG + 256], preferred_element_type=F32)
    product = product[:, :TOK] + product[:, TOK:]
    high = product.astype(BF16)
    wide_ref[:, QUERY : QUERY + TOK] = high
    wide_ref[:, QUERY + TOK : QUERY + 256] = (product - high.astype(F32)).astype(BF16)
    side = core_ref[0] * HEAD
    for z in range(ZED):
        rows_here = slice(z * HEAD, (z + 1) * HEAD)
        start = pl.multiple_of(z * 2 * HEAD + side, HEAD)
        own_ref[rows_here, : 2 * D] = kvw_ref[pl.ds(start, HEAD), :]
        own_ref[rows_here, 2 * D :] = plain[pl.ds(start, HEAD), :]
    mean = jnp.mean(kvw_ref[...].astype(F32), axis=0, keepdims=True)
    high = mean.astype(BF16).astype(F32)
    row = lax.broadcasted_iota(jnp.int32, (OWN - HALF, 2 * D), 0)
    own_ref[HALF:, : 2 * D] = jnp.where(row == 0, high, jnp.where(row == 1, mean - high, 0.0)).astype(BF16)
    own_ref[HALF:, 2 * D :] = jnp.zeros((OWN - HALF, DEEP), BF16)
    head = lax.broadcasted_iota(jnp.int32, (HEADS, D), 0)
    owner = lax.broadcasted_iota(jnp.int32, (HEADS, D), 1) >> 5
    spread[:32, :] = jnp.zeros((32, D), F32)
    for a in range(LATENT):
        block = jnp.where(head == owner, query_ref[a : a + 1, :].astype(F32), 0.0)
        spread[32 + a * HEADS : 32 + (a + 1) * HEADS, :] = block
        spread[80 + a * HEADS : 80 + (a + 1) * HEADS, :] = block
    tall_ref[2 * D : 2 * D + AH, :] = spread[80:128, :].astype(BF16)
    tall_ref[2 * D + AH :, :] = jnp.zeros((16, D), BF16)
    wide_ref[:, QBD : QBD + GS] = spread[:GS, :].T.astype(BF16)
    for a in range(LATENT):
        at = GRAD + a * TOK
        wide_ref[:, at : at + TOK] = grad_ref[a].astype(F32).T.astype(BF16)


def main_kernel(
    lon_ref, count_ref, recv_ref, tall_ref, wide_ref,
    keep_out, send_out,
    g_s, paug_s, hid_s, kv_s, left_s, pin_s, inv_s, sc_s, ga_s, w_s,
):
    lon = lon_ref[0]
    count = count_ref[0]
    for a in range(LATENT):
        g_s[a] = wide_ref[:, GRAD + a * TOK : GRAD + (a + 1) * TOK].astype(F32)
    left_s[2 * D : 2 * D + 32, :] = jnp.zeros((32, SPAN), BF16)
    left_s[2 * D + GS + AUG :, :] = jnp.zeros((TOK - AUG, SPAN), BF16)
    pin_s[AUG:, :] = jnp.zeros((TOK - AUG, SPAN), BF16)
    paug_s[AUG:, :] = jnp.zeros((TOK - AUG, SPAN), BF16)

    def lanes_of(group):
        return slice(group[0] * TOK, (group[-1] + 1) * TOK)

    def embed(group):
        at = lanes_of(group)
        row = lax.broadcasted_iota(jnp.int32, (AUG - FEAT, TOK), 0)
        for l in group:
            lanes = slice(l * TOK, (l + 1) * TOK)
            patches = recv_ref[(RING * l + lon) // LEVELS]
            one_hot = jnp.where(row == l, 1.0, 0.0).astype(BF16)
            paug_s[:FEAT, lanes] = patches
            paug_s[FEAT:AUG, lanes] = one_hot
        embedded = jnp.dot(wide_ref[:, RAW : RAW + TOK], paug_s[:, at], preferred_element_type=F32)
        center = embedded - jnp.mean(embedded, axis=0, keepdims=True)
        inv_std = lax.rsqrt(jnp.mean(center * center, axis=0, keepdims=True) + EPSILON)
        inv_s[:, at] = inv_std
        hid_s[:, at] = (center * inv_std).astype(BF16)
        pin_s[:AUG, at] = (paug_s[:AUG, at].astype(F32) * inv_std).astype(BF16)

    def keys(group):
        at = lanes_of(group)
        kv_s[:, at] = jnp.dot(tall_ref[: 2 * D, :], hid_s[:, at], preferred_element_type=F32).astype(BF16)

    def score(group):
        at = lanes_of(group)
        sc_s[:, at] = (
            jnp.dot(tall_ref[2 * D : 2 * D + AH, :], kv_s[:D, at], preferred_element_type=F32) * SCORE_SCALE
        )
        for h in range(HEADS):
            rows = slice(h * HEAD, (h + 1) * HEAD)
            grads = [g_s[a, rows, :] for a in range(LATENT)]
            for l in group:
                lanes = slice(l * TOK, (l + 1) * TOK)
                values = kv_s[D + h * HEAD : D + (h + 1) * HEAD, lanes].astype(F32)
                for a in range(LATENT):
                    product = (grads[a] * values).reshape(4, 8, TOK)
                    ah = a * HEADS + h
                    ga_s[ah : ah + 1, lanes] = jnp.sum(jnp.sum(product, axis=0), axis=0, keepdims=True)

    every = tuple(range(LEVELS))
    embed(every)
    keys(every)
    score(every)

    masked = [jnp.where(l < count, sc_s[:, l * TOK : (l + 1) * TOK], MASKED) for l in range(LEVELS)]
    peak = functools.reduce(jnp.maximum, masked)
    total = jnp.zeros_like(peak)
    for l in range(LEVELS):
        exponent = jnp.exp(masked[l] - peak)
        w_s[:, l * TOK : (l + 1) * TOK] = exponent
        total = total + exponent
    inverse = 1.0 / total
    inner = jnp.zeros_like(peak)
    for l in range(LEVELS):
        lanes = slice(l * TOK, (l + 1) * TOK)
        inner = inner + w_s[:, lanes] * inverse * ga_s[:, lanes]
    for l in range(LEVELS):
        lanes = slice(l * TOK, (l + 1) * TOK)
        attention = w_s[:, lanes] * inverse
        weight = attention.astype(BF16).astype(F32)
        w_s[:, lanes] = weight
        grad_attn = ga_s[:, lanes]
        grad_score = attention * (grad_attn - inner)
        slope = jnp.sum(grad_score * sc_s[:, lanes] + weight * grad_attn, axis=0, keepdims=True)
        scale = slope * inv_s[:, lanes] * (1.0 / D)
        left_s[2 * D + GS : 2 * D + GS + AUG, lanes] = (paug_s[:AUG, lanes].astype(F32) * scale).astype(BF16)
        grad_score = grad_score * SCORE_SCALE
        high = grad_score.astype(BF16)
        left_s[2 * D + 32 : 2 * D + 80, lanes] = (grad_score - high.astype(F32)).astype(BF16)
        left_s[2 * D + 80 : 2 * D + GS, lanes] = high

    def grad_kv(group):
        at = lanes_of(group)
        left_s[:D, at] = jnp.dot(
            wide_ref[:, QBD : QBD + GS], left_s[2 * D : 2 * D + GS, at], preferred_element_type=F32
        ).astype(BF16)
        for h in range(HEADS):
            rows = slice(h * HEAD, (h + 1) * HEAD)
            grads = [g_s[a, rows, :] for a in range(LATENT)]
            for l in group:
                lanes = slice(l * TOK, (l + 1) * TOK)
                grad_values = None
                for a in range(LATENT):
                    term = w_s[a * HEADS + h : a * HEADS + h + 1, lanes] * grads[a]
                    grad_values = term if grad_values is None else grad_values + term
                left_s[D + h * HEAD : D + (h + 1) * HEAD, lanes] = grad_values.astype(BF16)

    grad_kv(every)

    outer = lax.dot_general(left_s[...], pin_s[...], NT, preferred_element_type=F32)
    keep_out[...] = outer
    send_out[...] = outer.astype(BF16)


def post_kernel(core_ref, keep_ref, recv_ref, wide_ref, own_ref, part_ref):
    total = keep_ref[...] + recv_ref[...].astype(F32)
    outer = total[: 2 * D]
    high = outer.astype(BF16)
    low = (outer - high.astype(F32)).astype(BF16)
    start = pl.multiple_of(core_ref[0] * HALF, HALF)
    part_ref[:, : 2 * D] = lax.dot_general(
        wide_ref[pl.ds(start, HALF), WAUG : WAUG + DEEP],
        jnp.concatenate([high, high], axis=1),
        NT,
        preferred_element_type=F32,
    ).astype(BF16)
    grads = jnp.dot(own_ref[:, : 2 * D], jnp.concatenate([high, low], axis=1), preferred_element_type=F32)
    grads = grads[:, :TOK] + grads[:, TOK:]
    gram = total[2 * D + GS :].astype(BF16)
    grads = (
        grads[:HALF]
        - (grads[HALF : HALF + 1] + grads[HALF + 1 : HALF + 2])
        - jnp.dot(own_ref[:HALF, 2 * D :], jnp.concatenate([gram, gram], axis=0), preferred_element_type=F32)
    )
    scores = total[2 * D : 2 * D + GS]
    scores = jnp.concatenate([jnp.zeros((FEAT, TOK), F32), scores[80:] + scores[32:80]], axis=0).astype(BF16)
    queries = lax.dot_general(
        wide_ref[:, QUERY : QUERY + DEEP],
        jnp.concatenate([scores, scores], axis=1),
        NT,
        preferred_element_type=F32,
    )
    head = lax.broadcasted_iota(jnp.int32, (D, GS), 0) >> 5
    lane = lax.broadcasted_iota(jnp.int32, (D, GS), 1)
    queries = jnp.where((lane & 15) == head, queries, 0.0).reshape(HEADS, HEAD, GS)
    queries = jnp.concatenate([jnp.sum(queries, axis=0)] * ZED, axis=0)
    part_ref[:, 2 * D :] = jnp.where(lane[:HALF] < FEAT, grads, queries).astype(BF16)


def sum_z_kernel(part_ref, share_ref, total, tile):
    acc = part_ref[0].astype(F32)
    for source in range(1, ZED):
        acc = acc + part_ref[source].astype(F32)
    total[...] = acc
    block = acc[:, 2 * D :].astype(BF16)
    for target in range(RING):
        for c in range(8):
            tile[target, 2 * c : 2 * c + 2, :] = total[2 * target : 2 * target + 2, c * TOK : (c + 1) * TOK]
        share_ref[target, 0:16, :] = tile[target].astype(BF16)
        share_ref[target, 16:48, :] = block


def sum_lon_kernel(share_ref, kv_out, embed_out, query_out, tile, turned):
    acc = share_ref[0].astype(F32)
    for source in range(1, RING):
        acc = acc + share_ref[source].astype(F32)
    tile[...] = acc[:16]
    for c in range(8):
        kv_out[:, c * TOK : (c + 1) * TOK] = tile[2 * c : 2 * c + 2, :]
    embed_out[...] = acc[16:, :FEAT]
    turned[...] = acc[16:, :].T
    for a in range(LATENT):
        for h in range(HEADS):
            at = FEAT + a * HEADS + h
            query_out[a : a + 1, h * HEAD : (h + 1) * HEAD] = turned[at : at + 1, :]


def call(kernel, outs, in_specs, scratch, mib, name):
    return pl.pallas_call(
        kernel,
        out_shape=outs,
        in_specs=in_specs,
        out_specs=jax.tree.map(lambda _: VMEM, outs),
        scratch_shapes=scratch,
        compiler_params=params(mib),
        name=name,
    )


def on_device(level_patches, level_embed, embed_weight, kv_weight, query, band_levels, grad_out):
    lon = lax.axis_index("lon").astype(jnp.int32).reshape(1)
    core = (lax.axis_index("lat").astype(jnp.int32) & 1).reshape(1)
    slots = pl.pallas_call(
        slot_kernel,
        out_shape=shape(RING, FEAT, TOK),
        in_specs=[SMEM, HBM],
        out_specs=HBM,
        scratch_shapes=[pltpu.SemaphoreType.DMA((LEVELS,))],
        compiler_params=params(8),
        name="slots",
    )(lon, level_patches[0].T)
    tall, wide, own = call(
        prep_kernel,
        (shape(2 * D + 64, D), shape(D, RAW + TOK), shape(OWN, 2 * D + DEEP)),
        [SMEM] + [VMEM] * 5,
        [pltpu.VMEM((AUG, D), F32), pltpu.VMEM((DEEP, D), F32), pltpu.VMEM((D, DEEP), BF16)],
        24,
        "prep",
    )(core, kv_weight, embed_weight, level_embed, query, grad_out[0].transpose(1, 0, 2))
    recv = lax.all_to_all(slots, "lon", 0, 0, tiled=True)
    keep, send = call(
        main_kernel,
        (shape(LEFT, TOK, dtype=F32), shape(LEFT, TOK)),
        [SMEM, SMEM] + [VMEM] * 3,
        [
            pltpu.VMEM((LATENT, D, TOK), F32),
            pltpu.VMEM((TOK, SPAN), BF16),
            pltpu.VMEM((D, SPAN), BF16),
            pltpu.VMEM((2 * D, SPAN), BF16),
            pltpu.VMEM((LEFT, SPAN), BF16),
            pltpu.VMEM((TOK, SPAN), BF16),
            pltpu.VMEM((1, SPAN), F32),
            pltpu.VMEM((AH, SPAN), F32),
            pltpu.VMEM((AH, SPAN), F32),
            pltpu.VMEM((AH, SPAN), F32),
        ],
        28,
        "main",
    )(lon, band_levels, recv, tall, wide)
    lats = lax.axis_size("lat")
    other = lax.ppermute(send, "lat", [(i, i ^ 1) for i in range(lats)])
    part = call(post_kernel, shape(HALF, ROW), [SMEM] + [VMEM] * 4, [], 16, "post")(core, keep, other, wide, own)
    parts = lax.all_to_all(
        part.reshape(ZED, HALF // ZED, ROW),
        "lat",
        0,
        0,
        tiled=True,
        axis_index_groups=[[2 * z + c for z in range(ZED)] for c in range(2)],
    )
    share = call(
        sum_z_kernel,
        shape(RING, SHARE, TOK),
        [VMEM],
        [pltpu.VMEM((HALF // ZED, ROW), F32), pltpu.VMEM((RING, 16, TOK), F32)],
        8,
        "sum_z",
    )(parts)
    shared = lax.all_to_all(share, "lon", 0, 0, tiled=True)
    kv_grad, embed_grad, query_grad = call(
        sum_lon_kernel,
        (shape(2, 2 * D, dtype=F32), shape(32, FEAT, dtype=F32), shape(LATENT, D, dtype=F32)),
        [VMEM],
        [pltpu.VMEM((16, TOK), F32), pltpu.VMEM((TOK, 32), F32)],
        8,
        "sum_lon",
    )(shared)
    return (kv_grad, embed_grad.T, query_grad)


def solution(mesh):
    placed = (P("lat", "lon", None), P(), P(), P(), P(), P("lat"), P("lat", "lon", None, None))
    return jax.shard_map(
        on_device,
        mesh=mesh,
        in_specs=placed,
        out_specs=(P(("lon", "lat"), None), P(None, "lat"), P()),
        check_vma=False,
    )
```

```python
import functools

import jax
import jax.numpy as jnp
from jax import lax
from jax.experimental import pallas as pl
from jax.experimental.pallas import tpu as pltpu
from jax.sharding import PartitionSpec as P

HEADS = 16
SCORE_SCALE = 0.125
EPSILON = 1e-05
MASKED = -1e30
BF16 = jnp.bfloat16
F32 = jnp.float32

LEVELS = 13
TOK = 128
SPAN = LEVELS * TOK
D = 512
HEAD = D // HEADS
FEAT = 80
AUG = 96
LATENT = 3
AH = LATENT * HEADS
GS = 128
LEFT = D + 2 * GS
OWN = D // 2 + 32
NT = (((1,), (1,)), ((), ()))
RING = 16
ZED = 8
HALF = D // 2
WAUG = 0
QBD = 256
GRAD = 384
QUERY = 768
RAW = 1024
DEEP = 256
ROW = 2 * D + TOK
SHARE = 48

VMEM = pl.BlockSpec(memory_space=pltpu.VMEM)
SMEM = pl.BlockSpec(memory_space=pltpu.SMEM)
HBM = pl.BlockSpec(memory_space=pltpu.HBM)


def params(mib):
    return pltpu.CompilerParams(vmem_limit_bytes=mib * 1024 * 1024)


def shape(*dims, dtype=BF16):
    return jax.ShapeDtypeStruct(dims, dtype)


def slot_kernel(lon_ref, patch_ref, slot_ref, sems):
    lon = lon_ref[0]
    copies = [
        pltpu.make_async_copy(
            patch_ref.at[:, pl.ds(i * TOK, TOK)], slot_ref.at[lax.rem(lon * LEVELS + i, RING)], sems.at[i]
        )
        for i in range(LEVELS)
    ]
    for copy in copies:
        copy.start()
    for copy in copies:
        copy.wait()


def prep_kernel(
    core_ref, kvw_ref, embed_w_ref, level_ref, query_ref, grad_ref, tall_ref, wide_ref, own_ref, rows, spread, plain
):
    position = lax.broadcasted_iota(jnp.int32, (D, D), 0)
    feature = lax.broadcasted_iota(jnp.int32, (D, D), 1)
    core, z, lon, pair = position >> 8, (position >> 5) & 7, (position >> 1) & 15, position & 1
    reorder = jnp.where(lon * 32 + z * 4 + core * 2 + pair == feature, 1.0, 0.0).astype(BF16)
    for c in range(4):
        part = jnp.dot(reorder, kvw_ref[:, c * 256 : (c + 1) * 256], preferred_element_type=F32)
        tall_ref[c * 256 : (c + 1) * 256, :] = part.T.astype(BF16)
    rows[...] = jnp.zeros_like(rows)
    rows[:FEAT, :] = embed_w_ref[...].astype(F32)
    rows[FEAT : FEAT + LEVELS, :] = level_ref[...].astype(F32)
    weights = rows[...]
    spread[...] = jnp.zeros_like(spread)
    spread[:AUG, :] = weights
    plain[:, :TOK] = spread[:TOK, :].T.astype(BF16)
    wide_ref[:, RAW : RAW + TOK] = jnp.dot(reorder, plain[:, :TOK], preferred_element_type=F32).astype(BF16)
    weights = weights - jnp.mean(weights, axis=1, keepdims=True)
    high = weights.astype(BF16)
    spread[...] = jnp.zeros_like(spread)
    spread[:AUG, :] = high.astype(F32)
    spread[TOK : TOK + AUG, :] = weights - high.astype(F32)
    plain[...] = spread[...].T.astype(BF16)
    wide_ref[:, WAUG : WAUG + 256] = jnp.dot(reorder, plain[...], preferred_element_type=F32).astype(BF16)
    product = jnp.dot(tall_ref[:D, :], wide_ref[:, WAUG : WAUG + 256], preferred_element_type=F32)
    product = product[:, :TOK] + product[:, TOK:]
    high = product.astype(BF16)
    wide_ref[:, QUERY : QUERY + TOK] = high
    wide_ref[:, QUERY + TOK : QUERY + 256] = (product - high.astype(F32)).astype(BF16)
    side = core_ref[0] * HEAD
    for z in range(ZED):
        rows_here = slice(z * HEAD, (z + 1) * HEAD)
        start = pl.multiple_of(z * 2 * HEAD + side, HEAD)
        own_ref[rows_here, : 2 * D] = kvw_ref[pl.ds(start, HEAD), :]
        own_ref[rows_here, 2 * D :] = plain[pl.ds(start, HEAD), :]
    mean = jnp.mean(kvw_ref[...].astype(F32), axis=0, keepdims=True)
    high = mean.astype(BF16).astype(F32)
    row = lax.broadcasted_iota(jnp.int32, (OWN - HALF, 2 * D), 0)
    own_ref[HALF:, : 2 * D] = jnp.where(row == 0, high, jnp.where(row == 1, mean - high, 0.0)).astype(BF16)
    own_ref[HALF:, 2 * D :] = jnp.zeros((OWN - HALF, DEEP), BF16)
    head = lax.broadcasted_iota(jnp.int32, (HEADS, D), 0)
    owner = lax.broadcasted_iota(jnp.int32, (HEADS, D), 1) >> 5
    spread[:32, :] = jnp.zeros((32, D), F32)
    for a in range(LATENT):
        block = jnp.where(head == owner, query_ref[a : a + 1, :].astype(F32), 0.0)
        spread[32 + a * HEADS : 32 + (a + 1) * HEADS, :] = block
        spread[80 + a * HEADS : 80 + (a + 1) * HEADS, :] = block
    tall_ref[2 * D : 2 * D + AH, :] = spread[80:128, :].astype(BF16)
    tall_ref[2 * D + AH :, :] = jnp.zeros((16, D), BF16)
    wide_ref[:, QBD : QBD + GS] = spread[:GS, :].T.astype(BF16)
    for a in range(LATENT):
        at = GRAD + a * TOK
        wide_ref[:, at : at + TOK] = grad_ref[a].astype(F32).T.astype(BF16)


def main_kernel(
    lon_ref, count_ref, recv_ref, tall_ref, wide_ref,
    keep_out, send_out,
    g_s, paug_s, hid_s, kv_s, left_s, pin_s, inv_s, sc_s, ga_s, w_s,
):
    lon = lon_ref[0]
    count = count_ref[0]
    for a in range(LATENT):
        g_s[a] = wide_ref[:, GRAD + a * TOK : GRAD + (a + 1) * TOK].astype(F32)
    left_s[D : D + 32, :] = jnp.zeros((32, SPAN), BF16)
    left_s[D + GS + AUG :, :] = jnp.zeros((TOK - AUG, SPAN), BF16)
    pin_s[AUG:, :] = jnp.zeros((TOK - AUG, SPAN), BF16)
    paug_s[AUG:, :] = jnp.zeros((TOK - AUG, SPAN), BF16)

    def lanes_of(group):
        return slice(group[0] * TOK, (group[-1] + 1) * TOK)

    def embed(group):
        at = lanes_of(group)
        row = lax.broadcasted_iota(jnp.int32, (AUG - FEAT, TOK), 0)
        for l in group:
            lanes = slice(l * TOK, (l + 1) * TOK)
            patches = recv_ref[(RING * l + lon) // LEVELS]
            one_hot = jnp.where(row == l, 1.0, 0.0).astype(BF16)
            paug_s[:FEAT, lanes] = patches
            paug_s[FEAT:AUG, lanes] = one_hot
        embedded = jnp.dot(wide_ref[:, RAW : RAW + TOK], paug_s[:, at], preferred_element_type=F32)
        center = embedded - jnp.mean(embedded, axis=0, keepdims=True)
        inv_std = lax.rsqrt(jnp.mean(center * center, axis=0, keepdims=True) + EPSILON)
        inv_s[:, at] = inv_std
        hid_s[:, at] = (center * inv_std).astype(BF16)
        pin_s[:AUG, at] = (paug_s[:AUG, at].astype(F32) * inv_std).astype(BF16)

    def keys(group):
        at = lanes_of(group)
        kv_s[:, at] = jnp.dot(tall_ref[: 2 * D, :], hid_s[:, at], preferred_element_type=F32).astype(BF16)

    def score(group):
        at = lanes_of(group)
        sc_s[:, at] = (
            jnp.dot(tall_ref[2 * D : 2 * D + AH, :], kv_s[:D, at], preferred_element_type=F32) * SCORE_SCALE
        )
        for h in range(HEADS):
            rows = slice(h * HEAD, (h + 1) * HEAD)
            grads = [g_s[a, rows, :] for a in range(LATENT)]
            for l in group:
                lanes = slice(l * TOK, (l + 1) * TOK)
                values = kv_s[D + h * HEAD : D + (h + 1) * HEAD, lanes].astype(F32)
                for a in range(LATENT):
                    product = (grads[a] * values).reshape(4, 8, TOK)
                    ah = a * HEADS + h
                    ga_s[ah : ah + 1, lanes] = jnp.sum(jnp.sum(product, axis=0), axis=0, keepdims=True)

    every = tuple(range(LEVELS))
    embed(every)
    keys(every)
    score(every)

    masked = [jnp.where(l < count, sc_s[:, l * TOK : (l + 1) * TOK], MASKED) for l in range(LEVELS)]
    peak = functools.reduce(jnp.maximum, masked)
    total = jnp.zeros_like(peak)
    for l in range(LEVELS):
        exponent = jnp.exp(masked[l] - peak)
        w_s[:, l * TOK : (l + 1) * TOK] = exponent
        total = total + exponent
    inverse = 1.0 / total
    inner = jnp.zeros_like(peak)
    for l in range(LEVELS):
        lanes = slice(l * TOK, (l + 1) * TOK)
        inner = inner + w_s[:, lanes] * inverse * ga_s[:, lanes]
    for l in range(LEVELS):
        lanes = slice(l * TOK, (l + 1) * TOK)
        attention = w_s[:, lanes] * inverse
        weight = attention.astype(BF16).astype(F32)
        w_s[:, lanes] = weight
        grad_attn = ga_s[:, lanes]
        grad_score = attention * (grad_attn - inner)
        slope = jnp.sum(grad_score * sc_s[:, lanes] + weight * grad_attn, axis=0, keepdims=True)
        scale = slope * inv_s[:, lanes] * (1.0 / D)
        left_s[D + GS : D + GS + AUG, lanes] = (paug_s[:AUG, lanes].astype(F32) * scale).astype(BF16)
        grad_score = grad_score * SCORE_SCALE
        high = grad_score.astype(BF16)
        left_s[D + 32 : D + 80, lanes] = (grad_score - high.astype(F32)).astype(BF16)
        left_s[D + 80 : D + GS, lanes] = high

    def grad_values_of(group):
        for h in range(HEADS):
            rows = slice(h * HEAD, (h + 1) * HEAD)
            grads = [g_s[a, rows, :] for a in range(LATENT)]
            for l in group:
                lanes = slice(l * TOK, (l + 1) * TOK)
                grad_values = None
                for a in range(LATENT):
                    term = w_s[a * HEADS + h : a * HEADS + h + 1, lanes] * grads[a]
                    grad_values = term if grad_values is None else grad_values + term
                left_s[rows, lanes] = grad_values.astype(BF16)

    grad_values_of(every)

    outer = lax.dot_general(left_s[...], pin_s[...], NT, preferred_element_type=F32)
    keep_out[...] = outer
    send_out[...] = outer.astype(BF16)


def post_kernel(core_ref, keep_ref, recv_ref, wide_ref, own_ref, part_ref):
    total = keep_ref[...] + recv_ref[...].astype(F32)
    scores = total[D : D + GS]
    scores = scores[80:] + scores[32:80]
    high = scores.astype(BF16)
    low = (scores - high.astype(F32)).astype(BF16)
    outer = jnp.dot(
        wide_ref[:, QBD : QBD + GS],
        jnp.concatenate([jnp.zeros((32, TOK), BF16), low, high], axis=0),
        preferred_element_type=F32,
    )
    outer = jnp.concatenate([outer, total[:D]], axis=0)
    high = outer.astype(BF16)
    low = (outer - high.astype(F32)).astype(BF16)
    start = pl.multiple_of(core_ref[0] * HALF, HALF)
    part_ref[:, : 2 * D] = lax.dot_general(
        wide_ref[pl.ds(start, HALF), WAUG : WAUG + DEEP],
        jnp.concatenate([high, high], axis=1),
        NT,
        preferred_element_type=F32,
    ).astype(BF16)
    grads = jnp.dot(own_ref[:, : 2 * D], jnp.concatenate([high, low], axis=1), preferred_element_type=F32)
    grads = grads[:, :TOK] + grads[:, TOK:]
    gram = total[D + GS :].astype(BF16)
    grads = (
        grads[:HALF]
        - (grads[HALF : HALF + 1] + grads[HALF + 1 : HALF + 2])
        - jnp.dot(own_ref[:HALF, 2 * D :], jnp.concatenate([gram, gram], axis=0), preferred_element_type=F32)
    )
    scores = jnp.concatenate([jnp.zeros((FEAT, TOK), F32), scores], axis=0).astype(BF16)
    queries = lax.dot_general(
        wide_ref[:, QUERY : QUERY + DEEP],
        jnp.concatenate([scores, scores], axis=1),
        NT,
        preferred_element_type=F32,
    )
    head = lax.broadcasted_iota(jnp.int32, (D, GS), 0) >> 5
    lane = lax.broadcasted_iota(jnp.int32, (D, GS), 1)
    queries = jnp.where((lane & 15) == head, queries, 0.0).reshape(HEADS, HEAD, GS)
    queries = jnp.concatenate([jnp.sum(queries, axis=0)] * ZED, axis=0)
    part_ref[:, 2 * D :] = jnp.where(lane[:HALF] < FEAT, grads, queries).astype(BF16)


def sum_z_kernel(part_ref, share_ref, total, tile):
    acc = part_ref[0].astype(F32)
    for source in range(1, ZED):
        acc = acc + part_ref[source].astype(F32)
    total[...] = acc
    block = acc[:, 2 * D :].astype(BF16)
    for target in range(RING):
        for c in range(8):
            tile[target, 2 * c : 2 * c + 2, :] = total[2 * target : 2 * target + 2, c * TOK : (c + 1) * TOK]
        share_ref[target, 0:16, :] = tile[target].astype(BF16)
        share_ref[target, 16:48, :] = block


def sum_lon_kernel(share_ref, kv_out, embed_out, query_out, tile, turned):
    acc = share_ref[0].astype(F32)
    for source in range(1, RING):
        acc = acc + share_ref[source].astype(F32)
    tile[...] = acc[:16]
    for c in range(8):
        kv_out[:, c * TOK : (c + 1) * TOK] = tile[2 * c : 2 * c + 2, :]
    embed_out[...] = acc[16:, :FEAT]
    turned[...] = acc[16:, :].T
    for a in range(LATENT):
        for h in range(HEADS):
            at = FEAT + a * HEADS + h
            query_out[a : a + 1, h * HEAD : (h + 1) * HEAD] = turned[at : at + 1, :]


def call(kernel, outs, in_specs, scratch, mib, name):
    return pl.pallas_call(
        kernel,
        out_shape=outs,
        in_specs=in_specs,
        out_specs=jax.tree.map(lambda _: VMEM, outs),
        scratch_shapes=scratch,
        compiler_params=params(mib),
        name=name,
    )


def on_device(level_patches, level_embed, embed_weight, kv_weight, query, band_levels, grad_out):
    lon = lax.axis_index("lon").astype(jnp.int32).reshape(1)
    core = (lax.axis_index("lat").astype(jnp.int32) & 1).reshape(1)
    slots = pl.pallas_call(
        slot_kernel,
        out_shape=shape(RING, FEAT, TOK),
        in_specs=[SMEM, HBM],
        out_specs=HBM,
        scratch_shapes=[pltpu.SemaphoreType.DMA((LEVELS,))],
        compiler_params=params(8),
        name="slots",
    )(lon, level_patches[0].T)
    tall, wide, own = call(
        prep_kernel,
        (shape(2 * D + 64, D), shape(D, RAW + TOK), shape(OWN, 2 * D + DEEP)),
        [SMEM] + [VMEM] * 5,
        [pltpu.VMEM((AUG, D), F32), pltpu.VMEM((DEEP, D), F32), pltpu.VMEM((D, DEEP), BF16)],
        24,
        "prep",
    )(core, kv_weight, embed_weight, level_embed, query, grad_out[0].transpose(1, 0, 2))
    recv = lax.all_to_all(slots, "lon", 0, 0, tiled=True)
    keep, send = call(
        main_kernel,
        (shape(LEFT, TOK, dtype=F32), shape(LEFT, TOK)),
        [SMEM, SMEM] + [VMEM] * 3,
        [
            pltpu.VMEM((LATENT, D, TOK), F32),
            pltpu.VMEM((TOK, SPAN), BF16),
            pltpu.VMEM((D, SPAN), BF16),
            pltpu.VMEM((2 * D, SPAN), BF16),
            pltpu.VMEM((LEFT, SPAN), BF16),
            pltpu.VMEM((TOK, SPAN), BF16),
            pltpu.VMEM((1, SPAN), F32),
            pltpu.VMEM((AH, SPAN), F32),
            pltpu.VMEM((AH, SPAN), F32),
            pltpu.VMEM((AH, SPAN), F32),
        ],
        28,
        "main",
    )(lon, band_levels, recv, tall, wide)
    lats = lax.axis_size("lat")
    other = lax.ppermute(send, "lat", [(i, i ^ 1) for i in range(lats)])
    part = call(post_kernel, shape(HALF, ROW), [SMEM] + [VMEM] * 4, [], 16, "post")(core, keep, other, wide, own)
    parts = lax.all_to_all(
        part.reshape(ZED, HALF // ZED, ROW),
        "lat",
        0,
        0,
        tiled=True,
        axis_index_groups=[[2 * z + c for z in range(ZED)] for c in range(2)],
    )
    share = call(
        sum_z_kernel,
        shape(RING, SHARE, TOK),
        [VMEM],
        [pltpu.VMEM((HALF // ZED, ROW), F32), pltpu.VMEM((RING, 16, TOK), F32)],
        8,
        "sum_z",
    )(parts)
    shared = lax.all_to_all(share, "lon", 0, 0, tiled=True)
    kv_grad, embed_grad, query_grad = call(
        sum_lon_kernel,
        (shape(2, 2 * D, dtype=F32), shape(32, FEAT, dtype=F32), shape(LATENT, D, dtype=F32)),
        [VMEM],
        [pltpu.VMEM((16, TOK), F32), pltpu.VMEM((TOK, 32), F32)],
        8,
        "sum_lon",
    )(shared)
    return (kv_grad, embed_grad.T, query_grad)


def solution(mesh):
    placed = (P("lat", "lon", None), P(), P(), P(), P(), P("lat"), P("lat", "lon", None, None))
    return jax.shard_map(
        on_device,
        mesh=mesh,
        in_specs=placed,
        out_specs=(P(("lon", "lat"), None), P(None, "lat"), P()),
        check_vma=False,
    )
```

```python
import functools

import jax
import jax.numpy as jnp
from jax import lax
from jax.experimental import pallas as pl
from jax.experimental.pallas import tpu as pltpu
from jax.sharding import PartitionSpec as P

HEADS = 16
SCORE_SCALE = 0.125
EPSILON = 1e-05
MASKED = -1e30
BF16 = jnp.bfloat16
F32 = jnp.float32

LEVELS = 13
TOK = 128
SPAN = LEVELS * TOK
D = 512
HEAD = D // HEADS
FEAT = 80
AUG = 96
LATENT = 3
AH = LATENT * HEADS
GS = 128
LEFT = D + 2 * GS
OWN = D // 2 + 32
NT = (((1,), (1,)), ((), ()))
RING = 16
ZED = 8
HALF = D // 2
WAUG = 0
QBD = 256
GRAD = 384
QUERY = 768
RAW = 1024
DEEP = 256
ROW = 2 * D + TOK
SHARE = 48

VMEM = pl.BlockSpec(memory_space=pltpu.VMEM)
SMEM = pl.BlockSpec(memory_space=pltpu.SMEM)
HBM = pl.BlockSpec(memory_space=pltpu.HBM)


def params(mib):
    return pltpu.CompilerParams(vmem_limit_bytes=mib * 1024 * 1024)


def shape(*dims, dtype=BF16):
    return jax.ShapeDtypeStruct(dims, dtype)


def slot_kernel(lon_ref, patch_ref, slot_ref, sems):
    lon = lon_ref[0]
    copies = [
        pltpu.make_async_copy(
            patch_ref.at[:, pl.ds(i * TOK, TOK)], slot_ref.at[lax.rem(lon * LEVELS + i, RING)], sems.at[i]
        )
        for i in range(LEVELS)
    ]
    for copy in copies:
        copy.start()
    for copy in copies:
        copy.wait()


def prep_kernel(
    core_ref, kvw_ref, embed_w_ref, level_ref, query_ref, grad_ref, tall_ref, wide_ref, own_ref, rows, spread, plain
):
    position = lax.broadcasted_iota(jnp.int32, (D, D), 0)
    feature = lax.broadcasted_iota(jnp.int32, (D, D), 1)
    core, z, lon, pair = position >> 8, (position >> 5) & 7, (position >> 1) & 15, position & 1
    reorder = jnp.where(lon * 32 + z * 4 + core * 2 + pair == feature, 1.0, 0.0).astype(BF16)
    for c in range(4):
        part = jnp.dot(reorder, kvw_ref[:, c * 256 : (c + 1) * 256], preferred_element_type=F32)
        tall_ref[c * 256 : (c + 1) * 256, :] = part.T.astype(BF16)
    rows[...] = jnp.zeros_like(rows)
    rows[:FEAT, :] = embed_w_ref[...].astype(F32)
    rows[FEAT : FEAT + LEVELS, :] = level_ref[...].astype(F32)
    weights = rows[...]
    spread[...] = jnp.zeros_like(spread)
    spread[:AUG, :] = weights
    plain[:, :TOK] = spread[:TOK, :].T.astype(BF16)
    wide_ref[:, RAW : RAW + TOK] = jnp.dot(reorder, plain[:, :TOK], preferred_element_type=F32).astype(BF16)
    weights = weights - jnp.mean(weights, axis=1, keepdims=True)
    high = weights.astype(BF16)
    spread[...] = jnp.zeros_like(spread)
    spread[:AUG, :] = high.astype(F32)
    spread[TOK : TOK + AUG, :] = weights - high.astype(F32)
    plain[...] = spread[...].T.astype(BF16)
    wide_ref[:, WAUG : WAUG + 256] = jnp.dot(reorder, plain[...], preferred_element_type=F32).astype(BF16)
    product = jnp.dot(tall_ref[:D, :], wide_ref[:, WAUG : WAUG + 256], preferred_element_type=F32)
    product = product[:, :TOK] + product[:, TOK:]
    high = product.astype(BF16)
    wide_ref[:, QUERY : QUERY + TOK] = high
    wide_ref[:, QUERY + TOK : QUERY + 256] = (product - high.astype(F32)).astype(BF16)
    side = core_ref[0] * HEAD
    for z in range(ZED):
        rows_here = slice(z * HEAD, (z + 1) * HEAD)
        start = pl.multiple_of(z * 2 * HEAD + side, HEAD)
        own_ref[rows_here, : 2 * D] = kvw_ref[pl.ds(start, HEAD), :]
        own_ref[rows_here, 2 * D :] = plain[pl.ds(start, HEAD), :]
    mean = jnp.mean(kvw_ref[...].astype(F32), axis=0, keepdims=True)
    high = mean.astype(BF16).astype(F32)
    row = lax.broadcasted_iota(jnp.int32, (OWN - HALF, 2 * D), 0)
    own_ref[HALF:, : 2 * D] = jnp.where(row == 0, high, jnp.where(row == 1, mean - high, 0.0)).astype(BF16)
    own_ref[HALF:, 2 * D :] = jnp.zeros((OWN - HALF, DEEP), BF16)
    head = lax.broadcasted_iota(jnp.int32, (HEADS, D), 0)
    owner = lax.broadcasted_iota(jnp.int32, (HEADS, D), 1) >> 5
    spread[:32, :] = jnp.zeros((32, D), F32)
    for a in range(LATENT):
        block = jnp.where(head == owner, query_ref[a : a + 1, :].astype(F32), 0.0)
        spread[32 + a * HEADS : 32 + (a + 1) * HEADS, :] = block
        spread[80 + a * HEADS : 80 + (a + 1) * HEADS, :] = block
    tall_ref[2 * D : 2 * D + AH, :] = spread[80:128, :].astype(BF16)
    tall_ref[2 * D + AH :, :] = jnp.zeros((16, D), BF16)
    wide_ref[:, QBD : QBD + GS] = spread[:GS, :].T.astype(BF16)
    for a in range(LATENT):
        at = GRAD + a * TOK
        wide_ref[:, at : at + TOK] = grad_ref[a].astype(F32).T.astype(BF16)


def main_kernel(
    lon_ref, count_ref, recv_ref, tall_ref, wide_ref,
    keep_out, send_out,
    g_s, paug_s, hid_s, kv_s, left_s, pin_s, inv_s, sc_s, ga_s, w_s,
):
    lon = lon_ref[0]
    count = count_ref[0]
    for a in range(LATENT):
        g_s[a] = wide_ref[:, GRAD + a * TOK : GRAD + (a + 1) * TOK].astype(F32)
    left_s[D : D + 32, :] = jnp.zeros((32, SPAN), BF16)
    left_s[D + GS + AUG :, :] = jnp.zeros((TOK - AUG, SPAN), BF16)
    pin_s[AUG:, :] = jnp.zeros((TOK - AUG, SPAN), BF16)
    paug_s[AUG:, :] = jnp.zeros((TOK - AUG, SPAN), BF16)

    def lanes_of(group):
        return slice(group[0] * TOK, (group[-1] + 1) * TOK)

    def embed(group):
        at = lanes_of(group)
        row = lax.broadcasted_iota(jnp.int32, (AUG - FEAT, TOK), 0)
        for l in group:
            lanes = slice(l * TOK, (l + 1) * TOK)
            patches = recv_ref[(RING * l + lon) // LEVELS]
            one_hot = jnp.where(row == l, 1.0, 0.0).astype(BF16)
            paug_s[:FEAT, lanes] = patches
            paug_s[FEAT:AUG, lanes] = one_hot
        embedded = jnp.dot(wide_ref[:, RAW : RAW + TOK], paug_s[:, at], preferred_element_type=F32)
        center = embedded - jnp.mean(embedded, axis=0, keepdims=True)
        inv_std = lax.rsqrt(jnp.mean(center * center, axis=0, keepdims=True) + EPSILON)
        inv_s[:, at] = inv_std
        hid_s[:, at] = (center * inv_std).astype(BF16)
        pin_s[:AUG, at] = (paug_s[:AUG, at].astype(F32) * inv_std).astype(BF16)

    def keys(group):
        at = lanes_of(group)
        kv_s[:, at] = jnp.dot(tall_ref[: 2 * D, :], hid_s[:, at], preferred_element_type=F32).astype(BF16)

    def score(group):
        at = lanes_of(group)
        sc_s[:, at] = (
            jnp.dot(tall_ref[2 * D : 2 * D + AH, :], kv_s[:D, at], preferred_element_type=F32) * SCORE_SCALE
        )
        for h in range(HEADS):
            rows = slice(h * HEAD, (h + 1) * HEAD)
            grads = [g_s[a, rows, :] for a in range(LATENT)]
            for l in group:
                lanes = slice(l * TOK, (l + 1) * TOK)
                values = kv_s[D + h * HEAD : D + (h + 1) * HEAD, lanes].astype(F32)
                for a in range(LATENT):
                    product = (grads[a] * values).reshape(4, 8, TOK)
                    ah = a * HEADS + h
                    ga_s[ah : ah + 1, lanes] = jnp.sum(jnp.sum(product, axis=0), axis=0, keepdims=True)

    every = tuple(range(LEVELS))
    embed(every)
    keys(every)
    score(every)

    masked = [jnp.where(l < count, sc_s[:, l * TOK : (l + 1) * TOK], MASKED) for l in range(LEVELS)]
    peak = functools.reduce(jnp.maximum, masked)
    total = jnp.zeros_like(peak)
    for l in range(LEVELS):
        exponent = jnp.exp(masked[l] - peak)
        w_s[:, l * TOK : (l + 1) * TOK] = exponent
        total = total + exponent
    inverse = 1.0 / total
    inner = jnp.zeros_like(peak)
    for l in range(LEVELS):
        lanes = slice(l * TOK, (l + 1) * TOK)
        inner = inner + w_s[:, lanes] * inverse * ga_s[:, lanes]
    for l in range(LEVELS):
        lanes = slice(l * TOK, (l + 1) * TOK)
        attention = w_s[:, lanes] * inverse
        weight = attention.astype(BF16).astype(F32)
        w_s[:, lanes] = weight
        grad_attn = ga_s[:, lanes]
        grad_score = attention * (grad_attn - inner)
        slope = jnp.sum(grad_score * sc_s[:, lanes] + weight * grad_attn, axis=0, keepdims=True)
        scale = slope * inv_s[:, lanes] * (1.0 / D)
        left_s[D + GS : D + GS + AUG, lanes] = (paug_s[:AUG, lanes].astype(F32) * scale).astype(BF16)
        grad_score = grad_score * SCORE_SCALE
        high = grad_score.astype(BF16)
        left_s[D + 32 : D + 80, lanes] = (grad_score - high.astype(F32)).astype(BF16)
        left_s[D + 80 : D + GS, lanes] = high

    def grad_values_of(group):
        for h in range(HEADS):
            rows = slice(h * HEAD, (h + 1) * HEAD)
            grads = [g_s[a, rows, :] for a in range(LATENT)]
            for l in group:
                lanes = slice(l * TOK, (l + 1) * TOK)
                grad_values = None
                for a in range(LATENT):
                    term = w_s[a * HEADS + h : a * HEADS + h + 1, lanes] * grads[a]
                    grad_values = term if grad_values is None else grad_values + term
                left_s[rows, lanes] = grad_values.astype(BF16)

    outer = None
    for group in (every[:6], every[6:]):
        grad_values_of(group)
        at = lanes_of(group)
        term = lax.dot_general(left_s[:, at], pin_s[:, at], NT, preferred_element_type=F32)
        outer = term if outer is None else outer + term

    keep_out[...] = outer
    send_out[...] = outer.astype(BF16)


def post_kernel(core_ref, keep_ref, recv_ref, wide_ref, own_ref, part_ref):
    total = keep_ref[...] + recv_ref[...].astype(F32)
    scores = total[D : D + GS]
    scores = scores[80:] + scores[32:80]
    high = scores.astype(BF16)
    low = (scores - high.astype(F32)).astype(BF16)
    outer = jnp.dot(
        wide_ref[:, QBD : QBD + GS],
        jnp.concatenate([jnp.zeros((32, TOK), BF16), low, high], axis=0),
        preferred_element_type=F32,
    )
    outer = jnp.concatenate([outer, total[:D]], axis=0)
    high = outer.astype(BF16)
    low = (outer - high.astype(F32)).astype(BF16)
    start = pl.multiple_of(core_ref[0] * HALF, HALF)
    part_ref[:, : 2 * D] = lax.dot_general(
        wide_ref[pl.ds(start, HALF), WAUG : WAUG + DEEP],
        jnp.concatenate([high, high], axis=1),
        NT,
        preferred_element_type=F32,
    ).astype(BF16)
    grads = jnp.dot(own_ref[:, : 2 * D], jnp.concatenate([high, low], axis=1), preferred_element_type=F32)
    grads = grads[:, :TOK] + grads[:, TOK:]
    gram = total[D + GS :].astype(BF16)
    grads = (
        grads[:HALF]
        - (grads[HALF : HALF + 1] + grads[HALF + 1 : HALF + 2])
        - jnp.dot(own_ref[:HALF, 2 * D :], jnp.concatenate([gram, gram], axis=0), preferred_element_type=F32)
    )
    scores = jnp.concatenate([jnp.zeros((FEAT, TOK), F32), scores], axis=0).astype(BF16)
    queries = lax.dot_general(
        wide_ref[:, QUERY : QUERY + DEEP],
        jnp.concatenate([scores, scores], axis=1),
        NT,
        preferred_element_type=F32,
    )
    head = lax.broadcasted_iota(jnp.int32, (D, GS), 0) >> 5
    lane = lax.broadcasted_iota(jnp.int32, (D, GS), 1)
    queries = jnp.where((lane & 15) == head, queries, 0.0).reshape(HEADS, HEAD, GS)
    queries = jnp.concatenate([jnp.sum(queries, axis=0)] * ZED, axis=0)
    part_ref[:, 2 * D :] = jnp.where(lane[:HALF] < FEAT, grads, queries).astype(BF16)


def sum_z_kernel(part_ref, share_ref, total, tile):
    acc = part_ref[0].astype(F32)
    for source in range(1, ZED):
        acc = acc + part_ref[source].astype(F32)
    total[...] = acc
    block = acc[:, 2 * D :].astype(BF16)
    for target in range(RING):
        for c in range(8):
            tile[target, 2 * c : 2 * c + 2, :] = total[2 * target : 2 * target + 2, c * TOK : (c + 1) * TOK]
        share_ref[target, 0:16, :] = tile[target].astype(BF16)
        share_ref[target, 16:48, :] = block


def sum_lon_kernel(share_ref, kv_out, embed_out, query_out, tile, turned):
    acc = share_ref[0].astype(F32)
    for source in range(1, RING):
        acc = acc + share_ref[source].astype(F32)
    tile[...] = acc[:16]
    for c in range(8):
        kv_out[:, c * TOK : (c + 1) * TOK] = tile[2 * c : 2 * c + 2, :]
    embed_out[...] = acc[16:, :FEAT]
    turned[...] = acc[16:, :].T
    for a in range(LATENT):
        for h in range(HEADS):
            at = FEAT + a * HEADS + h
            query_out[a : a + 1, h * HEAD : (h + 1) * HEAD] = turned[at : at + 1, :]


def call(kernel, outs, in_specs, scratch, mib, name):
    return pl.pallas_call(
        kernel,
        out_shape=outs,
        in_specs=in_specs,
        out_specs=jax.tree.map(lambda _: VMEM, outs),
        scratch_shapes=scratch,
        compiler_params=params(mib),
        name=name,
    )


def on_device(level_patches, level_embed, embed_weight, kv_weight, query, band_levels, grad_out):
    lon = lax.axis_index("lon").astype(jnp.int32).reshape(1)
    core = (lax.axis_index("lat").astype(jnp.int32) & 1).reshape(1)
    slots = pl.pallas_call(
        slot_kernel,
        out_shape=shape(RING, FEAT, TOK),
        in_specs=[SMEM, HBM],
        out_specs=HBM,
        scratch_shapes=[pltpu.SemaphoreType.DMA((LEVELS,))],
        compiler_params=params(8),
        name="slots",
    )(lon, level_patches[0].T)
    tall, wide, own = call(
        prep_kernel,
        (shape(2 * D + 64, D), shape(D, RAW + TOK), shape(OWN, 2 * D + DEEP)),
        [SMEM] + [VMEM] * 5,
        [pltpu.VMEM((AUG, D), F32), pltpu.VMEM((DEEP, D), F32), pltpu.VMEM((D, DEEP), BF16)],
        24,
        "prep",
    )(core, kv_weight, embed_weight, level_embed, query, grad_out[0].transpose(1, 0, 2))
    recv = lax.all_to_all(slots, "lon", 0, 0, tiled=True)
    keep, send = call(
        main_kernel,
        (shape(LEFT, TOK, dtype=F32), shape(LEFT, TOK)),
        [SMEM, SMEM] + [VMEM] * 3,
        [
            pltpu.VMEM((LATENT, D, TOK), F32),
            pltpu.VMEM((TOK, SPAN), BF16),
            pltpu.VMEM((D, SPAN), BF16),
            pltpu.VMEM((2 * D, SPAN), BF16),
            pltpu.VMEM((LEFT, SPAN), BF16),
            pltpu.VMEM((TOK, SPAN), BF16),
            pltpu.VMEM((1, SPAN), F32),
            pltpu.VMEM((AH, SPAN), F32),
            pltpu.VMEM((AH, SPAN), F32),
            pltpu.VMEM((AH, SPAN), F32),
        ],
        28,
        "main",
    )(lon, band_levels, recv, tall, wide)
    lats = lax.axis_size("lat")
    other = lax.ppermute(send, "lat", [(i, i ^ 1) for i in range(lats)])
    part = call(post_kernel, shape(HALF, ROW), [SMEM] + [VMEM] * 4, [], 16, "post")(core, keep, other, wide, own)
    parts = lax.all_to_all(
        part.reshape(ZED, HALF // ZED, ROW),
        "lat",
        0,
        0,
        tiled=True,
        axis_index_groups=[[2 * z + c for z in range(ZED)] for c in range(2)],
    )
    share = call(
        sum_z_kernel,
        shape(RING, SHARE, TOK),
        [VMEM],
        [pltpu.VMEM((HALF // ZED, ROW), F32), pltpu.VMEM((RING, 16, TOK), F32)],
        8,
        "sum_z",
    )(parts)
    shared = lax.all_to_all(share, "lon", 0, 0, tiled=True)
    kv_grad, embed_grad, query_grad = call(
        sum_lon_kernel,
        (shape(2, 2 * D, dtype=F32), shape(32, FEAT, dtype=F32), shape(LATENT, D, dtype=F32)),
        [VMEM],
        [pltpu.VMEM((16, TOK), F32), pltpu.VMEM((TOK, 32), F32)],
        8,
        "sum_lon",
    )(shared)
    return (kv_grad, embed_grad.T, query_grad)


def solution(mesh):
    placed = (P("lat", "lon", None), P(), P(), P(), P(), P("lat"), P("lat", "lon", None, None))
    return jax.shard_map(
        on_device,
        mesh=mesh,
        in_specs=placed,
        out_specs=(P(("lon", "lat"), None), P(None, "lat"), P()),
        check_vma=False,
    )
```
